32 devices in a mesh: row: 4 (over y, x), col: 8 (over z, core).
Axes of the slice: x: 2, y: 2, z: 4, core: 2. Of those that a mesh axis runs over, the one named last changes fastest.
Arguments:
- elevation: float32 [2048, 8192], P('row', 'col'), may hold values from -6 to 6
- ocean: int32 [2048, 8192], P('row', 'col'), may hold values from 0 to 1, as said below
- outlet: int32 [2048, 8192], P('row', 'col'), may hold values from 0 to 1, as said below
Outputs:
- surface: float32 [2048, 8192], P('row', 'col')
The draws below stay inside these ranges and needn't reach their ends.
Inputs may be any that keep to these rules, and one draw needn't show every extreme that they name: ocean cells are scattered; no bound on their count in any region may be assumed. outlet cells are scattered; no bound on their count in any region may be assumed.
All inputs are finite; a program needn't handle non-finite values.
Results may differ from the reference program's by a relative error of at most 0.00002.
Values sent between devices are 32-bit elements; how exact they have to be, the bound alone decides.
No kernel may reach another device: no remote copies, remote signals or barrier semaphores. Data moves between devices by JAX's collectives and lax.ppermute only.
A program may use at most 128 MiB of HBM per device.

```python
import jax
import jax.numpy as jnp
from jax import lax

BLK = 16
COARSE = 4
FINE = 8
NX = 2048
NY = 8192


def dry_patch(key):
    anchor_key = jax.random.fold_in(key, 7)
    row_key, col_key = jax.random.split(anchor_key)
    block_rows = NX // BLK
    block_cols = NY // BLK
    top_row = jax.random.randint(row_key, (), 0, block_rows - 9) * BLK
    left_col = jax.random.randint(col_key, (), 0, block_cols - 9) * BLK
    rows_iota = lax.broadcasted_iota(jnp.int32, (NX, NY), 0)
    cols_iota = lax.broadcasted_iota(jnp.int32, (NX, NY), 1)
    inside_rows = (rows_iota >= top_row) & (rows_iota < top_row + 10 * BLK)
    inside_cols = (cols_iota >= left_col) & (cols_iota < left_col + 10 * BLK)
    return inside_rows & inside_cols


def draw_ocean(key, part):
    hits = jax.random.randint(jax.random.fold_in(key, 11), (NX, NY), 0, 512)
    marked = (hits == 0) & jnp.logical_not(dry_patch(key))
    return jnp.where(marked, 1, 0).astype(jnp.int32)


def draw_outlet(key, part):
    hits = jax.random.randint(jax.random.fold_in(key, 13), (NX, NY), 0, 1024)
    marked = (hits == 0) & jnp.logical_not(dry_patch(key))
    return jnp.where(marked, 1, 0).astype(jnp.int32)


def shard_levels(key, dims, shards, least, high):
    factor_of = 1.0
    for axis_at, blocks in shards:
        draws = jax.random.uniform(jax.random.fold_in(jax.random.fold_in(key, 6), axis_at), (blocks,), jnp.float32, least / len(shards), high / len(shards))
        factor_of = factor_of * jnp.repeat(jnp.exp(draws), dims[axis_at] // blocks).reshape((-1,) + (1,) * (len(dims) - 1 - axis_at))
    return factor_of


def centred(rng, shape, scale, reach, shards=(), kind=jnp.bfloat16):
    values = jax.random.normal(rng, shape, jnp.float32) * scale
    if len(shards) > 0:
        values = shard_levels(rng, shape, shards, -0.22, 0.18) * values
    return jnp.clip(values, min=-reach, max=reach).astype(kind)


def setup_inputs(seed: int = 0) -> dict:
    streams_of = jax.random.split(jax.random.key(seed), 4)
    elevation = centred(streams_of[0], (NX, NY), 1.0, 6.0, ((0, 4), (1, 8)), jnp.float32)
    ocean = draw_ocean(jax.random.fold_in(streams_of[3], 71), 0)
    outlet = draw_outlet(jax.random.fold_in(streams_of[3], 71), 0)
    return {"elevation": elevation, "ocean": ocean, "outlet": outlet}


huge_level = 1.0e30
fine_step = 2.0 ** -10
coarse_step = 2.0 ** -6


def extend(field):
    wrapped = jnp.concatenate([field[:, -1:], field, field[:, :1]], axis=1)
    return jnp.pad(wrapped, ((1, 1), (0, 0)), constant_values=huge_level)


def neighbour_min(extended):
    height = extended.shape[0] - 2
    width = extended.shape[1] - 2
    result = None
    for down in range(3):
        for across in range(3):
            if down == 1 and across == 1:
                continue
            piece = extended[down:down + height, across:across + width]
            result = piece if result is None else jnp.minimum(result, piece)
    return result


def update(extended, ground, lock, step_size):
    center = extended[1:-1, 1:-1]
    lowered = jnp.minimum(center, neighbour_min(extended) + step_size)
    return jnp.minimum(jnp.maximum(ground, lowered), lock)


def reference(elevation, ocean, outlet):
    ground = jnp.where(ocean == 1, jnp.float32(0.0), elevation)
    drains = (ocean == 1) | (outlet == 1)
    lock = jnp.where(drains, ground, jnp.float32(huge_level))
    shape_blocks = (NX // BLK, BLK, NY // BLK, BLK)
    ground_c = ground.reshape(shape_blocks).min(axis=(1, 3))
    lock_c = lock.reshape(shape_blocks).min(axis=(1, 3))
    coarse = ground.reshape(shape_blocks).max(axis=(1, 3))
    for sweep in range(COARSE):
        coarse = update(extend(coarse), ground_c, lock_c, coarse_step)
    lifted = jnp.repeat(jnp.repeat(coarse, BLK, axis=0), BLK, axis=1)
    surface = jnp.minimum(jnp.maximum(ground, lifted), lock)
    for sweep in range(FINE):
        surface = update(extend(surface), ground, lock, fine_step)
    return surface
```

```python
import functools

import jax
import jax.numpy as jnp
from jax import lax
from jax.experimental import pallas as pl
from jax.experimental.pallas import tpu as pltpu
from jax.sharding import PartitionSpec as P

BLK = 16
COARSE = 4
FINE = 8
LANES = 128
SUB = 8
HALO_C = 8
UNROLL = 22

huge_level = 1e30
fine_step = 2.0 ** (-10)
coarse_step = 2.0 ** (-6)
MIB = 2**20


def roll(x, shift, axis):
    return pltpu.roll(x, shift % x.shape[axis], axis)


def lane_iota(shape=(SUB, LANES)):
    return lax.broadcasted_iota(jnp.int32, shape, 1)


def gather_lanes(x, index):
    return jnp.take_along_axis(x, index, axis=1, mode="promise_in_bounds")


def prepare_kernel(elev, ocean, outlet, ground, lock, stats, north, south):
    step = pl.program_id(0)
    tiles = pl.num_programs(0)
    rows = elev.shape[0]
    blocks = rows // BLK
    lane = lane_iota()
    spread = (lane % 8) * BLK
    mine = lane // 8 == step

    @pl.when(step == 0)
    def _():
        stats[...] = jnp.zeros(stats.shape, jnp.float32)
        north[...] = jnp.zeros(north.shape, jnp.float32)
        south[...] = jnp.zeros(south.shape, jnp.float32)

    is_ocean = ocean[...] == 1
    g = jnp.where(is_ocean, jnp.float32(0.0), elev[...])
    k = jnp.where(is_ocean | (outlet[...] == 1), g, jnp.float32(huge_level))
    ground[0] = g
    lock[0] = k
    north[step, 0:FINE, :] = g[0:FINE]
    north[step, FINE:, :] = k[0:FINE]
    south[step, 0:FINE, :] = g[rows - FINE :]
    south[step, FINE:, :] = k[rows - FINE :]
    for q in range(blocks // SUB):
        for which, (source, pick) in enumerate(
            ((g, jnp.minimum), (k, jnp.minimum), (g, jnp.maximum))
        ):
            part = source[q * SUB * BLK : (q + 1) * SUB * BLK].reshape(SUB, BLK, LANES)
            reduce = jnp.max if which == 2 else jnp.min
            acc = reduce(part, axis=1)
            for shift in (1, 2, 4, 8):
                acc = pick(acc, roll(acc, -shift, 1))
            compact = gather_lanes(acc, spread)
            at = pl.ds(which * blocks + q * SUB, SUB)
            stats[at, :] = jnp.where(mine, compact, stats[at, :])

    @pl.when(step == tiles - 1)
    def _():
        for which in range(3):
            slot = tiles + which // 2
            at = (which % 2) * HALO_C
            first = which * blocks
            north[slot, at : at + HALO_C, :] = stats[first : first + HALO_C, :]
            south[slot, at : at + HALO_C, :] = stats[first + blocks - HALO_C : first + blocks, :]


def prepare(elevation, ocean, outlet):
    rows, cols = elevation.shape
    tiles = cols // LANES
    tile = pl.BlockSpec((rows, LANES), lambda j: (0, j))
    out_tile = pl.BlockSpec((1, rows, LANES), lambda j: (j, 0, 0))
    f32 = jnp.float32
    whole = lambda *shape: pl.BlockSpec(shape, lambda j: (0,) * len(shape))
    band = (tiles + 2, 2 * FINE, LANES)
    stats = (3 * rows // BLK, LANES)
    return pl.pallas_call(
        prepare_kernel,
        grid=(tiles,),
        in_specs=[tile, tile, tile],
        out_specs=[out_tile, out_tile, whole(*stats), whole(*band), whole(*band)],
        out_shape=[
            jax.ShapeDtypeStruct((tiles, rows, LANES), f32),
            jax.ShapeDtypeStruct((tiles, rows, LANES), f32),
            jax.ShapeDtypeStruct(stats, f32),
            jax.ShapeDtypeStruct(band, f32),
            jax.ShapeDtypeStruct(band, f32),
        ],
        compiler_params=pltpu.CompilerParams(vmem_limit_bytes=12 * MIB),
        name="prepare",
    )(elevation, ocean, outlet)


def sealed(value, is_edge):
    return jnp.where(is_edge, jnp.float32(huge_level), value)


def edges():
    pos = lax.axis_index("row")
    return pos == 0, pos == lax.axis_size("row") - 1


def coarse_fields(stats, from_north, from_south):
    tiles = from_north.shape[0] - 2
    blocks = stats.shape[0] // 3
    at_north, at_south = edges()
    fields = []
    for which in range(3):
        slot = tiles + which // 2
        at = (which % 2) * HALO_C
        top = sealed(from_north[slot, at : at + HALO_C, :], at_north)
        low = sealed(from_south[slot, at : at + HALO_C, :], at_south)
        mid = stats[which * blocks : (which + 1) * blocks, :]
        fields.append(jnp.concatenate([top, mid, low], axis=0))
    return fields


def coarse_sweeps(ground_c, lock_c, value):
    for _ in range(COARSE):
        across = jnp.minimum(value, jnp.minimum(roll(value, 1, 1), roll(value, -1, 1)))
        around = jnp.minimum(across, jnp.minimum(roll(across, 1, 0), roll(across, -1, 0)))
        lowered = jnp.minimum(value, around + coarse_step)
        value = jnp.minimum(jnp.maximum(ground_c, lowered), lock_c)
    return value


def start_tile(g, k, c):
    return jnp.minimum(jnp.maximum(g, c), k), jnp.minimum(g, k)


def across_min(tiles, lane, joined):
    count = len(tiles)
    left = [roll(v, 1, 1) for v in tiles]
    right = [roll(v, -1, 1) for v in tiles]
    out = []
    for j in range(count):
        west, east = left[j], right[j]
        if joined:
            west = jnp.where(lane == 0, left[j - 1], west)
            east = jnp.where(lane == LANES - 1, right[(j + 1) % count], east)
        out.append(jnp.minimum(tiles[j], jnp.minimum(west, east)))
    return out


def fine_sweep(src, dst, floor, stride, joined):
    count = src.shape[0]
    lane = lane_iota()

    def load(t):
        return [src[j, pl.ds(t, SUB, stride=stride), :] for j in range(count)]

    first = load(0)
    h_first = across_min(first, lane, joined)
    h_before = [roll(h, 1, 0) for h in across_min(load(stride - 1), lane, joined)]

    def advance(t, carry, after=None):
        h_up, h_here, here = carry
        if after is None:
            below = load(t + 1)
            h_down = across_min(below, lane, joined)
        else:
            below, h_down = here, after
        for j in range(count):
            low = jnp.minimum(jnp.minimum(h_up[j], h_down[j]), h_here[j])
            at = pl.ds(t, SUB, stride=stride)
            dst[j, at, :] = jnp.maximum(floor[j, at, :], jnp.minimum(here[j], low + fine_step))
        return h_here, h_down, below

    def body(q, carry):
        for u in range(UNROLL):
            carry = advance(q * UNROLL + u, carry)
        return carry

    loops = (stride - 1) // UNROLL
    carry = lax.fori_loop(0, loops, body, (h_before, h_first, first))
    for t in range(loops * UNROLL, stride - 1):
        carry = advance(t, carry)
    advance(stride - 1, carry, [roll(h, -1, 0) for h in h_first])


def all_sweeps(va, vb, floor, joined):
    stride = va.shape[1] // SUB

    def pair(i, carry):
        fine_sweep(va, vb, floor, stride, joined)
        fine_sweep(vb, va, floor, stride, joined)
        return carry

    lax.fori_loop(0, FINE // 2, pair, 0)


def padded_rows(rows):
    stride = -(-(rows + 2 * FINE) // SUB)
    return SUB * (stride + 1 - stride % 2)


def main_kernel(ground, lock, stats, from_north, from_south, out, va, vb, floor, lifted, sems):
    tiles, rows, _ = ground.shape
    blocks = rows // BLK
    at_north, at_south = edges()
    coarse = coarse_sweeps(*coarse_fields(stats, from_north, from_south))
    lane = lane_iota(coarse.shape)
    for j in range(tiles):
        lifted[j] = gather_lanes(coarse, lane // BLK + 8 * j)

    def put(j, at, size, g, k, c):
        v, low = start_tile(g, k, c)
        va[j, pl.ds(at, size), :] = v
        floor[j, pl.ds(at, size), :] = low

    for j in range(tiles):
        for band, is_edge, at, c_row in (
            (from_north, at_north, 0, HALO_C - 1),
            (from_south, at_south, FINE + rows, HALO_C + blocks),
        ):
            g = sealed(band[j, 0:FINE, :], is_edge)
            k = sealed(band[j, FINE:, :], is_edge)
            put(j, at, FINE, g, k, lifted[j, c_row : c_row + 1, :])
        rest = va.shape[1] - rows - 2 * FINE
        if rest:
            fill = jnp.full((rest, LANES), huge_level, jnp.float32)
            put(j, rows + 2 * FINE, rest, fill, fill, fill)

    def body(b, carry):
        for j in range(tiles):
            at = pl.ds(pl.multiple_of(b * BLK, BLK), BLK)
            c = lifted[j, pl.ds(HALO_C + b, 1), :]
            put(j, pl.multiple_of(FINE + b * BLK, SUB), BLK, ground[j, at, :], lock[j, at, :], c)
        return carry

    lax.fori_loop(0, blocks, body, 0, unroll=4)
    all_sweeps(va, vb, floor, True)
    copies = [
        pltpu.make_async_copy(
            va.at[j, pl.ds(FINE, rows), :], out.at[:, pl.ds(j * LANES, LANES)], sems.at[j]
        )
        for j in range(tiles)
    ]
    for copy in copies:
        copy.start()
    for copy in copies:
        copy.wait()


def main_part(ground, lock, stats, from_north, from_south):
    tiles, rows, _ = ground.shape
    blocks = rows // BLK
    vmem = pl.BlockSpec(memory_space=pltpu.VMEM)
    tall = (tiles, padded_rows(rows), LANES)
    return pl.pallas_call(
        main_kernel,
        in_specs=[vmem] * 5,
        out_specs=pl.BlockSpec(memory_space=pl.ANY),
        out_shape=jax.ShapeDtypeStruct((rows, tiles * LANES), jnp.float32),
        scratch_shapes=[
            pltpu.VMEM(tall, jnp.float32),
            pltpu.VMEM(tall, jnp.float32),
            pltpu.VMEM(tall, jnp.float32),
            pltpu.VMEM((tiles, blocks + 2 * HALO_C, LANES), jnp.float32),
            pltpu.SemaphoreType.DMA((tiles,)),
        ],
        compiler_params=pltpu.CompilerParams(vmem_limit_bytes=24 * MIB),
        cost_estimate=pl.CostEstimate(flops=100_000_000, bytes_accessed=40_000_000, transcendentals=0),
        name="middle",
    )(ground, lock, stats, from_north, from_south)


def column_sources(rows, blocks):
    fine = (rows + 2 * FINE) // SUB
    coarse = (blocks + 2 * HALO_C) // SUB
    return fine, coarse, -(-(2 * fine + 3 * coarse) // 16)


def pack_kernel(g_first, k_first, g_last, k_last, stats, from_north, from_south, west, east):
    rows = g_first.shape[1]
    blocks = rows // BLK
    tiles = from_north.shape[0] - 2
    at_north, at_south = edges()
    group = lane_iota() // 8
    fields = coarse_fields(stats, from_north, from_south)
    fine, coarse, slots = column_sources(rows, blocks)
    coarse_cols = tiles * LANES // BLK
    for dst, g_ref, k_ref, j, lane_at, lane_at_c in (
        (west, g_first, k_first, 0, 0, 0),
        (east, g_last, k_last, tiles - 1, LANES - 8, coarse_cols - 8),
    ):
        sources = []
        for half, ref in ((0, g_ref), (1, k_ref)):
            at = half * FINE
            sources.append((sealed(from_north[j, at : at + FINE, :], at_north), lane_at))
            for i in range(rows // SUB):
                sources.append((ref[0, i * SUB : (i + 1) * SUB, :], lane_at))
            sources.append((sealed(from_south[j, at : at + FINE, :], at_south), lane_at))
        for field in fields:
            for i in range(coarse):
                sources.append((field[i * SUB : (i + 1) * SUB], lane_at_c))
        for slot in range(slots):
            packed = jnp.zeros((SUB, LANES), jnp.float32)
            for n, (value, at) in enumerate(sources[slot * 16 : slot * 16 + 16]):
                packed = jnp.where(group == n, roll(value, 8 * n - at, 1), packed)
            dst[slot * SUB : (slot + 1) * SUB, :] = packed


def pack_columns(ground, lock, stats, from_north, from_south):
    tiles, rows, _ = ground.shape
    blocks = rows // BLK
    slots = column_sources(rows, blocks)[2]
    first = pl.BlockSpec((1, rows, LANES), lambda i: (0, 0, 0))
    last = pl.BlockSpec((1, rows, LANES), lambda i: (tiles - 1, 0, 0))
    whole = lambda x: pl.BlockSpec(x.shape, lambda i: (0,) * x.ndim)
    out = jax.ShapeDtypeStruct((slots * SUB, LANES), jnp.float32)
    return pl.pallas_call(
        pack_kernel,
        grid=(1,),
        in_specs=[first, first, last, last, whole(stats), whole(from_north), whole(from_south)],
        out_specs=[whole(out), whole(out)],
        out_shape=[out, out],
        compiler_params=pltpu.CompilerParams(vmem_limit_bytes=8 * MIB),
        name="pack",
    )(ground, lock, ground, lock, stats, from_north, from_south)


def strip_kernel(
    g_first, k_first, g_last, k_last, stats, from_north, from_south, from_west, from_east, partial,
    out, va, vb, floor, lifted, edge, in_sems, out_sems,
):
    rows = g_first.shape[1]
    blocks = rows // BLK
    tiles = from_north.shape[0] - 2
    coarse_cols = tiles * LANES // BLK
    at_north, at_south = edges()
    lane = lane_iota()
    fine, coarse, slots = column_sources(rows, blocks)
    edge_cols = [pl.ds(0, LANES), pl.ds((tiles - 1) * LANES, LANES)]
    loads = [
        pltpu.make_async_copy(partial.at[:, edge_cols[j]], edge.at[j], in_sems.at[j])
        for j in range(2)
    ]
    for copy in loads:
        copy.start()

    def piece(ref, n, to):
        value = ref[(n // 16) * SUB : (n // 16 + 1) * SUB, :]
        return roll(value, to - 8 * (n % 16), 1)

    fields = []
    for which, field in enumerate(coarse_fields(stats, from_north, from_south)):
        parts = []
        for i in range(coarse):
            n = 2 * fine + which * coarse + i
            here = field[i * SUB : (i + 1) * SUB]
            here = jnp.where(lane // 8 == coarse_cols // 8, piece(from_east, n, coarse_cols), here)
            here = jnp.where(lane // 8 == 15, piece(from_west, n, LANES - 8), here)
            parts.append(here)
        fields.append(jnp.concatenate(parts, axis=0))
    value = coarse_sweeps(*fields)
    wide = lane_iota(value.shape)
    lifted[0] = gather_lanes(value, ((wide - 8) >> 4) & (LANES - 1))
    lifted[1] = gather_lanes(value, coarse_cols - 8 + ((wide + 8) >> 4))

    for strip, (g_ref, k_ref, j, source) in enumerate(
        ((g_first, k_first, 0, from_west), (g_last, k_last, tiles - 1, from_east))
    ):
        outer = lane // 8 == (0 if strip == 0 else 15)
        shift = 8 if strip == 0 else -8
        to = 0 if strip == 0 else LANES - 8
        for i in range(fine):
            if i == 0:
                here = [sealed(from_north[j, h * FINE : (h + 1) * FINE, :], at_north) for h in range(2)]
            elif i == fine - 1:
                here = [sealed(from_south[j, h * FINE : (h + 1) * FINE, :], at_south) for h in range(2)]
            else:
                here = [ref[0, (i - 1) * SUB : i * SUB, :] for ref in (g_ref, k_ref)]
            both = [
                jnp.where(outer, piece(source, h * fine + i, to), roll(here[h], shift, 1))
                for h in range(2)
            ]
            c_row = (i + 2 * HALO_C - 1) // 2
            v, low = start_tile(both[0], both[1], lifted[strip, c_row : c_row + 1, :])
            va[strip, i * SUB : (i + 1) * SUB, :] = v
            floor[strip, i * SUB : (i + 1) * SUB, :] = low
        rest = va.shape[1] - fine * SUB
        if rest:
            fill = jnp.full((rest, LANES), huge_level, jnp.float32)
            va[strip, fine * SUB :, :] = fill
            floor[strip, fine * SUB :, :] = fill

    all_sweeps(va, vb, floor, False)
    for copy in loads:
        copy.wait()
    stores = []
    for strip in range(2):
        inner = (lane < LANES - 16) if strip == 0 else (lane >= 16)
        for i in range(rows // SUB):
            at = slice(i * SUB, (i + 1) * SUB)
            moved = roll(va[strip, FINE + i * SUB : FINE + (i + 1) * SUB, :], -8 if strip == 0 else 8, 1)
            edge[strip, at, :] = jnp.where(inner, moved, edge[strip, at, :])
        stores.append(
            pltpu.make_async_copy(edge.at[strip], out.at[:, edge_cols[strip]], out_sems.at[strip])
        )
        stores[-1].start()
    for copy in stores:
        copy.wait()


def strips(ground, lock, stats, from_north, from_south, from_west, from_east, partial):
    tiles, rows, _ = ground.shape
    blocks = rows // BLK
    first = pl.BlockSpec((1, rows, LANES), lambda i: (0, 0, 0))
    last = pl.BlockSpec((1, rows, LANES), lambda i: (tiles - 1, 0, 0))
    whole = lambda x: pl.BlockSpec(x.shape, lambda i: (0,) * x.ndim)
    hbm = pl.BlockSpec(memory_space=pl.ANY)
    tall = (2, padded_rows(rows), LANES)
    small = [stats, from_north, from_south, from_west, from_east]
    return pl.pallas_call(
        strip_kernel,
        grid=(1,),
        in_specs=[first, first, last, last] + [whole(x) for x in small] + [hbm],
        out_specs=hbm,
        out_shape=jax.ShapeDtypeStruct(partial.shape, jnp.float32),
        input_output_aliases={9: 0},
        scratch_shapes=[
            pltpu.VMEM(tall, jnp.float32),
            pltpu.VMEM(tall, jnp.float32),
            pltpu.VMEM(tall, jnp.float32),
            pltpu.VMEM((2, blocks + 2 * HALO_C, LANES), jnp.float32),
            pltpu.VMEM((2, rows, LANES), jnp.float32),
            pltpu.SemaphoreType.DMA((2,)),
            pltpu.SemaphoreType.DMA((2,)),
        ],
        compiler_params=pltpu.CompilerParams(vmem_limit_bytes=12 * MIB),
        name="strips",
    )(ground, lock, ground, lock, *small, partial)


def ring(value, axis, shift):
    count = lax.axis_size(axis)
    return lax.ppermute(value, axis, [(i, (i + shift) % count) for i in range(count)])


def shards(elevation, ocean, outlet):
    ground, lock, stats, north, south = prepare(elevation, ocean, outlet)
    from_south = ring(north, "row", -1)
    from_north = ring(south, "row", 1)
    rows_args = (ground, lock, stats, from_north, from_south)
    west, east = pack_columns(*rows_args)
    from_east = ring(west, "col", -1)
    from_west = ring(east, "col", 1)
    partial = main_part(*rows_args)
    return strips(*rows_args, from_west, from_east, partial)


def solution(mesh):
    return jax.shard_map(
        shards,
        mesh=mesh,
        in_specs=(P("row", "col"), P("row", "col"), P("row", "col")),
        out_specs=P("row", "col"),
        check_vma=False,
    )
```

```python
import functools

import jax
import jax.numpy as jnp
from jax import lax
from jax.experimental import pallas as pl
from jax.experimental.pallas import tpu as pltpu
from jax.sharding import PartitionSpec as P

BLK = 16
COARSE = 4
FINE = 8
LANES = 128
SUB = 8
HALO_C = 8
UNROLL = 22
UNROLL_T = 15

huge_level = 1e30
fine_step = 2.0 ** (-10)
coarse_step = 2.0 ** (-6)
MIB = 2**20


def roll(x, shift, axis):
    return pltpu.roll(x, shift % x.shape[axis], axis)


def lane_iota(shape=(SUB, LANES)):
    return lax.broadcasted_iota(jnp.int32, shape, 1)


def gather_lanes(x, index):
    return jnp.take_along_axis(x, index, axis=1, mode="promise_in_bounds")


def interior(tiles):
    margin = COARSE * BLK
    chunk = (tiles * LANES - 2 * margin) // SUB
    return margin, chunk


def plane_row(col, tiles):
    margin, chunk = interior(tiles)
    return col + (col + chunk - margin) // chunk


def plane_rows(tiles):
    return -(-(plane_row(tiles * LANES, tiles) + 1) // SUB) * SUB


def prepare_kernel(
    elev, ocean, outlet, ground, lock, ground_t, lock_t, stats, stats_t, north, south,
    elev_buf, ocean_buf, outlet_buf, turn, sems,
):
    tiles, rows, _ = ground.shape
    planes = rows // LANES
    blocks = rows // BLK
    lane = lane_iota()
    sub = lax.broadcasted_iota(jnp.int32, (SUB, LANES), 0)

    def copies(j):
        cols = pl.ds(pl.multiple_of(j * LANES, LANES), LANES)
        return [
            pltpu.make_async_copy(src.at[:, cols], dst.at[j], sems.at[n, j])
            for n, (src, dst) in enumerate(
                ((elev, elev_buf), (ocean, ocean_buf), (outlet, outlet_buf))
            )
        ]

    for j in range(tiles):
        for copy in copies(j):
            copy.start()
    turn[...] = jnp.zeros(turn.shape, jnp.float32)
    for band in (north, south):
        band[tiles:, :, :] = jnp.zeros((2, 2 * FINE, LANES), jnp.float32)

    def tile(j, carry):
        for copy in copies(j):
            copy.wait()
        is_ocean = ocean_buf[j] == 1
        g = jnp.where(is_ocean, jnp.float32(0.0), elev_buf[j])
        k = jnp.where(is_ocean | (outlet_buf[j] == 1), g, jnp.float32(huge_level))
        ground[j] = g
        lock[j] = k
        north[j, 0:FINE, :] = g[0:FINE]
        north[j, FINE:, :] = k[0:FINE]
        south[j, 0:FINE, :] = g[rows - FINE :]
        south[j, FINE:, :] = k[rows - FINE :]
        found = [[None] * 8 for _ in range(3)]
        for c in range(planes):
            for which, (ref, dst) in enumerate(((ground, ground_t), (lock, lock_t))):
                parts = [
                    ref[j, pl.ds(a * SUB * planes + c, SUB, stride=planes), :]
                    for a in range(LANES // SUB)
                ]
                turned = jnp.concatenate(parts, axis=0).T
                for v in range(LANES // SUB):
                    value = turned[v * SUB : (v + 1) * SUB]
                    at = plane_row(j * LANES + v * SUB, tiles)
                    dst[c, pl.ds(at, SUB), :] = value
                    b = v // 2
                    for to, pick in ((which, jnp.minimum), (2, jnp.maximum)):
                        if to == 2 and which == 1:
                            continue
                        old = found[to][b]
                        found[to][b] = value if old is None else pick(old, value)
        for which in range(3):
            pick = jnp.maximum if which == 2 else jnp.minimum
            total = None
            for b in range(8):
                value = found[which][b]
                for shift in (4, 2, 1):
                    value = pick(value, roll(value, shift, 0))
                total = value if b == 0 else jnp.where(sub == b, value, total)
            for swap in (1, 2):
                total = pick(total, gather_lanes(total, lane ^ swap))
            at = pl.ds(pl.multiple_of(j * SUB, SUB), SUB)
            stats_t[which, at, :] = total
            turn[which, at, :] = total
        return carry

    lax.fori_loop(0, tiles, tile, 0)
    for which in range(3):
        turn[which] = turn[which].T
        for q in range(blocks // SUB):
            stats[which * blocks + q * SUB : which * blocks + (q + 1) * SUB, :] = turn[
                which, pl.ds(q * SUB * BLK // planes, SUB, stride=BLK // planes), :
            ]
        slot = tiles + which // 2
        at = (which % 2) * HALO_C
        first = which * blocks
        north[slot, at : at + HALO_C, :] = stats[first : first + HALO_C, :]
        south[slot, at : at + HALO_C, :] = stats[first + blocks - HALO_C : first + blocks, :]


def prepare(elevation, ocean, outlet):
    rows, cols = elevation.shape
    tiles = cols // LANES
    f32 = jnp.float32
    hbm = pl.BlockSpec(memory_space=pltpu.HBM)
    vmem = pl.BlockSpec(memory_space=pltpu.VMEM)
    natural = (tiles, rows, LANES)
    turned = (rows // LANES, plane_rows(tiles), LANES)
    band = (tiles + 2, 2 * FINE, LANES)
    shapes = [natural, natural, turned, turned, (3 * rows // BLK, LANES), (3, cols // BLK, LANES), band, band]
    return pl.pallas_call(
        prepare_kernel,
        in_specs=[hbm] * 3,
        out_specs=[vmem] * len(shapes),
        out_shape=[jax.ShapeDtypeStruct(shape, f32) for shape in shapes],
        scratch_shapes=[
            pltpu.VMEM(natural, f32),
            pltpu.VMEM(natural, jnp.int32),
            pltpu.VMEM(natural, jnp.int32),
            pltpu.VMEM((3, LANES, LANES), f32),
            pltpu.SemaphoreType.DMA((3, tiles)),
        ],
        compiler_params=pltpu.CompilerParams(vmem_limit_bytes=24 * MIB),
        name="prepare",
    )(*(pltpu.with_memory_space_constraint(x, pltpu.HBM) for x in (elevation, ocean, outlet)))


def sealed(value, is_edge):
    return jnp.where(is_edge, jnp.float32(huge_level), value)


def edges():
    pos = lax.axis_index("row")
    return pos == 0, pos == lax.axis_size("row") - 1


def coarse_fields(stats, from_north, from_south):
    tiles = from_north.shape[0] - 2
    blocks = stats.shape[0] // 3
    at_north, at_south = edges()
    fields = []
    for which in range(3):
        slot = tiles + which // 2
        at = (which % 2) * HALO_C
        top = sealed(from_north[slot, at : at + HALO_C, :], at_north)
        low = sealed(from_south[slot, at : at + HALO_C, :], at_south)
        mid = stats[which * blocks : (which + 1) * blocks, :]
        fields.append(jnp.concatenate([top, mid, low], axis=0))
    return fields


def coarse_sweeps(ground_c, lock_c, value):
    for _ in range(COARSE):
        across = jnp.minimum(value, jnp.minimum(roll(value, 1, 1), roll(value, -1, 1)))
        around = jnp.minimum(across, jnp.minimum(roll(across, 1, 0), roll(across, -1, 0)))
        lowered = jnp.minimum(value, around + coarse_step)
        value = jnp.minimum(jnp.maximum(ground_c, lowered), lock_c)
    return value


def start_tile(g, k, c):
    return jnp.minimum(jnp.maximum(g, c), k), jnp.minimum(g, k)


def across_min(tiles, lane, joined):
    count = len(tiles)
    left = [roll(v, 1, 1) for v in tiles]
    right = [roll(v, -1, 1) for v in tiles]
    out = []
    for j in range(count):
        west, east = left[j], right[j]
        if joined:
            west = jnp.where(lane == 0, left[j - 1], west)
            east = jnp.where(lane == LANES - 1, right[(j + 1) % count], east)
        out.append(jnp.minimum(tiles[j], jnp.minimum(west, east)))
    return out


def fine_sweep(src, dst, floor, stride, joined):
    count = src.shape[0]
    lane = lane_iota()

    def load(t):
        return [src[j, pl.ds(t, SUB, stride=stride), :] for j in range(count)]

    first = load(0)
    h_first = across_min(first, lane, joined)
    h_before = [roll(h, 1, 0) for h in across_min(load(stride - 1), lane, joined)]

    def advance(t, carry, after=None):
        h_up, h_here, here = carry
        if after is None:
            below = load(t + 1)
            h_down = across_min(below, lane, joined)
        else:
            below, h_down = here, after
        for j in range(count):
            low = jnp.minimum(jnp.minimum(h_up[j], h_down[j]), h_here[j])
            at = pl.ds(t, SUB, stride=stride)
            dst[j, at, :] = jnp.maximum(floor[j, at, :], jnp.minimum(here[j], low + fine_step))
        return h_here, h_down, below

    def body(q, carry):
        for u in range(UNROLL):
            carry = advance(q * UNROLL + u, carry)
        return carry

    loops = (stride - 1) // UNROLL
    carry = lax.fori_loop(0, loops, body, (h_before, h_first, first))
    for t in range(loops * UNROLL, stride - 1):
        carry = advance(t, carry)
    advance(stride - 1, carry, [roll(h, -1, 0) for h in h_first])


def all_sweeps(va, vb, floor, joined):
    stride = va.shape[1] // SUB

    def pair(i, carry):
        fine_sweep(va, vb, floor, stride, joined)
        fine_sweep(vb, va, floor, stride, joined)
        return carry

    lax.fori_loop(0, FINE // 2, pair, 0)


def padded_rows(rows):
    stride = -(-(rows + 2 * FINE) // SUB)
    return SUB * (stride + 1 - stride % 2)


def turned_sweep(count, planes, load, store, floor):
    def across(tiles):
        up = [roll(tiles[planes - 1], 1, 1)] + tiles[:-1]
        down = tiles[1:] + [roll(tiles[0], -1, 1)]
        return [jnp.minimum(jnp.minimum(u, v), d) for u, v, d in zip(up, tiles, down)]

    first = load(0)
    h_first = across(first)
    h_before = [roll(h, 1, 0) for h in across(load(count - 1))]

    def advance(t, carry, after=None):
        h_west, h_here, here = carry
        if after is None:
            east = load(t + 1)
            h_east = across(east)
        else:
            east, h_east = here, after
        for c in range(planes):
            low = jnp.minimum(jnp.minimum(h_west[c], h_east[c]), h_here[c])
            store(c, t, jnp.maximum(floor[c, t], jnp.minimum(here[c], low + fine_step)))
        return h_here, h_east, east

    def body(q, carry):
        for u in range(UNROLL_T):
            carry = advance(q * UNROLL_T + u, carry)
        return carry

    loops = (count - 1) // UNROLL_T
    carry = lax.fori_loop(0, loops, body, (h_before, h_first, first))
    for t in range(loops * UNROLL_T, count - 1):
        carry = advance(t, carry)
    advance(count - 1, carry, [roll(h, -1, 0) for h in h_first])


def main_kernel(ground_t, lock_t, stats_t, out, va, vb, floor, coarse, turned, natural, sems):
    tiles, rows, _ = natural.shape
    planes = rows // LANES
    margin, chunk = interior(tiles)
    first = plane_row(margin, tiles)
    pitch = chunk + 1
    value = stats_t[2]
    for _ in range(COARSE):
        across = jnp.minimum(value, jnp.minimum(roll(value, 1, 0), roll(value, -1, 0)))
        reach = BLK // planes
        around = jnp.minimum(across, jnp.minimum(roll(across, reach, 1), roll(across, -reach, 1)))
        lowered = jnp.minimum(value, around + coarse_step)
        value = jnp.minimum(jnp.maximum(stats_t[0], lowered), stats_t[1])
    coarse[...] = value

    def start(b, carry):
        c_value = coarse[pl.ds(margin // BLK + b, SUB, stride=chunk // BLK), :]
        for u in range(BLK):
            t = b * BLK + u
            at = pl.ds(first + t, SUB, stride=pitch)
            for c in range(planes):
                va[c, t], floor[c, t] = start_tile(ground_t[c, at, :], lock_t[c, at, :], c_value)
        return carry

    lax.fori_loop(0, chunk // BLK, start, 0)

    def sweep(src, dst):
        def store(c, t, value):
            dst[c, t] = value

        turned_sweep(chunk, planes, lambda t: [src[c, t] for c in range(planes)], store, floor)

    def pair(i, carry):
        sweep(va, vb)
        sweep(vb, va)
        return carry

    lax.fori_loop(0, FINE // 2 - 1, pair, 0)
    sweep(va, vb)

    def store_last(c, t, value):
        turned[c, pl.ds(first + t, SUB, stride=pitch), :] = value

    turned_sweep(chunk, planes, lambda t: [vb[c, t] for c in range(planes)], store_last, floor)
    cols = tiles * LANES
    for c in range(planes):
        for col in list(range(0, margin, SUB)) + list(range(cols - margin, cols, SUB)):
            at = plane_row(col, tiles)
            turned[c, at : at + SUB, :] = jnp.zeros((SUB, LANES), jnp.float32)

    keep = pl.ds(margin + FINE, rows - 2 * margin - 2 * FINE)

    def copy_out(j):
        cols_j = pl.ds(pl.multiple_of(j * LANES, LANES), LANES)
        return pltpu.make_async_copy(natural.at[j, keep, :], out.at[keep, cols_j], sems.at[j])

    def finish(j, carry):
        for c in range(planes):
            parts = []
            for v in range(LANES // SUB):
                at = plane_row(j * LANES + v * SUB, tiles)
                parts.append(turned[c, pl.ds(at, SUB), :])
            back = jnp.concatenate(parts, axis=0).T
            for a in range(LANES // SUB):
                natural[j, pl.ds(a * SUB * planes + c, SUB, stride=planes), :] = back[
                    a * SUB : (a + 1) * SUB
                ]
        copy_out(j).start()
        return carry

    lax.fori_loop(0, tiles, finish, 0)
    for j in range(tiles):
        copy_out(j).wait()


def main_part(ground_t, lock_t, stats_t):
    planes, length, _ = ground_t.shape
    tiles = stats_t.shape[1] * BLK // LANES
    rows = planes * LANES
    chunk = interior(tiles)[1]
    vmem = pl.BlockSpec(memory_space=pltpu.VMEM)
    tall = (planes, chunk, SUB, LANES)
    f32 = jnp.float32
    return pl.pallas_call(
        main_kernel,
        in_specs=[vmem] * 3,
        out_specs=pl.BlockSpec(memory_space=pltpu.HBM),
        out_shape=jax.ShapeDtypeStruct((rows, tiles * LANES), f32),
        scratch_shapes=[
            pltpu.VMEM(tall, f32),
            pltpu.VMEM(tall, f32),
            pltpu.VMEM(tall, f32),
            pltpu.VMEM(stats_t.shape[1:], f32),
            pltpu.VMEM((planes, length, LANES), f32),
            pltpu.VMEM((tiles, rows, LANES), f32),
            pltpu.SemaphoreType.DMA((tiles,)),
        ],
        compiler_params=pltpu.CompilerParams(vmem_limit_bytes=24 * MIB),
        cost_estimate=pl.CostEstimate(flops=100_000_000, bytes_accessed=20_000_000, transcendentals=0),
        name="middle",
    )(ground_t, lock_t, stats_t)


def bands_kernel(ground, lock, stats, from_north, from_south, partial, out, va, vb, floor, lifted, sems):
    tiles, rows, _ = ground.shape
    blocks = rows // BLK
    height = va.shape[2]
    inner = height - FINE
    at_north, at_south = edges()
    coarse = coarse_sweeps(*coarse_fields(stats, from_north, from_south))
    lane = lane_iota(coarse.shape)
    for j in range(tiles):
        lifted[j] = gather_lanes(coarse, lane // BLK + 8 * j)
    for side, (band, is_edge, at_band, at_inner, first) in enumerate(
        ((from_north, at_north, 0, FINE, 0), (from_south, at_south, inner, 0, rows - inner))
    ):
        for j in range(tiles):

            def put(at, g, k, c_row):
                c = lifted[j, c_row : c_row + 1, :]
                v, low = start_tile(g, k, c)
                va[side, j, at : at + SUB, :] = v
                floor[side, j, at : at + SUB, :] = low

            put(
                at_band,
                sealed(band[j, 0:FINE, :], is_edge),
                sealed(band[j, FINE:, :], is_edge),
                HALO_C - 1 if side == 0 else HALO_C + blocks,
            )
            for i in range(inner // SUB):
                at = slice(first + i * SUB, first + (i + 1) * SUB)
                c_row = HALO_C + (first + i * SUB) // BLK
                put(at_inner + i * SUB, ground[j, at, :], lock[j, at, :], c_row)

    def pair(i, carry):
        for src, dst in ((va, vb), (vb, va)):
            for side in range(2):
                fine_sweep(src.at[side], dst.at[side], floor.at[side], height // SUB, True)
        return carry

    lax.fori_loop(0, FINE // 2, pair, 0)
    valid = inner - FINE
    copies = []
    for side, (at, to) in enumerate(((FINE, 0), (FINE, rows - valid))):
        for j in range(tiles):
            copies.append(
                pltpu.make_async_copy(
                    va.at[side, j, pl.ds(at, valid), :],
                    out.at[pl.ds(to, valid), pl.ds(j * LANES, LANES)],
                    sems.at[side, j],
                )
            )
            copies[-1].start()
    for copy in copies:
        copy.wait()


def bands(ground, lock, stats, from_north, from_south, partial):
    tiles, rows, _ = ground.shape
    blocks = rows // BLK
    vmem = pl.BlockSpec(memory_space=pltpu.VMEM)
    hbm = pl.BlockSpec(memory_space=pltpu.HBM)
    tall = (2, tiles, COARSE * BLK + 3 * FINE, LANES)
    f32 = jnp.float32
    return pl.pallas_call(
        bands_kernel,
        in_specs=[vmem] * 5 + [hbm],
        out_specs=hbm,
        out_shape=jax.ShapeDtypeStruct(partial.shape, f32),
        input_output_aliases={5: 0},
        scratch_shapes=[
            pltpu.VMEM(tall, f32),
            pltpu.VMEM(tall, f32),
            pltpu.VMEM(tall, f32),
            pltpu.VMEM((tiles, blocks + 2 * HALO_C, LANES), f32),
            pltpu.SemaphoreType.DMA((2, tiles)),
        ],
        compiler_params=pltpu.CompilerParams(vmem_limit_bytes=16 * MIB),
        cost_estimate=pl.CostEstimate(flops=60_000_000, bytes_accessed=12_000_000, transcendentals=0),
        name="bands",
    )(ground, lock, stats, from_north, from_south, partial)


def column_sources(rows, blocks):
    fine = (rows + 2 * FINE) // SUB
    coarse = (blocks + 2 * HALO_C) // SUB
    return fine, coarse, -(-(2 * fine + 3 * coarse) // 16)


def pack_kernel(g_first, k_first, g_last, k_last, stats, from_north, from_south, west, east):
    rows = g_first.shape[1]
    blocks = rows // BLK
    tiles = from_north.shape[0] - 2
    at_north, at_south = edges()
    group = lane_iota() // 8
    fields = coarse_fields(stats, from_north, from_south)
    fine, coarse, slots = column_sources(rows, blocks)
    coarse_cols = tiles * LANES // BLK
    for dst, g_ref, k_ref, j, lane_at, lane_at_c in (
        (west, g_first, k_first, 0, 0, 0),
        (east, g_last, k_last, tiles - 1, LANES - 8, coarse_cols - 8),
    ):
        sources = []
        for half, ref in ((0, g_ref), (1, k_ref)):
            at = half * FINE
            sources.append((sealed(from_north[j, at : at + FINE, :], at_north), lane_at))
            for i in range(rows // SUB):
                sources.append((ref[0, i * SUB : (i + 1) * SUB, :], lane_at))
            sources.append((sealed(from_south[j, at : at + FINE, :], at_south), lane_at))
        for field in fields:
            for i in range(coarse):
                sources.append((field[i * SUB : (i + 1) * SUB], lane_at_c))
        for slot in range(slots):
            packed = jnp.zeros((SUB, LANES), jnp.float32)
            for n, (value, at) in enumerate(sources[slot * 16 : slot * 16 + 16]):
                packed = jnp.where(group == n, roll(value, 8 * n - at, 1), packed)
            dst[slot * SUB : (slot + 1) * SUB, :] = packed


def pack_columns(ground, lock, stats, from_north, from_south):
    tiles, rows, _ = ground.shape
    blocks = rows // BLK
    slots = column_sources(rows, blocks)[2]
    first = pl.BlockSpec((1, rows, LANES), lambda i: (0, 0, 0))
    last = pl.BlockSpec((1, rows, LANES), lambda i: (tiles - 1, 0, 0))
    whole = lambda x: pl.BlockSpec(x.shape, lambda i: (0,) * x.ndim)
    out = jax.ShapeDtypeStruct((slots * SUB, LANES), jnp.float32)
    return pl.pallas_call(
        pack_kernel,
        grid=(1,),
        in_specs=[first, first, last, last, whole(stats), whole(from_north), whole(from_south)],
        out_specs=[whole(out), whole(out)],
        out_shape=[out, out],
        compiler_params=pltpu.CompilerParams(vmem_limit_bytes=8 * MIB),
        name="pack",
    )(ground, lock, ground, lock, stats, from_north, from_south)


def strip_kernel(
    g_first, k_first, g_last, k_last, stats, from_north, from_south, from_west, from_east, partial,
    out, va, vb, floor, lifted, edge, in_sems, out_sems,
):
    rows = g_first.shape[1]
    blocks = rows // BLK
    tiles = from_north.shape[0] - 2
    coarse_cols = tiles * LANES // BLK
    at_north, at_south = edges()
    lane = lane_iota()
    fine, coarse, slots = column_sources(rows, blocks)
    edge_cols = [pl.ds(0, LANES), pl.ds((tiles - 1) * LANES, LANES)]
    loads = [
        pltpu.make_async_copy(partial.at[:, edge_cols[j]], edge.at[j], in_sems.at[j])
        for j in range(2)
    ]
    for copy in loads:
        copy.start()

    def piece(ref, n, to):
        value = ref[(n // 16) * SUB : (n // 16 + 1) * SUB, :]
        return roll(value, to - 8 * (n % 16), 1)

    fields = []
    for which, field in enumerate(coarse_fields(stats, from_north, from_south)):
        parts = []
        for i in range(coarse):
            n = 2 * fine + which * coarse + i
            here = field[i * SUB : (i + 1) * SUB]
            here = jnp.where(lane // 8 == coarse_cols // 8, piece(from_east, n, coarse_cols), here)
            here = jnp.where(lane // 8 == 15, piece(from_west, n, LANES - 8), here)
            parts.append(here)
        fields.append(jnp.concatenate(parts, axis=0))
    value = coarse_sweeps(*fields)
    wide = lane_iota(value.shape)
    lifted[0] = gather_lanes(value, ((wide - 8) >> 4) & (LANES - 1))
    lifted[1] = gather_lanes(value, coarse_cols - 8 + ((wide + 8) >> 4))

    for strip, (g_ref, k_ref, j, source) in enumerate(
        ((g_first, k_first, 0, from_west), (g_last, k_last, tiles - 1, from_east))
    ):
        outer = lane // 8 == (0 if strip == 0 else 15)
        shift = 8 if strip == 0 else -8
        to = 0 if strip == 0 else LANES - 8
        for i in range(fine):
            if i == 0:
                here = [sealed(from_north[j, h * FINE : (h + 1) * FINE, :], at_north) for h in range(2)]
            elif i == fine - 1:
                here = [sealed(from_south[j, h * FINE : (h + 1) * FINE, :], at_south) for h in range(2)]
            else:
                here = [ref[0, (i - 1) * SUB : i * SUB, :] for ref in (g_ref, k_ref)]
            both = [
                jnp.where(outer, piece(source, h * fine + i, to), roll(here[h], shift, 1))
                for h in range(2)
            ]
            c_row = (i + 2 * HALO_C - 1) // 2
            v, low = start_tile(both[0], both[1], lifted[strip, c_row : c_row + 1, :])
            va[strip, i * SUB : (i + 1) * SUB, :] = v
            floor[strip, i * SUB : (i + 1) * SUB, :] = low
        rest = va.shape[1] - fine * SUB
        if rest:
            fill = jnp.full((rest, LANES), huge_level, jnp.float32)
            va[strip, fine * SUB :, :] = fill
            floor[strip, fine * SUB :, :] = fill

    all_sweeps(va, vb, floor, False)
    for copy in loads:
        copy.wait()
    stores = []
    for strip in range(2):
        inner = (lane < LANES - 16) if strip == 0 else (lane >= 16)
        for i in range(rows // SUB):
            at = slice(i * SUB, (i + 1) * SUB)
            moved = roll(va[strip, FINE + i * SUB : FINE + (i + 1) * SUB, :], -8 if strip == 0 else 8, 1)
            edge[strip, at, :] = jnp.where(inner, moved, edge[strip, at, :])
        stores.append(
            pltpu.make_async_copy(edge.at[strip], out.at[:, edge_cols[strip]], out_sems.at[strip])
        )
        stores[-1].start()
    for copy in stores:
        copy.wait()


def strips(ground, lock, stats, from_north, from_south, from_west, from_east, partial):
    tiles, rows, _ = ground.shape
    blocks = rows // BLK
    first = pl.BlockSpec((1, rows, LANES), lambda i: (0, 0, 0))
    last = pl.BlockSpec((1, rows, LANES), lambda i: (tiles - 1, 0, 0))
    whole = lambda x: pl.BlockSpec(x.shape, lambda i: (0,) * x.ndim)
    hbm = pl.BlockSpec(memory_space=pl.ANY)
    tall = (2, padded_rows(rows), LANES)
    small = [stats, from_north, from_south, from_west, from_east]
    return pl.pallas_call(
        strip_kernel,
        grid=(1,),
        in_specs=[first, first, last, last] + [whole(x) for x in small] + [hbm],
        out_specs=hbm,
        out_shape=jax.ShapeDtypeStruct(partial.shape, jnp.float32),
        input_output_aliases={9: 0},
        scratch_shapes=[
            pltpu.VMEM(tall, jnp.float32),
            pltpu.VMEM(tall, jnp.float32),
            pltpu.VMEM(tall, jnp.float32),
            pltpu.VMEM((2, blocks + 2 * HALO_C, LANES), jnp.float32),
            pltpu.VMEM((2, rows, LANES), jnp.float32),
            pltpu.SemaphoreType.DMA((2,)),
            pltpu.SemaphoreType.DMA((2,)),
        ],
        compiler_params=pltpu.CompilerParams(vmem_limit_bytes=12 * MIB),
        name="strips",
    )(ground, lock, ground, lock, *small, partial)


def ring(value, axis, shift):
    count = lax.axis_size(axis)
    return lax.ppermute(value, axis, [(i, (i + shift) % count) for i in range(count)])


def shards(elevation, ocean, outlet):
    ground, lock, ground_t, lock_t, stats, stats_t, north, south = prepare(elevation, ocean, outlet)
    from_south = ring(north, "row", -1)
    from_north = ring(south, "row", 1)
    partial = main_part(ground_t, lock_t, stats_t)
    from_north, from_south, partial = lax.optimization_barrier((from_north, from_south, partial))
    rows_args = (ground, lock, stats, from_north, from_south)
    west, east = pack_columns(*rows_args)
    from_east = ring(west, "col", -1)
    from_west = ring(east, "col", 1)
    partial = bands(*rows_args, partial)
    return strips(*rows_args, from_west, from_east, partial)


def solution(mesh):
    return jax.shard_map(
        shards,
        mesh=mesh,
        in_specs=(P("row", "col"), P("row", "col"), P("row", "col")),
        out_specs=P("row", "col"),
        check_vma=False,
    )
```

```python
import functools

import jax
import jax.numpy as jnp
from jax import lax
from jax.experimental import pallas as pl
from jax.experimental.pallas import tpu as pltpu
from jax.sharding import PartitionSpec as P

BLK = 16
COARSE = 4
FINE = 8
LANES = 128
SUB = 8
HALO_C = 8
UNROLL = 22
UNROLL_T = 37

huge_level = 1e30
fine_step = 2.0 ** (-10)
coarse_step = 2.0 ** (-6)
MIB = 2**20


def roll(x, shift, axis):
    return pltpu.roll(x, shift % x.shape[axis], axis)


def lane_iota(shape=(SUB, LANES)):
    return lax.broadcasted_iota(jnp.int32, shape, 1)


def gather_lanes(x, index):
    return jnp.take_along_axis(x, index, axis=1, mode="promise_in_bounds")


def interior(tiles):
    margin = COARSE * BLK
    chunk = (tiles * LANES - 2 * margin) // SUB
    return margin, chunk


def plane_row(col, tiles):
    margin, chunk = interior(tiles)
    return col + (col + chunk - margin) // chunk


def plane_rows(tiles):
    return -(-(plane_row(tiles * LANES, tiles) + 1) // SUB) * SUB


def prepare_kernel(
    elev, ocean, outlet, floor, lock, floor_t, lock_t, stats, stats_t, north, south,
    elev_buf, ocean_buf, outlet_buf, turn, sems,
):
    tiles, rows, _ = floor.shape
    planes = rows // LANES
    blocks = rows // BLK
    lane = lane_iota()
    sub = lax.broadcasted_iota(jnp.int32, (SUB, LANES), 0)

    def copies(j):
        cols = pl.ds(pl.multiple_of(j * LANES, LANES), LANES)
        return [
            pltpu.make_async_copy(src.at[:, cols], dst.at[j], sems.at[n, j])
            for n, (src, dst) in enumerate(
                ((elev, elev_buf), (ocean, ocean_buf), (outlet, outlet_buf))
            )
        ]

    for j in range(tiles):
        for copy in copies(j):
            copy.start()
    turn[...] = jnp.zeros(turn.shape, jnp.float32)
    for band in (north, south):
        band[tiles:, :, :] = jnp.zeros((2, 2 * FINE, LANES), jnp.float32)

    def tile(j, carry):
        for copy in copies(j):
            copy.wait()
        is_ocean = ocean_buf[j] == 1
        g = jnp.where(is_ocean, jnp.float32(0.0), elev_buf[j])
        k = jnp.where(is_ocean | (outlet_buf[j] == 1), g, jnp.float32(huge_level))
        low = jnp.minimum(g, k)
        elev_buf[j] = g
        floor[j] = low
        lock[j] = k
        north[j, 0:FINE, :] = low[0:FINE]
        north[j, FINE:, :] = k[0:FINE]
        south[j, 0:FINE, :] = low[rows - FINE :]
        south[j, FINE:, :] = k[rows - FINE :]
        found = [[None] * 8 for _ in range(3)]
        for c in range(planes):
            turned = [
                jnp.concatenate(
                    [
                        ref[j, pl.ds(a * SUB * planes + c, SUB, stride=planes), :]
                        for a in range(LANES // SUB)
                    ],
                    axis=0,
                ).T
                for ref in (elev_buf, lock)
            ]
            for v in range(LANES // SUB):
                g, k = (x[v * SUB : (v + 1) * SUB] for x in turned)
                at = plane_row(j * LANES + v * SUB, tiles)
                floor_t[c, pl.ds(at, SUB), :] = jnp.minimum(g, k)
                lock_t[c, pl.ds(at, SUB), :] = k
                for to, pick, value in ((0, jnp.minimum, g), (1, jnp.minimum, k), (2, jnp.maximum, g)):
                    old = found[to][v // 2]
                    found[to][v // 2] = value if old is None else pick(old, value)
        for which in range(3):
            pick = jnp.maximum if which == 2 else jnp.minimum
            total = None
            for b in range(8):
                value = found[which][b]
                for shift in (4, 2, 1):
                    value = pick(value, roll(value, shift, 0))
                total = value if b == 0 else jnp.where(sub == b, value, total)
            for swap in (1, 2):
                total = pick(total, gather_lanes(total, lane ^ swap))
            at = pl.ds(pl.multiple_of(j * SUB, SUB), SUB)
            stats_t[which, at, :] = total
            turn[which, at, :] = total
        return carry

    lax.fori_loop(0, tiles, tile, 0)
    for which in range(3):
        turn[which] = turn[which].T
        for q in range(blocks // SUB):
            stats[which * blocks + q * SUB : which * blocks + (q + 1) * SUB, :] = turn[
                which, pl.ds(q * SUB * BLK // planes, SUB, stride=BLK // planes), :
            ]
        slot = tiles + which // 2
        at = (which % 2) * HALO_C
        first = which * blocks
        north[slot, at : at + HALO_C, :] = stats[first : first + HALO_C, :]
        south[slot, at : at + HALO_C, :] = stats[first + blocks - HALO_C : first + blocks, :]


def prepare(elevation, ocean, outlet):
    rows, cols = elevation.shape
    tiles = cols // LANES
    f32 = jnp.float32
    hbm = pl.BlockSpec(memory_space=pltpu.HBM)
    vmem = pl.BlockSpec(memory_space=pltpu.VMEM)
    natural = (tiles, rows, LANES)
    turned = (rows // LANES, plane_rows(tiles), LANES)
    band = (tiles + 2, 2 * FINE, LANES)
    shapes = [natural, natural, turned, turned, (3 * rows // BLK, LANES), (3, cols // BLK, LANES), band, band]
    return pl.pallas_call(
        prepare_kernel,
        in_specs=[hbm] * 3,
        out_specs=[vmem] * len(shapes),
        out_shape=[jax.ShapeDtypeStruct(shape, f32) for shape in shapes],
        scratch_shapes=[
            pltpu.VMEM(natural, f32),
            pltpu.VMEM(natural, jnp.int32),
            pltpu.VMEM(natural, jnp.int32),
            pltpu.VMEM((3, LANES, LANES), f32),
            pltpu.SemaphoreType.DMA((3, tiles)),
        ],
        compiler_params=pltpu.CompilerParams(vmem_limit_bytes=24 * MIB),
        name="prepare",
    )(*(pltpu.with_memory_space_constraint(x, pltpu.HBM) for x in (elevation, ocean, outlet)))


def sealed(value, is_edge):
    return jnp.where(is_edge, jnp.float32(huge_level), value)


def edges():
    pos = lax.axis_index("row")
    return pos == 0, pos == lax.axis_size("row") - 1


def coarse_fields(stats, from_north, from_south):
    tiles = from_north.shape[0] - 2
    blocks = stats.shape[0] // 3
    at_north, at_south = edges()
    fields = []
    for which in range(3):
        slot = tiles + which // 2
        at = (which % 2) * HALO_C
        top = sealed(from_north[slot, at : at + HALO_C, :], at_north)
        low = sealed(from_south[slot, at : at + HALO_C, :], at_south)
        mid = stats[which * blocks : (which + 1) * blocks, :]
        fields.append(jnp.concatenate([top, mid, low], axis=0))
    return fields


def coarse_sweeps(ground_c, lock_c, value):
    for _ in range(COARSE):
        across = jnp.minimum(value, jnp.minimum(roll(value, 1, 1), roll(value, -1, 1)))
        around = jnp.minimum(across, jnp.minimum(roll(across, 1, 0), roll(across, -1, 0)))
        lowered = jnp.minimum(value, around + coarse_step)
        value = jnp.minimum(jnp.maximum(ground_c, lowered), lock_c)
    return value


def start_value(floor, lock, lifted):
    return jnp.maximum(floor, jnp.minimum(lifted, lock))


def across_min(tiles, lane, joined):
    count = len(tiles)
    left = [roll(v, 1, 1) for v in tiles]
    right = [roll(v, -1, 1) for v in tiles]
    out = []
    for j in range(count):
        west, east = left[j], right[j]
        if joined:
            west = jnp.where(lane == 0, left[j - 1], west)
            east = jnp.where(lane == LANES - 1, right[(j + 1) % count], east)
        out.append(jnp.minimum(tiles[j], jnp.minimum(west, east)))
    return out


def fine_sweep(src, dst, floor, stride, joined):
    count = src.shape[0]
    lane = lane_iota()

    def load(t):
        return [src[j, pl.ds(t, SUB, stride=stride), :] for j in range(count)]

    first = load(0)
    h_first = across_min(first, lane, joined)
    h_before = [roll(h, 1, 0) for h in across_min(load(stride - 1), lane, joined)]

    def advance(t, carry, after=None):
        h_up, h_here, here = carry
        if after is None:
            below = load(t + 1)
            h_down = across_min(below, lane, joined)
        else:
            below, h_down = here, after
        for j in range(count):
            low = jnp.minimum(jnp.minimum(h_up[j], h_down[j]), h_here[j])
            at = pl.ds(t, SUB, stride=stride)
            dst[j, at, :] = jnp.maximum(floor[j, at, :], jnp.minimum(here[j], low + fine_step))
        return h_here, h_down, below

    def body(q, carry):
        for u in range(UNROLL):
            carry = advance(q * UNROLL + u, carry)
        return carry

    loops = (stride - 1) // UNROLL
    carry = lax.fori_loop(0, loops, body, (h_before, h_first, first))
    for t in range(loops * UNROLL, stride - 1):
        carry = advance(t, carry)
    advance(stride - 1, carry, [roll(h, -1, 0) for h in h_first])


def turned_sweeps(count, planes, load, store, load_floor):
    def across(tiles):
        up = [roll(tiles[planes - 1], 1, 1)] + tiles[:-1]
        down = tiles[1:] + [roll(tiles[0], -1, 1)]
        return [jnp.minimum(jnp.minimum(u, v), d) for u, v, d in zip(up, tiles, down)]

    def lowered(west, here, east, value, low):
        out = []
        for w, h, e, v, f in zip(west, here, east, value, low):
            around = jnp.minimum(jnp.minimum(w, e), h)
            out.append(jnp.maximum(f, jnp.minimum(v, around + fine_step)))
        return out

    def eastward(tiles):
        return [roll(h, 1, 0) for h in tiles]

    def westward(tiles):
        return [roll(h, -1, 0) for h in tiles]

    value_a, value_b, value_z = load(0), load(1), load(count - 1)
    h_a, h_b, h_z = across(value_a), across(value_b), across(value_z)
    h_y = across(load(count - 2))
    low_a = load_floor(0)
    once_z = lowered(h_y, h_z, westward(h_a), value_z, load_floor(count - 1))
    once_a = lowered(eastward(h_z), h_a, h_b, value_a, low_a)
    g_a = across(once_a)

    def advance(t, carry, h_next=None, g_next=None):
        h_here, h_east, v_east, g_west, g_here, once, low = carry
        if g_next is None:
            v_next = v_east
            if h_next is None:
                v_next = load(t + 2)
                h_next = across(v_next)
            low_east = load_floor(t + 1)
            once_east = lowered(h_here, h_east, h_next, v_east, low_east)
            g_next = across(once_east)
            carry = (h_east, h_next, v_next, g_here, g_next, once_east, low_east)
        for c, value in enumerate(lowered(g_west, g_here, g_next, once, low)):
            store(c, t, value)
        return carry

    def body(q, carry):
        for u in range(UNROLL_T):
            carry = advance(q * UNROLL_T + u, carry)
        return carry

    loops = (count - 2) // UNROLL_T
    carry = (h_a, h_b, value_b, eastward(across(once_z)), g_a, once_a, low_a)
    carry = lax.fori_loop(0, loops, body, carry)
    for t in range(loops * UNROLL_T, count - 2):
        carry = advance(t, carry)
    carry = advance(count - 2, carry, h_next=westward(h_a))
    advance(count - 1, carry, g_next=westward(g_a))


def main_kernel(floor_t, lock_t, stats_t, natural, va, vb, coarse, turned):
    tiles, rows, _ = natural.shape
    planes = rows // LANES
    margin, chunk = interior(tiles)
    first = plane_row(margin, tiles)
    pitch = chunk + 1
    value = stats_t[2]
    for _ in range(COARSE):
        across = jnp.minimum(value, jnp.minimum(roll(value, 1, 0), roll(value, -1, 0)))
        reach = BLK // planes
        around = jnp.minimum(across, jnp.minimum(roll(across, reach, 1), roll(across, -reach, 1)))
        lowered = jnp.minimum(value, around + coarse_step)
        value = jnp.minimum(jnp.maximum(stats_t[0], lowered), stats_t[1])
    coarse[...] = value

    def strided(ref):
        return lambda t: [ref[c, pl.ds(first + t, SUB, stride=pitch), :] for c in range(planes)]

    load_floor, load_lock = strided(floor_t), strided(lock_t)

    def load_start(t):
        lifted = coarse[pl.ds(margin // BLK + t // BLK, SUB, stride=chunk // BLK), :]
        return [start_value(f, k, lifted) for f, k in zip(load_floor(t), load_lock(t))]

    passes = FINE // 2
    src = None
    for n in range(passes):
        dst = (va, vb)[n % 2]

        def load(t):
            return load_start(t) if src is None else [src[c, t] for c in range(planes)]

        def store(c, t, value):
            if n == passes - 1:
                turned[c, pl.ds(first + t, SUB, stride=pitch), :] = value
            else:
                dst[c, t] = value

        turned_sweeps(chunk, planes, load, store, load_floor)
        src = dst

    cols = tiles * LANES
    for c in range(planes):
        for col in list(range(0, margin, SUB)) + list(range(cols - margin, cols, SUB)):
            at = plane_row(col, tiles)
            turned[c, at : at + SUB, :] = jnp.zeros((SUB, LANES), jnp.float32)

    def finish(j, carry):
        for c in range(planes):
            parts = []
            for v in range(LANES // SUB):
                at = plane_row(j * LANES + v * SUB, tiles)
                parts.append(turned[c, pl.ds(at, SUB), :])
            back = jnp.concatenate(parts, axis=0).T
            for a in range(LANES // SUB):
                natural[j, pl.ds(a * SUB * planes + c, SUB, stride=planes), :] = back[
                    a * SUB : (a + 1) * SUB
                ]
        return carry

    lax.fori_loop(0, tiles, finish, 0, unroll=2)


def main_part(floor_t, lock_t, stats_t):
    planes, length, _ = floor_t.shape
    tiles = stats_t.shape[1] * BLK // LANES
    chunk = interior(tiles)[1]
    vmem = pl.BlockSpec(memory_space=pltpu.VMEM)
    tall = (planes, chunk, SUB, LANES)
    f32 = jnp.float32
    return pl.pallas_call(
        main_kernel,
        in_specs=[vmem] * 3,
        out_specs=vmem,
        out_shape=jax.ShapeDtypeStruct((tiles, planes * LANES, LANES), f32),
        scratch_shapes=[
            pltpu.VMEM(tall, f32),
            pltpu.VMEM(tall, f32),
            pltpu.VMEM(stats_t.shape[1:], f32),
            pltpu.VMEM((planes, length, LANES), f32),
        ],
        compiler_params=pltpu.CompilerParams(vmem_limit_bytes=16 * MIB),
        cost_estimate=pl.CostEstimate(flops=100_000_000, bytes_accessed=20_000_000, transcendentals=0),
        name="middle",
    )(floor_t, lock_t, stats_t)


def bands_kernel(floor_in, lock, stats, from_north, from_south, va, vb, floor, lifted):
    tiles, rows, _ = floor_in.shape
    blocks = rows // BLK
    height = va.shape[2]
    inner = height - FINE
    at_north, at_south = edges()
    coarse = coarse_sweeps(*coarse_fields(stats, from_north, from_south))
    lane = lane_iota(coarse.shape)
    for j in range(tiles):
        lifted[j] = gather_lanes(coarse, lane // BLK + 8 * j)
    for side, (band, is_edge, at_band, at_inner, first) in enumerate(
        ((from_north, at_north, 0, FINE, 0), (from_south, at_south, inner, 0, rows - inner))
    ):
        for j in range(tiles):

            def put(at, low, k, c_row):
                floor[side, j, at : at + SUB, :] = low
                va[side, j, at : at + SUB, :] = start_value(low, k, lifted[j, c_row : c_row + 1, :])

            put(
                at_band,
                sealed(band[j, 0:FINE, :], is_edge),
                sealed(band[j, FINE:, :], is_edge),
                HALO_C - 1 if side == 0 else HALO_C + blocks,
            )
            for i in range(inner // SUB):
                at = slice(first + i * SUB, first + (i + 1) * SUB)
                c_row = HALO_C + (first + i * SUB) // BLK
                put(at_inner + i * SUB, floor_in[j, at, :], lock[j, at, :], c_row)

    def pair(i, carry):
        for src, dst in ((va, vb), (vb, va)):
            for side in range(2):
                fine_sweep(src.at[side], dst.at[side], floor.at[side], height // SUB, True)
        return carry

    lax.fori_loop(0, FINE // 2, pair, 0)


def bands(floor, lock, stats, from_north, from_south):
    tiles, rows, _ = floor.shape
    blocks = rows // BLK
    vmem = pl.BlockSpec(memory_space=pltpu.VMEM)
    tall = (2, tiles, COARSE * BLK + 3 * FINE, LANES)
    f32 = jnp.float32
    return pl.pallas_call(
        bands_kernel,
        in_specs=[vmem] * 5,
        out_specs=vmem,
        out_shape=jax.ShapeDtypeStruct(tall, f32),
        scratch_shapes=[
            pltpu.VMEM(tall, f32),
            pltpu.VMEM(tall, f32),
            pltpu.VMEM((tiles, blocks + 2 * HALO_C, LANES), f32),
        ],
        compiler_params=pltpu.CompilerParams(vmem_limit_bytes=12 * MIB),
        cost_estimate=pl.CostEstimate(flops=60_000_000, bytes_accessed=12_000_000, transcendentals=0),
        name="bands",
    )(floor, lock, stats, from_north, from_south)


def strip_planes(rows):
    return -(-(rows + 2 * FINE) // LANES)


def pack_kernel(
    f_first, k_first, f_last, k_last, stats, from_north, from_south, west, east, turned, tall
):
    rows = f_first.shape[1]
    blocks = rows // BLK
    tiles = from_north.shape[0] - 2
    planes = turned.shape[2]
    at_north, at_south = edges()
    group = lane_iota() // 8
    fields = coarse_fields(stats, from_north, from_south)
    coarse = fields[0].shape[0] // SUB
    coarse_cols = tiles * LANES // BLK
    rest = tall.shape[2] - rows - 2 * FINE
    for side, (dst, refs, j, col_at, lane_at) in enumerate(
        (
            (west, (f_first, k_first), 0, 0, 0),
            (east, (f_last, k_last), tiles - 1, LANES - FINE, coarse_cols - 8),
        )
    ):
        for which, ref in enumerate(refs):
            at = slice(which * FINE, (which + 1) * FINE)
            tall[side, which, 0:FINE, :] = sealed(from_north[j, at, :], at_north)
            tall[side, which, FINE : FINE + rows, :] = ref[0]
            tall[side, which, FINE + rows : 2 * FINE + rows, :] = sealed(from_south[j, at, :], at_south)
            tall[side, which, 2 * FINE + rows :, :] = jnp.full((rest, LANES), huge_level, jnp.float32)
            for c in range(planes):
                parts = [
                    tall[side, which, pl.ds(a * SUB * planes + c, SUB, stride=planes), :]
                    for a in range(LANES // SUB)
                ]
                value = jnp.concatenate(parts, axis=0).T
                turned[side, which, c] = value
                slot = which * planes + c
                dst[slot * SUB : (slot + 1) * SUB, :] = value[col_at : col_at + FINE]
        sources = [field[i * SUB : (i + 1) * SUB] for field in fields for i in range(coarse)]
        for n in range(0, len(sources), 16):
            packed = jnp.zeros((SUB, LANES), jnp.float32)
            for m, value in enumerate(sources[n : n + 16]):
                packed = jnp.where(group == m, roll(value, 8 * m - lane_at, 1), packed)
            slot = 2 * planes + n // 16
            dst[slot * SUB : (slot + 1) * SUB, :] = packed


def pack_columns(floor, lock, stats, from_north, from_south):
    tiles, rows, _ = floor.shape
    blocks = rows // BLK
    planes = strip_planes(rows)
    slots = 2 * planes + -(-3 * (blocks + 2 * HALO_C) // SUB // 16)
    first = pl.BlockSpec((1, rows, LANES), lambda i: (0, 0, 0))
    last = pl.BlockSpec((1, rows, LANES), lambda i: (tiles - 1, 0, 0))
    whole = lambda x: pl.BlockSpec(x.shape, lambda i: (0,) * len(x.shape))
    f32 = jnp.float32
    out = jax.ShapeDtypeStruct((slots * SUB, LANES), f32)
    turned = jax.ShapeDtypeStruct((2, 2, planes, LANES, LANES), f32)
    return pl.pallas_call(
        pack_kernel,
        grid=(1,),
        in_specs=[first, first, last, last, whole(stats), whole(from_north), whole(from_south)],
        out_specs=[whole(out), whole(out), whole(turned)],
        out_shape=[out, out, turned],
        scratch_shapes=[pltpu.VMEM((2, 2, planes * LANES, LANES), f32)],
        compiler_params=pltpu.CompilerParams(vmem_limit_bytes=12 * MIB),
        name="pack",
    )(floor, lock, floor, lock, stats, from_north, from_south)


def strip_kernel(
    stats, from_north, from_south, turned, from_west, from_east, natural, banded,
    out, va, vb, floor, lifted, tall, edge, sems, edge_sems,
):
    tiles, rows, _ = natural.shape
    planes = turned.shape[2]
    coarse_cols = tiles * LANES // BLK
    lane = lane_iota()
    width = va.shape[2]
    inner = width - FINE
    valid = inner - FINE
    spans = (
        (pl.ds(0, valid), lambda j: banded.at[0, j, pl.ds(FINE, valid), :]),
        (pl.ds(valid, rows - 2 * valid), lambda j: natural.at[j, pl.ds(valid, rows - 2 * valid), :]),
        (pl.ds(rows - valid, valid), lambda j: banded.at[1, j, pl.ds(FINE, valid), :]),
    )
    copies = [
        pltpu.make_async_copy(part(j), out.at[span, pl.ds(j * LANES, LANES)], sems.at[n, j])
        for j in range(1, tiles - 1)
        for n, (span, part) in enumerate(spans)
    ]
    for copy in copies:
        copy.start()

    def piece(ref, n, to):
        slot = 2 * planes + n // 16
        return roll(ref[slot * SUB : (slot + 1) * SUB, :], to - 8 * (n % 16), 1)

    fields = []
    for which, field in enumerate(coarse_fields(stats, from_north, from_south)):
        parts = []
        count = field.shape[0] // SUB
        for i in range(count):
            n = which * count + i
            here = field[i * SUB : (i + 1) * SUB]
            here = jnp.where(lane // 8 == coarse_cols // 8, piece(from_east, n, coarse_cols), here)
            here = jnp.where(lane // 8 == 15, piece(from_west, n, LANES - 8), here)
            parts.append(here)
        fields.append(jnp.concatenate(parts, axis=0))
    value = coarse_sweeps(*fields)
    value = jnp.concatenate([value, jnp.zeros((LANES - value.shape[0], LANES), jnp.float32)], axis=0).T
    for c in range(planes):
        index = (planes * lane + (c + HALO_C * BLK - FINE)) // BLK
        for side, groups in enumerate(((LANES - 8, 0), (coarse_cols - 8, coarse_cols))):
            for n, at in enumerate(groups):
                lifted[side, c, n * SUB : (n + 1) * SUB, :] = gather_lanes(value[at : at + SUB], index)

    for side, ref in enumerate((from_west, from_east)):
        for c in range(planes):
            for i in range(width // SUB):
                if (side, i) in ((0, 0), (1, width // SUB - 1)):
                    low, k = (ref[(w * planes + c) * SUB : (w * planes + c + 1) * SUB, :] for w in range(2))
                else:
                    col = (i - 1) * SUB if side == 0 else LANES - inner + i * SUB
                    low, k = (turned[side, w, c, col : col + SUB, :] for w in range(2))
                c_row = (i + 15) // 2 if side == 0 else 8 - COARSE - 1 + i // 2
                at = slice(i * SUB, (i + 1) * SUB)
                floor[side, c, at, :] = low
                va[side, c, at, :] = start_value(low, k, lifted[side, c, c_row : c_row + 1, :])

    count = width // SUB

    def strided(ref, side):
        return lambda t: [ref[side, c, pl.ds(t, SUB, stride=count), :] for c in range(planes)]

    def twice(i, carry):
        for src, dst in ((va, vb), (vb, va)):
            for side in range(2):

                def store(c, t, value):
                    dst[side, c, pl.ds(t, SUB, stride=count), :] = value

                turned_sweeps(count, planes, strided(src, side), store, strided(floor, side))
        return carry

    lax.fori_loop(0, FINE // 4, twice, 0)

    stores = []
    for side, j in enumerate((0, tiles - 1)):
        fill = jnp.zeros((LANES - inner, LANES), jnp.float32)
        for c in range(planes):
            parts = [va[side, c, FINE:, :], fill] if side == 0 else [fill, va[side, c, 0:inner, :]]
            back = jnp.concatenate(parts, axis=0).T
            for a in range(LANES // SUB):
                tall[side, pl.ds(a * SUB * planes + c, SUB, stride=planes), :] = back[a * SUB : (a + 1) * SUB]
        mine = (lane < valid) if side == 0 else (lane >= LANES - valid)
        for i in range(rows // SUB):
            at = i * SUB
            if at < valid:
                other = banded[0, j, FINE + at : FINE + at + SUB, :]
            elif at >= rows - valid:
                at_band = FINE + at - (rows - valid)
                other = banded[1, j, at_band : at_band + SUB, :]
            else:
                other = natural[j, at : at + SUB, :]
            edge[side, at : at + SUB, :] = jnp.where(mine, tall[side, FINE + at : FINE + at + SUB, :], other)
        stores.append(
            pltpu.make_async_copy(edge.at[side], out.at[:, pl.ds(j * LANES, LANES)], edge_sems.at[side])
        )
        stores[-1].start()
    for copy in copies + stores:
        copy.wait()


def strips(stats, from_north, from_south, turned, from_west, from_east, natural, banded):
    tiles, rows, _ = natural.shape
    planes = turned.shape[2]
    vmem = pl.BlockSpec(memory_space=pltpu.VMEM)
    wide = (2, planes, COARSE * BLK + 3 * FINE, LANES)
    f32 = jnp.float32
    return pl.pallas_call(
        strip_kernel,
        in_specs=[vmem] * 8,
        out_specs=pl.BlockSpec(memory_space=pltpu.HBM),
        out_shape=jax.ShapeDtypeStruct((rows, tiles * LANES), f32),
        scratch_shapes=[
            pltpu.VMEM(wide, f32),
            pltpu.VMEM(wide, f32),
            pltpu.VMEM(wide, f32),
            pltpu.VMEM((2, planes, 2 * SUB, LANES), f32),
            pltpu.VMEM((2, planes * LANES, LANES), f32),
            pltpu.VMEM((2, rows, LANES), f32),
            pltpu.SemaphoreType.DMA((3, tiles)),
            pltpu.SemaphoreType.DMA((2,)),
        ],
        compiler_params=pltpu.CompilerParams(vmem_limit_bytes=12 * MIB),
        name="strips",
    )(stats, from_north, from_south, turned, from_west, from_east, natural, banded)


def ring(value, axis, shift):
    count = lax.axis_size(axis)
    return lax.ppermute(value, axis, [(i, (i + shift) % count) for i in range(count)])


def shards(elevation, ocean, outlet):
    floor, lock, floor_t, lock_t, stats, stats_t, north, south = prepare(elevation, ocean, outlet)
    from_south = ring(north, "row", -1)
    from_north = ring(south, "row", 1)
    natural = main_part(floor_t, lock_t, stats_t)
    from_north, from_south, natural = lax.optimization_barrier((from_north, from_south, natural))
    halo_args = (stats, from_north, from_south)
    west, east, turned = pack_columns(floor, lock, *halo_args)
    from_east = ring(west, "col", -1)
    from_west = ring(east, "col", 1)
    banded = bands(floor, lock, *halo_args)
    return strips(*halo_args, turned, from_west, from_east, natural, banded)


def solution(mesh):
    return jax.shard_map(
        shards,
        mesh=mesh,
        in_specs=(P("row", "col"), P("row", "col"), P("row", "col")),
        out_specs=P("row", "col"),
        check_vma=False,
    )
```

```python
import functools

import jax
import jax.numpy as jnp
from jax import lax
from jax.experimental import pallas as pl
from jax.experimental.pallas import tpu as pltpu
from jax.sharding import PartitionSpec as P

BLK = 16
COARSE = 4
FINE = 8
LANES = 128
SUB = 8
HALO_C = 8
UNROLL_T = 112

huge_level = 1e30
fine_step = 2.0 ** (-10)
coarse_step = 2.0 ** (-6)
MIB = 2**20


def roll(x, shift, axis):
    return pltpu.roll(x, shift % x.shape[axis], axis)


def lane_iota(shape=(SUB, LANES)):
    return lax.broadcasted_iota(jnp.int32, shape, 1)


def gather_lanes(x, index):
    return jnp.take_along_axis(x, index, axis=1, mode="promise_in_bounds")


def interior(tiles):
    margin = COARSE * BLK
    chunk = (tiles * LANES - 2 * margin) // SUB
    return margin, chunk


def interior_planes(rows):
    return (rows - 2 * COARSE * BLK) // LANES


def plane_row(col, tiles):
    margin, chunk = interior(tiles)
    return col + (col + chunk - margin) // chunk


def plane_rows(tiles):
    return -(-(plane_row(tiles * LANES, tiles) + 1) // SUB) * SUB


def prepare_kernel(
    elev, ocean, outlet, floor, lock, floor_t, lock_t, stats, stats_t, north, south,
    elev_buf, ocean_buf, outlet_buf, turn, sems,
):
    tiles, rows, _ = floor.shape
    planes = floor_t.shape[0]
    margin = interior(tiles)[0]
    blocks = rows // BLK
    lane = lane_iota()
    sub = lax.broadcasted_iota(jnp.int32, (SUB, LANES), 0)
    unused = jnp.zeros((LANES - 3 * blocks, LANES), jnp.float32)

    def copies(j):
        cols = pl.ds(pl.multiple_of(j * LANES, LANES), LANES)
        return [
            pltpu.make_async_copy(src.at[:, cols], dst.at[j], sems.at[n, j])
            for n, (src, dst) in enumerate(
                ((elev, elev_buf), (ocean, ocean_buf), (outlet, outlet_buf))
            )
        ]

    for j in range(tiles):
        for copy in copies(j):
            copy.start()
    turn[...] = jnp.zeros(turn.shape, jnp.float32)
    for band in (north, south):
        band[tiles:, :, :] = jnp.zeros((2, 2 * FINE, LANES), jnp.float32)

    def tile(j, carry):
        for copy in copies(j):
            copy.wait()
        is_ocean = ocean_buf[j] == 1
        g = jnp.where(is_ocean, jnp.float32(0.0), elev_buf[j])
        k = jnp.where(is_ocean | (outlet_buf[j] == 1), g, jnp.float32(huge_level))
        low = jnp.minimum(g, k)
        elev_buf[j] = g
        floor[j] = low
        lock[j] = k
        north[j, 0:FINE, :] = low[0:FINE]
        north[j, FINE:, :] = k[0:FINE]
        south[j, 0:FINE, :] = low[rows - FINE :]
        south[j, FINE:, :] = k[rows - FINE :]
        for c in range(planes):
            turned = [
                jnp.concatenate(
                    [
                        ref[j, pl.ds(margin + a * SUB * planes + c, SUB, stride=planes), :]
                        for a in range(LANES // SUB)
                    ],
                    axis=0,
                ).T
                for ref in (elev_buf, lock)
            ]
            for v in range(LANES // SUB):
                g, k = (x[v * SUB : (v + 1) * SUB] for x in turned)
                at = plane_row(j * LANES + v * SUB, tiles)
                floor_t[c, pl.ds(at, SUB), :] = jnp.minimum(g, k)
                lock_t[c, pl.ds(at, SUB), :] = k
        found = [[], [], []]
        for q in range(blocks // SUB):
            for r in range(BLK):
                g, k = (ref[j, pl.ds(q * SUB * BLK + r, SUB, stride=BLK), :] for ref in (elev_buf, lock))
                low_g = g if r == 0 else jnp.minimum(low_g, g)
                low_k = k if r == 0 else jnp.minimum(low_k, k)
                high_g = g if r == 0 else jnp.maximum(high_g, g)
            for which, value in enumerate((low_g, low_k, -high_g)):
                found[which].append(value)
        turned = jnp.concatenate(found[0] + found[1] + found[2] + [unused], axis=0).T
        total = None
        for b in range(LANES // BLK):
            value = jnp.minimum(
                turned[b * BLK : b * BLK + SUB], turned[b * BLK + SUB : (b + 1) * BLK]
            )
            for shift in (4, 2, 1):
                value = jnp.minimum(value, roll(value, shift, 0))
            total = value if b == 0 else jnp.where(sub == b, value, total)
        total = jnp.where(lane // blocks == 2, -total, total)
        at = pl.ds(pl.multiple_of(j * SUB, SUB), SUB)
        stats_t[at, :] = total
        turn[at, :] = total
        return carry

    lax.fori_loop(0, tiles, tile, 0)
    stats[...] = turn[...].T[: 3 * blocks]
    for which in range(3):
        slot = tiles + which // 2
        at = (which % 2) * HALO_C
        first = which * blocks
        north[slot, at : at + HALO_C, :] = stats[first : first + HALO_C, :]
        south[slot, at : at + HALO_C, :] = stats[first + blocks - HALO_C : first + blocks, :]


def prepare(elevation, ocean, outlet):
    rows, cols = elevation.shape
    tiles = cols // LANES
    f32 = jnp.float32
    hbm = pl.BlockSpec(memory_space=pltpu.HBM)
    vmem = pl.BlockSpec(memory_space=pltpu.VMEM)
    natural = (tiles, rows, LANES)
    turned = (interior_planes(rows), plane_rows(tiles), LANES)
    band = (tiles + 2, 2 * FINE, LANES)
    shapes = [natural, natural, turned, turned, (3 * rows // BLK, LANES), (cols // BLK, LANES), band, band]
    return pl.pallas_call(
        prepare_kernel,
        in_specs=[hbm] * 3,
        out_specs=[vmem] * len(shapes),
        out_shape=[jax.ShapeDtypeStruct(shape, f32) for shape in shapes],
        scratch_shapes=[
            pltpu.VMEM(natural, f32),
            pltpu.VMEM(natural, jnp.int32),
            pltpu.VMEM(natural, jnp.int32),
            pltpu.VMEM((LANES, LANES), f32),
            pltpu.SemaphoreType.DMA((3, tiles)),
        ],
        compiler_params=pltpu.CompilerParams(vmem_limit_bytes=24 * MIB),
        name="prepare",
    )(*(pltpu.with_memory_space_constraint(x, pltpu.HBM) for x in (elevation, ocean, outlet)))


def sealed(value, is_edge):
    return jnp.where(is_edge, jnp.float32(huge_level), value)


def edges():
    pos = lax.axis_index("row")
    return pos == 0, pos == lax.axis_size("row") - 1


def coarse_fields(stats, from_north, from_south):
    tiles = from_north.shape[0] - 2
    blocks = stats.shape[0] // 3
    at_north, at_south = edges()
    fields = []
    for which in range(3):
        slot = tiles + which // 2
        at = (which % 2) * HALO_C
        top = sealed(from_north[slot, at : at + HALO_C, :], at_north)
        low = sealed(from_south[slot, at : at + HALO_C, :], at_south)
        mid = stats[which * blocks : (which + 1) * blocks, :]
        fields.append(jnp.concatenate([top, mid, low], axis=0))
    return fields


def coarse_sweeps(ground_c, lock_c, value):
    for _ in range(COARSE):
        across = jnp.minimum(value, jnp.minimum(roll(value, 1, 1), roll(value, -1, 1)))
        around = jnp.minimum(across, jnp.minimum(roll(across, 1, 0), roll(across, -1, 0)))
        lowered = jnp.minimum(value, around + coarse_step)
        value = jnp.minimum(jnp.maximum(ground_c, lowered), lock_c)
    return value


def start_value(floor, lock, lifted):
    return jnp.maximum(floor, jnp.minimum(lifted, lock))


def edge_rolls(tiles):
    return roll(tiles[-1], 1, 1), roll(tiles[0], -1, 1)


def grouped_sweep(count, load, edges_at, load_floor, store, store_edges, unroll):
    def plane_min(t, groups):
        out = []
        for (above, below), tiles in zip(edges_at(t, groups), groups):
            line = [above] + tiles + [below]
            mins = []
            for c in range(0, len(tiles), 2):
                pair = jnp.minimum(line[c + 1], line[c + 2])
                mins.append(jnp.minimum(line[c], pair))
                if c + 1 < len(tiles):
                    mins.append(jnp.minimum(pair, line[c + 3]))
            out.append(mins)
        return out

    def each(function, *args):
        return [[function(*values) for values in zip(*groups)] for groups in zip(*args)]

    def least(*args):
        return each(lambda *values: functools.reduce(jnp.minimum, values), *args)

    def finish(t, around, value):
        new = each(
            lambda f, v, m: jnp.maximum(f, jnp.minimum(v, m + fine_step)),
            load_floor(t),
            value,
            around,
        )
        store(t, new)
        if store_edges is not None:
            store_edges(t, new)

    first, last = load(0), load(count - 1)
    h_first = plane_min(0, first)
    h_before = each(lambda h: roll(h, 1, 0), plane_min(count - 1, last))
    h_after = each(lambda h: roll(h, -1, 0), h_first)

    def line_at(t):
        if isinstance(t, int) and t == count:
            return None, h_after
        value = load(t)
        return value, plane_min(t, value)

    def span(start, size, carry):
        h_west, h_here, here = carry
        u = 0
        while u < size:
            t = start + u
            value, h_east = line_at(t + 1)
            pair = least(h_here, h_east)
            finish(t, least(h_west, pair), here)
            if u + 1 < size:
                far, h_far = line_at(t + 2)
                finish(t + 1, least(pair, h_far), value)
                h_west, h_here, here = h_east, h_far, far
                u += 2
            else:
                h_west, h_here, here = h_here, h_east, value
                u += 1
        return h_west, h_here, here

    loops = (count - 1) // unroll
    carry = (h_before, h_first, first)
    if loops:
        carry = lax.fori_loop(0, loops, lambda q, c: span(q * unroll, unroll, c), carry)
    span(loops * unroll, count - loops * unroll, carry)


def main_kernel(
    floor_t, lock_t, stats_t, natural, va, vb, edge_a, edge_b, coarse, spread, turned
):
    tiles, rows, _ = natural.shape
    planes = floor_t.shape[0]
    blocks = rows // BLK
    margin, chunk = interior(tiles)
    first = plane_row(margin, tiles)
    pitch = chunk + 1
    ground_c = stats_t[...]
    lock_c = roll(ground_c, -blocks, 1)
    value = roll(ground_c, -2 * blocks, 1)
    for _ in range(COARSE):
        across = jnp.minimum(value, jnp.minimum(roll(value, 1, 0), roll(value, -1, 0)))
        around = jnp.minimum(across, jnp.minimum(roll(across, 1, 1), roll(across, -1, 1)))
        lowered = jnp.minimum(value, around + coarse_step)
        value = jnp.minimum(jnp.maximum(ground_c, lowered), lock_c)
    coarse[...] = value
    lane = lane_iota()
    for b in range(chunk // BLK):
        part = coarse[pl.ds(margin // BLK + b, SUB, stride=chunk // BLK), :]
        for c in range(planes):
            spread[c, b] = gather_lanes(part, (planes * lane + c + margin) // BLK)

    def strided(ref):
        return lambda t: [[ref[c, pl.ds(first + t, SUB, stride=pitch), :] for c in range(planes)]]

    load_floor, load_lock = strided(floor_t), strided(lock_t)

    def keep_edges(edges):
        def store_edges(t, groups):
            edges[0, t], edges[1, t] = edge_rolls(groups[0])

        return store_edges

    def keep(dst):
        def store(t, groups):
            for c, value in enumerate(groups[0]):
                dst[c, t] = value

        return store

    def start(b, carry):
        for u in range(BLK):
            t = b * BLK + u
            both = zip(load_floor(t)[0], load_lock(t)[0])
            tiles = [[start_value(f, k, spread[c, b]) for c, (f, k) in enumerate(both)]]
            keep(va)(t, tiles)
            keep_edges(edge_a)(t, tiles)
        return carry

    lax.fori_loop(0, chunk // BLK, start, 0, unroll=True)

    def sweep(src, edges_in, store, store_edges):
        grouped_sweep(
            chunk,
            lambda t: [[src[c, t] for c in range(planes)]],
            lambda t, _: [(edges_in[0, t], edges_in[1, t])],
            load_floor,
            store,
            store_edges,
            UNROLL_T,
        )

    def twice(i, carry):
        sweep(va, edge_a, keep(vb), keep_edges(edge_b))
        sweep(vb, edge_b, keep(va), keep_edges(edge_a))
        return carry

    lax.fori_loop(0, FINE // 2 - 1, twice, 0)
    sweep(va, edge_a, keep(vb), keep_edges(edge_b))

    def store_last(t, groups):
        for c, value in enumerate(groups[0]):
            turned[c, pl.ds(first + t, SUB, stride=pitch), :] = value

    sweep(vb, edge_b, store_last, None)
    cols = tiles * LANES
    for c in range(planes):
        for col in list(range(0, margin, SUB)) + list(range(cols - margin, cols, SUB)):
            at = plane_row(col, tiles)
            turned[c, at : at + SUB, :] = jnp.zeros((SUB, LANES), jnp.float32)

    def finish(j, carry):
        for c in range(planes):
            parts = []
            for v in range(LANES // SUB):
                at = plane_row(j * LANES + v * SUB, tiles)
                parts.append(turned[c, pl.ds(at, SUB), :])
            back = jnp.concatenate(parts, axis=0).T
            for a in range(LANES // SUB):
                natural[j, pl.ds(margin + a * SUB * planes + c, SUB, stride=planes), :] = back[
                    a * SUB : (a + 1) * SUB
                ]
        return carry

    lax.fori_loop(0, tiles, finish, 0, unroll=True)


def main_part(floor_t, lock_t, stats_t, rows):
    planes, length, _ = floor_t.shape
    tiles = stats_t.shape[0] * BLK // LANES
    chunk = interior(tiles)[1]
    vmem = pl.BlockSpec(memory_space=pltpu.VMEM)
    tall = (planes, chunk, SUB, LANES)
    f32 = jnp.float32
    return pl.pallas_call(
        main_kernel,
        in_specs=[vmem] * 3,
        out_specs=vmem,
        out_shape=jax.ShapeDtypeStruct((tiles, rows, LANES), f32),
        scratch_shapes=[
            pltpu.VMEM(tall, f32),
            pltpu.VMEM(tall, f32),
            pltpu.VMEM((2, chunk, SUB, LANES), f32),
            pltpu.VMEM((2, chunk, SUB, LANES), f32),
            pltpu.VMEM(stats_t.shape, f32),
            pltpu.VMEM((planes, chunk // BLK, SUB, LANES), f32),
            pltpu.VMEM((planes, length, LANES), f32),
        ],
        compiler_params=pltpu.CompilerParams(vmem_limit_bytes=16 * MIB),
        cost_estimate=pl.CostEstimate(flops=100_000_000, bytes_accessed=20_000_000, transcendentals=0),
        name="middle",
    )(floor_t, lock_t, stats_t)


def split_pair(first, second, even_lane):
    even = jnp.where(even_lane, first, roll(second, 1, 1))
    odd = jnp.where(even_lane, roll(first, -1, 1), second)
    return even, odd


def join_pair(even, odd, even_lane):
    first = jnp.where(even_lane, even, roll(odd, 1, 1))
    second = jnp.where(even_lane, roll(even, -1, 1), odd)
    return first, second


def bands_kernel(
    floor_in, lock, stats, from_north, from_south, out, va_n, va_s, vb_n, vb_s, floor_n, floor_s, lifted
):
    tiles, rows, _ = floor_in.shape
    blocks = rows // BLK
    va, vb, floor = (va_n, va_s), (vb_n, vb_s), (floor_n, floor_s)
    height = va_n.shape[1]
    inner = height - FINE
    pairs = tiles // 2
    at_north, at_south = edges()
    lane = lane_iota()
    even_lane = lane % 2 == 0
    coarse = coarse_sweeps(*coarse_fields(stats, from_north, from_south))
    wide = lane_iota(coarse.shape)
    for j in range(tiles):
        lifted[j] = gather_lanes(coarse, wide // BLK + 8 * j)
    for side, (band, is_edge, at_band, at_inner, first) in enumerate(
        ((from_north, at_north, 0, FINE, 0), (from_south, at_south, inner, 0, rows - inner))
    ):

        def put(at, c_row, fields):
            both = []
            for j in range(2):
                low, k, tile = fields[j]
                both.append((start_value(low, k, lifted[tile, c_row : c_row + 1, :]), low))
            q = fields[0][2]
            for dst, pair in zip((va, floor), zip(*both)):
                for n, value in enumerate(split_pair(*pair, even_lane)):
                    dst[side][q + n, at : at + SUB, :] = value

        for q in range(pairs):
            pair = (2 * q, 2 * q + 1)
            put(
                at_band,
                HALO_C - 1 if side == 0 else HALO_C + blocks,
                [
                    (sealed(band[j, 0:FINE, :], is_edge), sealed(band[j, FINE:, :], is_edge), j)
                    for j in pair
                ],
            )
            for i in range(inner // SUB):
                at = slice(first + i * SUB, first + (i + 1) * SUB)
                c_row = HALO_C + (first + i * SUB) // BLK
                put(at_inner + i * SUB, c_row, [(floor_in[j, at, :], lock[j, at, :], j) for j in pair])

    count = height // SUB
    before = jnp.where(lane < 2, LANES - 1 - lane, lane - 2)
    after = jnp.where(lane < LANES - 2, lane + 2, LANES - 1 - lane)

    def strided(ref):
        return lambda t: [
            [ref[2 * q + n, pl.ds(t, SUB, stride=count), :] for n in range(2)]
            for q in range(pairs)
        ]

    def pair_edges(t, groups):
        above = [gather_lanes(odd, before) for _, odd in groups]
        below = [gather_lanes(even, after) for even, _ in groups]
        return [
            (
                jnp.where(lane == 0, above[q - 1], above[q]),
                jnp.where(lane == LANES - 1, below[(q + 1) % pairs], below[q]),
            )
            for q in range(pairs)
        ]

    def keep(dst):
        def store(t, groups):
            for q, pair in enumerate(groups):
                for n, value in enumerate(pair):
                    dst[2 * q + n, pl.ds(t, SUB, stride=count), :] = value

        return store

    def twice(i, carry):
        for src, dst in ((va, vb), (vb, va)):
            for side in range(2):
                grouped_sweep(
                    count,
                    strided(src[side]),
                    pair_edges,
                    strided(floor[side]),
                    keep(dst[side]),
                    None,
                    count,
                )
        return carry

    lax.fori_loop(0, FINE // 2, twice, 0, unroll=True)
    for side in range(2):
        for i in range(out.shape[2] // SUB):
            at = slice(FINE + i * SUB, FINE + (i + 1) * SUB)
            for q in range(pairs):
                pair = join_pair(va[side][2 * q, at, :], va[side][2 * q + 1, at, :], even_lane)
                for n, value in enumerate(pair):
                    out[side, 2 * q + n, i * SUB : (i + 1) * SUB, :] = value


def bands(floor, lock, stats, from_north, from_south):
    tiles, rows, _ = floor.shape
    blocks = rows // BLK
    vmem = pl.BlockSpec(memory_space=pltpu.VMEM)
    height = COARSE * BLK + 3 * FINE
    tall = (tiles, height, LANES)
    f32 = jnp.float32
    return pl.pallas_call(
        bands_kernel,
        in_specs=[vmem] * 5,
        out_specs=vmem,
        out_shape=jax.ShapeDtypeStruct((2, tiles, height - 2 * FINE, LANES), f32),
        scratch_shapes=[
            *[pltpu.VMEM(tall, f32)] * 6,
            pltpu.VMEM((tiles, blocks + 2 * HALO_C, LANES), f32),
        ],
        compiler_params=pltpu.CompilerParams(vmem_limit_bytes=16 * MIB),
        cost_estimate=pl.CostEstimate(flops=60_000_000, bytes_accessed=12_000_000, transcendentals=0),
        name="bands",
    )(floor, lock, stats, from_north, from_south)


def strip_planes(rows):
    return -(-(rows + 2 * FINE) // LANES)


def pack_kernel(
    floor, lock, stats, from_north, from_south, west, east, turned, tall
):
    tiles, rows, _ = floor.shape
    blocks = rows // BLK
    planes = turned.shape[2]
    at_north, at_south = edges()
    group = lane_iota() // 8
    fields = coarse_fields(stats, from_north, from_south)
    coarse = fields[0].shape[0] // SUB
    coarse_cols = tiles * LANES // BLK
    rest = tall.shape[2] - rows - 2 * FINE
    for side, (dst, j, col_at, lane_at) in enumerate(
        ((west, 0, 0, 0), (east, tiles - 1, LANES - FINE, coarse_cols - 8))
    ):
        for which, ref in enumerate((floor, lock)):
            at = slice(which * FINE, (which + 1) * FINE)
            tall[side, which, 0:FINE, :] = sealed(from_north[j, at, :], at_north)
            tall[side, which, FINE : FINE + rows, :] = ref[j]
            tall[side, which, FINE + rows : 2 * FINE + rows, :] = sealed(from_south[j, at, :], at_south)
            tall[side, which, 2 * FINE + rows :, :] = jnp.full((rest, LANES), huge_level, jnp.float32)
            for c in range(planes):
                parts = [
                    tall[side, which, pl.ds(a * SUB * planes + c, SUB, stride=planes), :]
                    for a in range(LANES // SUB)
                ]
                value = jnp.concatenate(parts, axis=0).T
                turned[side, which, c] = value
                slot = which * planes + c
                dst[slot * SUB : (slot + 1) * SUB, :] = value[col_at : col_at + FINE]
        sources = [field[i * SUB : (i + 1) * SUB] for field in fields for i in range(coarse)]
        for n in range(0, len(sources), 16):
            packed = jnp.zeros((SUB, LANES), jnp.float32)
            for m, value in enumerate(sources[n : n + 16]):
                packed = jnp.where(group == m, roll(value, 8 * m - lane_at, 1), packed)
            slot = 2 * planes + n // 16
            dst[slot * SUB : (slot + 1) * SUB, :] = packed


def pack_columns(floor, lock, stats, from_north, from_south):
    tiles, rows, _ = floor.shape
    blocks = rows // BLK
    planes = strip_planes(rows)
    slots = 2 * planes + -(-3 * (blocks + 2 * HALO_C) // SUB // 16)
    vmem = pl.BlockSpec(memory_space=pltpu.VMEM)
    f32 = jnp.float32
    out = jax.ShapeDtypeStruct((slots * SUB, LANES), f32)
    turned = jax.ShapeDtypeStruct((2, 2, planes, LANES, LANES), f32)
    return pl.pallas_call(
        pack_kernel,
        in_specs=[vmem] * 5,
        out_specs=[vmem] * 3,
        out_shape=[out, out, turned],
        scratch_shapes=[pltpu.VMEM((2, 2, planes * LANES, LANES), f32)],
        compiler_params=pltpu.CompilerParams(vmem_limit_bytes=12 * MIB),
        name="pack",
    )(floor, lock, stats, from_north, from_south)


def strip_kernel(
    stats, from_north, from_south, turned, from_west, from_east, natural, banded,
    out, va_w, va_e, vb_w, vb_e, floor_w, floor_e, lifted, tall, edge, sems, edge_sems,
):
    tiles, rows, _ = natural.shape
    planes = turned.shape[2]
    coarse_cols = tiles * LANES // BLK
    lane = lane_iota()
    va, vb, floor = (va_w, va_e), (vb_w, vb_e), (floor_w, floor_e)
    width = va_w.shape[1]
    inner = width - FINE
    valid = inner - FINE
    spans = (
        (pl.ds(0, valid), lambda j: banded.at[0, j]),
        (pl.ds(valid, rows - 2 * valid), lambda j: natural.at[j, pl.ds(valid, rows - 2 * valid), :]),
        (pl.ds(rows - valid, valid), lambda j: banded.at[1, j]),
    )
    copies = [
        pltpu.make_async_copy(part(j), out.at[span, pl.ds(j * LANES, LANES)], sems.at[n, j])
        for j in range(1, tiles - 1)
        for n, (span, part) in enumerate(spans)
    ]
    for copy in copies:
        copy.start()

    def piece(ref, n, to):
        slot = 2 * planes + n // 16
        return roll(ref[slot * SUB : (slot + 1) * SUB, :], to - 8 * (n % 16), 1)

    fields = []
    for which, field in enumerate(coarse_fields(stats, from_north, from_south)):
        parts = []
        count = field.shape[0] // SUB
        for i in range(count):
            n = which * count + i
            here = field[i * SUB : (i + 1) * SUB]
            here = jnp.where(lane // 8 == coarse_cols // 8, piece(from_east, n, coarse_cols), here)
            here = jnp.where(lane // 8 == 15, piece(from_west, n, LANES - 8), here)
            parts.append(here)
        fields.append(jnp.concatenate(parts, axis=0))
    value = coarse_sweeps(*fields)
    value = jnp.concatenate([value, jnp.zeros((LANES - value.shape[0], LANES), jnp.float32)], axis=0).T
    for c in range(planes):
        index = (planes * lane + (c + HALO_C * BLK - FINE)) // BLK
        for side, groups in enumerate(((LANES - 8, 0), (coarse_cols - 8, coarse_cols))):
            for n, at in enumerate(groups):
                lifted[side, c, n * SUB : (n + 1) * SUB, :] = gather_lanes(value[at : at + SUB], index)

    for side, ref in enumerate((from_west, from_east)):
        for c in range(planes):
            for i in range(width // SUB):
                if (side, i) in ((0, 0), (1, width // SUB - 1)):
                    low, k = (ref[(w * planes + c) * SUB : (w * planes + c + 1) * SUB, :] for w in range(2))
                else:
                    col = (i - 1) * SUB if side == 0 else LANES - inner + i * SUB
                    low, k = (turned[side, w, c, col : col + SUB, :] for w in range(2))
                c_row = (i + 15) // 2 if side == 0 else 8 - COARSE - 1 + i // 2
                at = slice(i * SUB, (i + 1) * SUB)
                floor[side][c, at, :] = low
                va[side][c, at, :] = start_value(low, k, lifted[side, c, c_row : c_row + 1, :])

    count = width // SUB

    def strided(ref):
        return lambda t: [[ref[c, pl.ds(t, SUB, stride=count), :] for c in range(planes)]]

    def keep(dst):
        def store(t, groups):
            for c, value in enumerate(groups[0]):
                dst[c, pl.ds(t, SUB, stride=count), :] = value

        return store

    def twice(i, carry):
        for src, dst in ((va, vb), (vb, va)):
            for side in range(2):
                grouped_sweep(
                    count,
                    strided(src[side]),
                    lambda t, groups: [edge_rolls(groups[0])],
                    strided(floor[side]),
                    keep(dst[side]),
                    None,
                    count,
                )
        return carry

    lax.fori_loop(0, FINE // 2, twice, 0)

    stores = []
    for side, j in enumerate((0, tiles - 1)):
        fill = jnp.zeros((LANES - inner, LANES), jnp.float32)
        for c in range(planes):
            parts = [va[side][c, FINE:, :], fill] if side == 0 else [fill, va[side][c, 0:inner, :]]
            back = jnp.concatenate(parts, axis=0).T
            for a in range(LANES // SUB):
                tall[side, pl.ds(a * SUB * planes + c, SUB, stride=planes), :] = back[a * SUB : (a + 1) * SUB]
        mine = (lane < valid) if side == 0 else (lane >= LANES - valid)
        for i in range(rows // SUB):
            at = i * SUB
            if at < valid:
                other = banded[0, j, at : at + SUB, :]
            elif at >= rows - valid:
                at_band = at - (rows - valid)
                other = banded[1, j, at_band : at_band + SUB, :]
            else:
                other = natural[j, at : at + SUB, :]
            edge[side, at : at + SUB, :] = jnp.where(mine, tall[side, FINE + at : FINE + at + SUB, :], other)
        stores.append(
            pltpu.make_async_copy(edge.at[side], out.at[:, pl.ds(j * LANES, LANES)], edge_sems.at[side])
        )
        stores[-1].start()
    for copy in copies + stores:
        copy.wait()


def strips(stats, from_north, from_south, turned, from_west, from_east, natural, banded):
    tiles, rows, _ = natural.shape
    planes = turned.shape[2]
    vmem = pl.BlockSpec(memory_space=pltpu.VMEM)
    wide = (planes, COARSE * BLK + 3 * FINE, LANES)
    f32 = jnp.float32
    return pl.pallas_call(
        strip_kernel,
        in_specs=[vmem] * 8,
        out_specs=pl.BlockSpec(memory_space=pltpu.HBM),
        out_shape=jax.ShapeDtypeStruct((rows, tiles * LANES), f32),
        scratch_shapes=[
            *[pltpu.VMEM(wide, f32)] * 6,
            pltpu.VMEM((2, planes, 2 * SUB, LANES), f32),
            pltpu.VMEM((2, planes * LANES, LANES), f32),
            pltpu.VMEM((2, rows, LANES), f32),
            pltpu.SemaphoreType.DMA((3, tiles)),
            pltpu.SemaphoreType.DMA((2,)),
        ],
        compiler_params=pltpu.CompilerParams(vmem_limit_bytes=12 * MIB),
        name="strips",
    )(stats, from_north, from_south, turned, from_west, from_east, natural, banded)


def ring(value, axis, shift):
    count = lax.axis_size(axis)
    return lax.ppermute(value, axis, [(i, (i + shift) % count) for i in range(count)])


def shards(elevation, ocean, outlet):
    floor, lock, floor_t, lock_t, stats, stats_t, north, south = prepare(elevation, ocean, outlet)
    from_south = ring(north, "row", -1)
    from_north = ring(south, "row", 1)
    natural = main_part(floor_t, lock_t, stats_t, elevation.shape[0])
    from_north, from_south, natural = lax.optimization_barrier((from_north, from_south, natural))
    halo_args = (stats, from_north, from_south)
    west, east, turned = pack_columns(floor, lock, *halo_args)
    from_east = ring(west, "col", -1)
    from_west = ring(east, "col", 1)
    banded = bands(floor, lock, *halo_args)
    return strips(*halo_args, turned, from_west, from_east, natural, banded)


def solution(mesh):
    return jax.shard_map(
        shards,
        mesh=mesh,
        in_specs=(P("row", "col"), P("row", "col"), P("row", "col")),
        out_specs=P("row", "col"),
        check_vma=False,
    )
```

```python
import functools

import jax
import jax.numpy as jnp
from jax import lax
from jax.experimental import pallas as pl
from jax.experimental.pallas import tpu as pltpu
from jax.sharding import PartitionSpec as P

BLK = 16
COARSE = 4
FINE = 8
LANES = 128
SUB = 8
HALO_C = 8
UNROLL_T = 112
PITCH = SUB + 1

huge_level = 1e30
fine_step = 2.0 ** (-10)
coarse_step = 2.0 ** (-6)
MIB = 2**20


def roll(x, shift, axis):
    return pltpu.roll(x, shift % x.shape[axis], axis)


def lane_iota(shape=(SUB, LANES)):
    return lax.broadcasted_iota(jnp.int32, shape, 1)


def gather_lanes(x, index):
    return jnp.take_along_axis(x, index, axis=1, mode="promise_in_bounds")


def interior(tiles):
    margin = COARSE * BLK
    chunk = (tiles * LANES - 2 * margin) // SUB
    return margin, chunk


def interior_planes(rows):
    return (rows - 2 * COARSE * BLK) // LANES


def plane_row(col, tiles):
    margin, chunk = interior(tiles)
    return col + (col + chunk - margin) // chunk


def plane_rows(tiles):
    return -(-(plane_row(tiles * LANES, tiles) + 1) // SUB) * SUB


def prepare_kernel(
    elev, ocean, outlet, floor, lock, floor_t, lock_t, stats, stats_t, north, south,
    elev_buf, ocean_buf, outlet_buf, paired, turn, sems,
):
    tiles, rows, _ = floor.shape
    planes = floor_t.shape[0]
    margin = interior(tiles)[0]
    blocks = rows // BLK
    lane = lane_iota()
    sub = lax.broadcasted_iota(jnp.int32, (SUB, LANES), 0)
    unused = jnp.zeros((LANES - 3 * blocks, LANES), jnp.float32)

    def copies(j):
        cols = pl.ds(pl.multiple_of(j * LANES, LANES), LANES)
        return [
            pltpu.make_async_copy(src.at[:, cols], dst.at[j], sems.at[n, j])
            for n, (src, dst) in enumerate(
                ((elev, elev_buf), (ocean, ocean_buf), (outlet, outlet_buf))
            )
        ]

    for j in range(tiles):
        for copy in copies(j):
            copy.start()
    turn[...] = jnp.zeros(turn.shape, jnp.float32)
    for band in (north, south):
        band[tiles:, :, :] = jnp.zeros((2, 2 * FINE, LANES), jnp.float32)

    def tile(j, carry):
        for copy in copies(j):
            copy.wait()
        is_ocean = ocean_buf[j] == 1
        g = jnp.where(is_ocean, jnp.float32(0.0), elev_buf[j])
        k = jnp.where(is_ocean | (outlet_buf[j] == 1), g, jnp.float32(huge_level))
        low = jnp.minimum(g, k)
        elev_buf[j] = g
        floor[j] = low
        lock[j] = k
        north[j, 0:FINE, :] = low[0:FINE]
        north[j, FINE:, :] = k[0:FINE]
        south[j, 0:FINE, :] = low[rows - FINE :]
        south[j, FINE:, :] = k[rows - FINE :]
        for b in range(blocks):
            at = slice(b * BLK, b * BLK + SUB)
            also = slice(b * BLK + SUB, (b + 1) * BLK)
            to = slice(b * PITCH, b * PITCH + SUB)
            paired[0, to, :] = jnp.minimum(g[at], g[also])
            paired[1, to, :] = jnp.minimum(k[at], k[also])
            paired[2, to, :] = -jnp.maximum(g[at], g[also])
        for c in range(planes):
            turned = [
                jnp.concatenate(
                    [
                        ref[j, pl.ds(margin + a * SUB * planes + c, SUB, stride=planes), :]
                        for a in range(LANES // SUB)
                    ],
                    axis=0,
                ).T
                for ref in (elev_buf, lock)
            ]
            for v in range(LANES // SUB):
                g, k = (x[v * SUB : (v + 1) * SUB] for x in turned)
                at = plane_row(j * LANES + v * SUB, tiles)
                floor_t[c, pl.ds(at, SUB), :] = jnp.minimum(g, k)
                lock_t[c, pl.ds(at, SUB), :] = k
        found = [[], [], []]
        for q in range(blocks // SUB):
            for which in range(3):
                for r in range(SUB):
                    value = paired[which, pl.ds(q * SUB * PITCH + r, SUB, stride=PITCH), :]
                    low = value if r == 0 else jnp.minimum(low, value)
                found[which].append(low)
        turned = jnp.concatenate(found[0] + found[1] + found[2] + [unused], axis=0).T
        total = None
        for b in range(LANES // BLK):
            value = jnp.minimum(
                turned[b * BLK : b * BLK + SUB], turned[b * BLK + SUB : (b + 1) * BLK]
            )
            for shift in (4, 2, 1):
                value = jnp.minimum(value, roll(value, shift, 0))
            total = value if b == 0 else jnp.where(sub == b, value, total)
        total = jnp.where(lane // blocks == 2, -total, total)
        at = pl.ds(pl.multiple_of(j * SUB, SUB), SUB)
        stats_t[at, :] = total
        turn[at, :] = total
        return carry

    lax.fori_loop(0, tiles, tile, 0)
    stats[...] = turn[...].T[: 3 * blocks]
    for which in range(3):
        slot = tiles + which // 2
        at = (which % 2) * HALO_C
        first = which * blocks
        north[slot, at : at + HALO_C, :] = stats[first : first + HALO_C, :]
        south[slot, at : at + HALO_C, :] = stats[first + blocks - HALO_C : first + blocks, :]


def prepare(elevation, ocean, outlet):
    rows, cols = elevation.shape
    tiles = cols // LANES
    f32 = jnp.float32
    hbm = pl.BlockSpec(memory_space=pltpu.HBM)
    vmem = pl.BlockSpec(memory_space=pltpu.VMEM)
    natural = (tiles, rows, LANES)
    turned = (interior_planes(rows), plane_rows(tiles), LANES)
    band = (tiles + 2, 2 * FINE, LANES)
    shapes = [natural, natural, turned, turned, (3 * rows // BLK, LANES), (cols // BLK, LANES), band, band]
    return pl.pallas_call(
        prepare_kernel,
        in_specs=[hbm] * 3,
        out_specs=[vmem] * len(shapes),
        out_shape=[jax.ShapeDtypeStruct(shape, f32) for shape in shapes],
        scratch_shapes=[
            pltpu.VMEM(natural, f32),
            pltpu.VMEM(natural, jnp.int32),
            pltpu.VMEM(natural, jnp.int32),
            pltpu.VMEM((3, rows // BLK * PITCH, LANES), f32),
            pltpu.VMEM((LANES, LANES), f32),
            pltpu.SemaphoreType.DMA((3, tiles)),
        ],
        compiler_params=pltpu.CompilerParams(vmem_limit_bytes=24 * MIB),
        name="prepare",
    )(*(pltpu.with_memory_space_constraint(x, pltpu.HBM) for x in (elevation, ocean, outlet)))


def sealed(value, is_edge):
    return jnp.where(is_edge, jnp.float32(huge_level), value)


def edges():
    pos = lax.axis_index("row")
    return pos == 0, pos == lax.axis_size("row") - 1


def coarse_fields(stats, from_north, from_south):
    tiles = from_north.shape[0] - 2
    blocks = stats.shape[0] // 3
    at_north, at_south = edges()
    fields = []
    for which in range(3):
        slot = tiles + which // 2
        at = (which % 2) * HALO_C
        top = sealed(from_north[slot, at : at + HALO_C, :], at_north)
        low = sealed(from_south[slot, at : at + HALO_C, :], at_south)
        mid = stats[which * blocks : (which + 1) * blocks, :]
        fields.append(jnp.concatenate([top, mid, low], axis=0))
    return fields


def coarse_sweeps(ground_c, lock_c, value):
    for _ in range(COARSE):
        across = jnp.minimum(value, jnp.minimum(roll(value, 1, 1), roll(value, -1, 1)))
        around = jnp.minimum(across, jnp.minimum(roll(across, 1, 0), roll(across, -1, 0)))
        lowered = jnp.minimum(value, around + coarse_step)
        value = jnp.minimum(jnp.maximum(ground_c, lowered), lock_c)
    return value


def start_value(floor, lock, lifted):
    return jnp.maximum(floor, jnp.minimum(lifted, lock))


def edge_rolls(tiles):
    return roll(tiles[-1], 1, 1), roll(tiles[0], -1, 1)


def grouped_sweep(count, load, edges_at, load_floor, store, unroll):
    def plane_min(t, groups):
        out = []
        for (above, below), tiles in zip(edges_at(t, groups), groups):
            line = [above] + tiles + [below]
            mins = []
            for c in range(0, len(tiles), 2):
                pair = jnp.minimum(line[c + 1], line[c + 2])
                mins.append(jnp.minimum(line[c], pair))
                if c + 1 < len(tiles):
                    mins.append(jnp.minimum(pair, line[c + 3]))
            out.append(mins)
        return out

    def each(function, *args):
        return [[function(*values) for values in zip(*groups)] for groups in zip(*args)]

    def least(*args):
        return each(lambda *values: functools.reduce(jnp.minimum, values), *args)

    def finish(t, around, value):
        new = each(
            lambda f, v, m: jnp.maximum(f, jnp.minimum(v, m + fine_step)),
            load_floor(t),
            value,
            around,
        )
        store(t, new)

    first, last = load(0), load(count - 1)
    h_first = plane_min(0, first)
    h_before = each(lambda h: roll(h, 1, 0), plane_min(count - 1, last))
    h_after = each(lambda h: roll(h, -1, 0), h_first)

    def line_at(t):
        if isinstance(t, int) and t == count:
            return None, h_after
        value = load(t)
        return value, plane_min(t, value)

    def span(start, size, carry):
        h_west, h_here, here = carry
        u = 0
        while u < size:
            t = start + u
            value, h_east = line_at(t + 1)
            pair = least(h_here, h_east)
            finish(t, least(h_west, pair), here)
            if u + 1 < size:
                far, h_far = line_at(t + 2)
                finish(t + 1, least(pair, h_far), value)
                h_west, h_here, here = h_east, h_far, far
                u += 2
            else:
                h_west, h_here, here = h_here, h_east, value
                u += 1
        return h_west, h_here, here

    loops = (count - 1) // unroll
    carry = (h_before, h_first, first)
    if loops:
        carry = lax.fori_loop(0, loops, lambda q, c: span(q * unroll, unroll, c), carry)
    span(loops * unroll, count - loops * unroll, carry)


def main_kernel(
    floor_t, lock_t, stats_t, natural, va, vb, coarse, spread, turned
):
    tiles, rows, _ = natural.shape
    planes = floor_t.shape[0]
    blocks = rows // BLK
    margin, chunk = interior(tiles)
    first = plane_row(margin, tiles)
    pitch = chunk + 1
    ground_c = stats_t[...]
    lock_c = roll(ground_c, -blocks, 1)
    value = roll(ground_c, -2 * blocks, 1)
    for _ in range(COARSE):
        across = jnp.minimum(value, jnp.minimum(roll(value, 1, 0), roll(value, -1, 0)))
        around = jnp.minimum(across, jnp.minimum(roll(across, 1, 1), roll(across, -1, 1)))
        lowered = jnp.minimum(value, around + coarse_step)
        value = jnp.minimum(jnp.maximum(ground_c, lowered), lock_c)
    coarse[...] = value
    lane = lane_iota()
    for b in range(chunk // BLK):
        part = coarse[pl.ds(margin // BLK + b, SUB, stride=chunk // BLK), :]
        for c in range(planes):
            spread[c, b] = gather_lanes(part, (planes * lane + c + margin) // BLK)

    def strided(ref):
        return lambda t: [[ref[c, pl.ds(first + t, SUB, stride=pitch), :] for c in range(planes)]]

    load_floor, load_lock = strided(floor_t), strided(lock_t)

    def keep(dst):
        def store(t, groups):
            for c, value in enumerate(groups[0]):
                dst[c, t] = value

        return store

    def start(b, carry):
        for u in range(BLK):
            t = b * BLK + u
            both = zip(load_floor(t)[0], load_lock(t)[0])
            tiles = [[start_value(f, k, spread[c, b]) for c, (f, k) in enumerate(both)]]
            keep(va)(t, tiles)
        return carry

    lax.fori_loop(0, chunk // BLK, start, 0, unroll=True)

    def sweep(src, store):
        grouped_sweep(
            chunk,
            lambda t: [[src[c, t] for c in range(planes)]],
            lambda t, groups: [edge_rolls(groups[0])],
            load_floor,
            store,
            UNROLL_T,
        )

    def twice(i, carry):
        sweep(va, keep(vb))
        sweep(vb, keep(va))
        return carry

    lax.fori_loop(0, FINE // 2 - 1, twice, 0)
    sweep(va, keep(vb))

    def store_last(t, groups):
        for c, value in enumerate(groups[0]):
            turned[c, pl.ds(first + t, SUB, stride=pitch), :] = value

    sweep(vb, store_last)
    cols = tiles * LANES
    for c in range(planes):
        for col in list(range(0, margin, SUB)) + list(range(cols - margin, cols, SUB)):
            at = plane_row(col, tiles)
            turned[c, at : at + SUB, :] = jnp.zeros((SUB, LANES), jnp.float32)

    def finish(j, carry):
        for c in range(planes):
            parts = []
            for v in range(LANES // SUB):
                at = plane_row(j * LANES + v * SUB, tiles)
                parts.append(turned[c, pl.ds(at, SUB), :])
            back = jnp.concatenate(parts, axis=0).T
            for a in range(LANES // SUB):
                natural[j, pl.ds(margin + a * SUB * planes + c, SUB, stride=planes), :] = back[
                    a * SUB : (a + 1) * SUB
                ]
        return carry

    lax.fori_loop(0, tiles, finish, 0, unroll=True)


def main_part(floor_t, lock_t, stats_t, rows):
    planes, length, _ = floor_t.shape
    tiles = stats_t.shape[0] * BLK // LANES
    chunk = interior(tiles)[1]
    vmem = pl.BlockSpec(memory_space=pltpu.VMEM)
    tall = (planes, chunk, SUB, LANES)
    f32 = jnp.float32
    return pl.pallas_call(
        main_kernel,
        in_specs=[vmem] * 3,
        out_specs=vmem,
        out_shape=jax.ShapeDtypeStruct((tiles, rows, LANES), f32),
        scratch_shapes=[
            pltpu.VMEM(tall, f32),
            pltpu.VMEM(tall, f32),
            pltpu.VMEM(stats_t.shape, f32),
            pltpu.VMEM((planes, chunk // BLK, SUB, LANES), f32),
            pltpu.VMEM((planes, length, LANES), f32),
        ],
        compiler_params=pltpu.CompilerParams(vmem_limit_bytes=16 * MIB),
        cost_estimate=pl.CostEstimate(flops=100_000_000, bytes_accessed=20_000_000, transcendentals=0),
        name="middle",
    )(floor_t, lock_t, stats_t)


def split_pair(first, second, even_lane):
    even = jnp.where(even_lane, first, roll(second, 1, 1))
    odd = jnp.where(even_lane, roll(first, -1, 1), second)
    return even, odd


def join_pair(even, odd, even_lane):
    first = jnp.where(even_lane, even, roll(odd, 1, 1))
    second = jnp.where(even_lane, roll(even, -1, 1), odd)
    return first, second


def bands_kernel(
    floor_in, lock, stats, from_north, from_south, out, va_n, va_s, vb_n, vb_s, floor_n, floor_s, lifted
):
    tiles, rows, _ = floor_in.shape
    blocks = rows // BLK
    va, vb, floor = (va_n, va_s), (vb_n, vb_s), (floor_n, floor_s)
    height = va_n.shape[1]
    inner = height - FINE
    pairs = tiles // 2
    at_north, at_south = edges()
    lane = lane_iota()
    even_lane = lane % 2 == 0
    coarse = coarse_sweeps(*coarse_fields(stats, from_north, from_south))
    wide = lane_iota(coarse.shape)
    for j in range(tiles):
        lifted[j] = gather_lanes(coarse, wide // BLK + 8 * j)
    for side, (band, is_edge, at_band, at_inner, first) in enumerate(
        ((from_north, at_north, 0, FINE, 0), (from_south, at_south, inner, 0, rows - inner))
    ):

        def put(at, c_row, fields):
            both = []
            for j in range(2):
                low, k, tile = fields[j]
                both.append((start_value(low, k, lifted[tile, c_row : c_row + 1, :]), low))
            q = fields[0][2]
            for dst, pair in zip((va, floor), zip(*both)):
                for n, value in enumerate(split_pair(*pair, even_lane)):
                    dst[side][q + n, at : at + SUB, :] = value

        for q in range(pairs):
            pair = (2 * q, 2 * q + 1)
            put(
                at_band,
                HALO_C - 1 if side == 0 else HALO_C + blocks,
                [
                    (sealed(band[j, 0:FINE, :], is_edge), sealed(band[j, FINE:, :], is_edge), j)
                    for j in pair
                ],
            )
            for i in range(inner // SUB):
                at = slice(first + i * SUB, first + (i + 1) * SUB)
                c_row = HALO_C + (first + i * SUB) // BLK
                put(at_inner + i * SUB, c_row, [(floor_in[j, at, :], lock[j, at, :], j) for j in pair])

    count = height // SUB
    before = jnp.where(lane < 2, LANES - 1 - lane, lane - 2)
    after = jnp.where(lane < LANES - 2, lane + 2, LANES - 1 - lane)

    def strided(ref):
        return lambda t: [
            [ref[2 * q + n, pl.ds(t, SUB, stride=count), :] for n in range(2)]
            for q in range(pairs)
        ]

    def pair_edges(t, groups):
        above = [gather_lanes(odd, before) for _, odd in groups]
        below = [gather_lanes(even, after) for even, _ in groups]
        return [
            (
                jnp.where(lane == 0, above[q - 1], above[q]),
                jnp.where(lane == LANES - 1, below[(q + 1) % pairs], below[q]),
            )
            for q in range(pairs)
        ]

    def keep(dst):
        def store(t, groups):
            for q, pair in enumerate(groups):
                for n, value in enumerate(pair):
                    dst[2 * q + n, pl.ds(t, SUB, stride=count), :] = value

        return store

    def twice(i, carry):
        for src, dst in ((va, vb), (vb, va)):
            for side in range(2):
                grouped_sweep(
                    count,
                    strided(src[side]),
                    pair_edges,
                    strided(floor[side]),
                    keep(dst[side]),
                    count,
                )
        return carry

    lax.fori_loop(0, FINE // 2, twice, 0, unroll=True)
    for side in range(2):
        for i in range(out.shape[2] // SUB):
            at = slice(FINE + i * SUB, FINE + (i + 1) * SUB)
            for q in range(pairs):
                pair = join_pair(va[side][2 * q, at, :], va[side][2 * q + 1, at, :], even_lane)
                for n, value in enumerate(pair):
                    out[side, 2 * q + n, i * SUB : (i + 1) * SUB, :] = value


def bands(floor, lock, stats, from_north, from_south):
    tiles, rows, _ = floor.shape
    blocks = rows // BLK
    vmem = pl.BlockSpec(memory_space=pltpu.VMEM)
    height = COARSE * BLK + 3 * FINE
    tall = (tiles, height, LANES)
    f32 = jnp.float32
    return pl.pallas_call(
        bands_kernel,
        in_specs=[vmem] * 5,
        out_specs=vmem,
        out_shape=jax.ShapeDtypeStruct((2, tiles, height - 2 * FINE, LANES), f32),
        scratch_shapes=[
            *[pltpu.VMEM(tall, f32)] * 6,
            pltpu.VMEM((tiles, blocks + 2 * HALO_C, LANES), f32),
        ],
        compiler_params=pltpu.CompilerParams(vmem_limit_bytes=16 * MIB),
        cost_estimate=pl.CostEstimate(flops=60_000_000, bytes_accessed=12_000_000, transcendentals=0),
        name="bands",
    )(floor, lock, stats, from_north, from_south)


def strip_planes(rows):
    return -(-(rows + 2 * FINE) // LANES)


def pack_kernel(
    floor, lock, stats, from_north, from_south, west, east, turned, tall
):
    tiles, rows, _ = floor.shape
    blocks = rows // BLK
    planes = turned.shape[2]
    at_north, at_south = edges()
    group = lane_iota() // 8
    fields = coarse_fields(stats, from_north, from_south)
    coarse = fields[0].shape[0] // SUB
    coarse_cols = tiles * LANES // BLK
    rest = tall.shape[2] - rows - 2 * FINE
    for side, (dst, j, col_at, lane_at) in enumerate(
        ((west, 0, 0, 0), (east, tiles - 1, LANES - FINE, coarse_cols - 8))
    ):
        for which, ref in enumerate((floor, lock)):
            at = slice(which * FINE, (which + 1) * FINE)
            tall[side, which, 0:FINE, :] = sealed(from_north[j, at, :], at_north)
            tall[side, which, FINE : FINE + rows, :] = ref[j]
            tall[side, which, FINE + rows : 2 * FINE + rows, :] = sealed(from_south[j, at, :], at_south)
            tall[side, which, 2 * FINE + rows :, :] = jnp.full((rest, LANES), huge_level, jnp.float32)
            for c in range(planes):
                parts = [
                    tall[side, which, pl.ds(a * SUB * planes + c, SUB, stride=planes), :]
                    for a in range(LANES // SUB)
                ]
                value = jnp.concatenate(parts, axis=0).T
                turned[side, which, c] = value
                slot = which * planes + c
                dst[slot * SUB : (slot + 1) * SUB, :] = value[col_at : col_at + FINE]
        sources = [field[i * SUB : (i + 1) * SUB] for field in fields for i in range(coarse)]
        for n in range(0, len(sources), 16):
            packed = jnp.zeros((SUB, LANES), jnp.float32)
            for m, value in enumerate(sources[n : n + 16]):
                packed = jnp.where(group == m, roll(value, 8 * m - lane_at, 1), packed)
            slot = 2 * planes + n // 16
            dst[slot * SUB : (slot + 1) * SUB, :] = packed


def pack_columns(floor, lock, stats, from_north, from_south):
    tiles, rows, _ = floor.shape
    blocks = rows // BLK
    planes = strip_planes(rows)
    slots = 2 * planes + -(-3 * (blocks + 2 * HALO_C) // SUB // 16)
    vmem = pl.BlockSpec(memory_space=pltpu.VMEM)
    f32 = jnp.float32
    out = jax.ShapeDtypeStruct((slots * SUB, LANES), f32)
    turned = jax.ShapeDtypeStruct((2, 2, planes, LANES, LANES), f32)
    return pl.pallas_call(
        pack_kernel,
        in_specs=[vmem] * 5,
        out_specs=[vmem] * 3,
        out_shape=[out, out, turned],
        scratch_shapes=[pltpu.VMEM((2, 2, planes * LANES, LANES), f32)],
        compiler_params=pltpu.CompilerParams(vmem_limit_bytes=12 * MIB),
        name="pack",
    )(floor, lock, stats, from_north, from_south)


def strip_kernel(
    stats, from_north, from_south, turned, from_west, from_east, natural, banded,
    out, va_w, va_e, vb_w, vb_e, floor_w, floor_e, lifted, tall, edge, sems, edge_sems,
):
    tiles, rows, _ = natural.shape
    planes = turned.shape[2]
    coarse_cols = tiles * LANES // BLK
    lane = lane_iota()
    va, vb, floor = (va_w, va_e), (vb_w, vb_e), (floor_w, floor_e)
    width = va_w.shape[1]
    inner = width - FINE
    valid = inner - FINE
    spans = (
        (pl.ds(0, valid), lambda j: banded.at[0, j]),
        (pl.ds(valid, rows - 2 * valid), lambda j: natural.at[j, pl.ds(valid, rows - 2 * valid), :]),
        (pl.ds(rows - valid, valid), lambda j: banded.at[1, j]),
    )
    copies = [
        pltpu.make_async_copy(part(j), out.at[span, pl.ds(j * LANES, LANES)], sems.at[n, j])
        for j in range(1, tiles - 1)
        for n, (span, part) in enumerate(spans)
    ]
    for copy in copies:
        copy.start()

    def piece(ref, n, to):
        slot = 2 * planes + n // 16
        return roll(ref[slot * SUB : (slot + 1) * SUB, :], to - 8 * (n % 16), 1)

    fields = []
    for which, field in enumerate(coarse_fields(stats, from_north, from_south)):
        parts = []
        count = field.shape[0] // SUB
        for i in range(count):
            n = which * count + i
            here = field[i * SUB : (i + 1) * SUB]
            here = jnp.where(lane // 8 == coarse_cols // 8, piece(from_east, n, coarse_cols), here)
            here = jnp.where(lane // 8 == 15, piece(from_west, n, LANES - 8), here)
            parts.append(here)
        fields.append(jnp.concatenate(parts, axis=0))
    value = coarse_sweeps(*fields)
    value = jnp.concatenate([value, jnp.zeros((LANES - value.shape[0], LANES), jnp.float32)], axis=0).T
    for c in range(planes):
        index = (planes * lane + (c + HALO_C * BLK - FINE)) // BLK
        for side, groups in enumerate(((LANES - 8, 0), (coarse_cols - 8, coarse_cols))):
            for n, at in enumerate(groups):
                lifted[side, c, n * SUB : (n + 1) * SUB, :] = gather_lanes(value[at : at + SUB], index)

    for side, ref in enumerate((from_west, from_east)):
        for c in range(planes):
            for i in range(width // SUB):
                if (side, i) in ((0, 0), (1, width // SUB - 1)):
                    low, k = (ref[(w * planes + c) * SUB : (w * planes + c + 1) * SUB, :] for w in range(2))
                else:
                    col = (i - 1) * SUB if side == 0 else LANES - inner + i * SUB
                    low, k = (turned[side, w, c, col : col + SUB, :] for w in range(2))
                c_row = (i + 15) // 2 if side == 0 else 8 - COARSE - 1 + i // 2
                at = slice(i * SUB, (i + 1) * SUB)
                floor[side][c, at, :] = low
                va[side][c, at, :] = start_value(low, k, lifted[side, c, c_row : c_row + 1, :])

    count = width // SUB

    def strided(ref):
        return lambda t: [[ref[c, pl.ds(t, SUB, stride=count), :] for c in range(planes)]]

    def keep(dst):
        def store(t, groups):
            for c, value in enumerate(groups[0]):
                dst[c, pl.ds(t, SUB, stride=count), :] = value

        return store

    def twice(i, carry):
        for src, dst in ((va, vb), (vb, va)):
            for side in range(2):
                grouped_sweep(
                    count,
                    strided(src[side]),
                    lambda t, groups: [edge_rolls(groups[0])],
                    strided(floor[side]),
                    keep(dst[side]),
                    count,
                )
        return carry

    lax.fori_loop(0, FINE // 2, twice, 0)

    stores = []
    for side, j in enumerate((0, tiles - 1)):
        fill = jnp.zeros((LANES - inner, LANES), jnp.float32)
        for c in range(planes):
            parts = [va[side][c, FINE:, :], fill] if side == 0 else [fill, va[side][c, 0:inner, :]]
            back = jnp.concatenate(parts, axis=0).T
            for a in range(LANES // SUB):
                tall[side, pl.ds(a * SUB * planes + c, SUB, stride=planes), :] = back[a * SUB : (a + 1) * SUB]
        mine = (lane < valid) if side == 0 else (lane >= LANES - valid)
        for i in range(rows // SUB):
            at = i * SUB
            if at < valid:
                other = banded[0, j, at : at + SUB, :]
            elif at >= rows - valid:
                at_band = at - (rows - valid)
                other = banded[1, j, at_band : at_band + SUB, :]
            else:
                other = natural[j, at : at + SUB, :]
            edge[side, at : at + SUB, :] = jnp.where(mine, tall[side, FINE + at : FINE + at + SUB, :], other)
        stores.append(
            pltpu.make_async_copy(edge.at[side], out.at[:, pl.ds(j * LANES, LANES)], edge_sems.at[side])
        )
        stores[-1].start()
    for copy in copies + stores:
        copy.wait()


def strips(stats, from_north, from_south, turned, from_west, from_east, natural, banded):
    tiles, rows, _ = natural.shape
    planes = turned.shape[2]
    vmem = pl.BlockSpec(memory_space=pltpu.VMEM)
    wide = (planes, COARSE * BLK + 3 * FINE, LANES)
    f32 = jnp.float32
    return pl.pallas_call(
        strip_kernel,
        in_specs=[vmem] * 8,
        out_specs=pl.BlockSpec(memory_space=pltpu.HBM),
        out_shape=jax.ShapeDtypeStruct((rows, tiles * LANES), f32),
        scratch_shapes=[
            *[pltpu.VMEM(wide, f32)] * 6,
            pltpu.VMEM((2, planes, 2 * SUB, LANES), f32),
            pltpu.VMEM((2, planes * LANES, LANES), f32),
            pltpu.VMEM((2, rows, LANES), f32),
            pltpu.SemaphoreType.DMA((3, tiles)),
            pltpu.SemaphoreType.DMA((2,)),
        ],
        compiler_params=pltpu.CompilerParams(vmem_limit_bytes=12 * MIB),
        name="strips",
    )(stats, from_north, from_south, turned, from_west, from_east, natural, banded)


def ring(value, axis, shift):
    count = lax.axis_size(axis)
    return lax.ppermute(value, axis, [(i, (i + shift) % count) for i in range(count)])


def shards(elevation, ocean, outlet):
    floor, lock, floor_t, lock_t, stats, stats_t, north, south = prepare(elevation, ocean, outlet)
    from_south = ring(north, "row", -1)
    from_north = ring(south, "row", 1)
    natural = main_part(floor_t, lock_t, stats_t, elevation.shape[0])
    from_north, from_south, natural = lax.optimization_barrier((from_north, from_south, natural))
    halo_args = (stats, from_north, from_south)
    west, east, turned = pack_columns(floor, lock, *halo_args)
    from_east = ring(west, "col", -1)
    from_west = ring(east, "col", 1)
    banded = bands(floor, lock, *halo_args)
    return strips(*halo_args, turned, from_west, from_east, natural, banded)


def solution(mesh):
    return jax.shard_map(
        shards,
        mesh=mesh,
        in_specs=(P("row", "col"), P("row", "col"), P("row", "col")),
        out_specs=P("row", "col"),
        check_vma=False,
    )
```

```python
import functools

import jax
import jax.numpy as jnp
from jax import lax
from jax.experimental import pallas as pl
from jax.experimental.pallas import tpu as pltpu
from jax.sharding import PartitionSpec as P

BLK = 16
COARSE = 4
FINE = 8
LANES = 128
SUB = 8
HALO_C = 8
UNROLL_T = 112
PITCH = SUB + 1

huge_level = 1e30
fine_step = 2.0 ** (-10)
coarse_step = 2.0 ** (-6)
MIB = 2**20


def roll(x, shift, axis):
    return pltpu.roll(x, shift % x.shape[axis], axis)


def lane_iota(shape=(SUB, LANES)):
    return lax.broadcasted_iota(jnp.int32, shape, 1)


def gather_lanes(x, index):
    return jnp.take_along_axis(x, index, axis=1, mode="promise_in_bounds")


def interior(tiles):
    margin = COARSE * BLK
    chunk = (tiles * LANES - 2 * margin) // SUB
    return margin, chunk


def interior_planes(rows):
    return (rows - 2 * COARSE * BLK) // LANES


def plane_row(col, tiles):
    margin, chunk = interior(tiles)
    return col + (col + chunk - margin) // chunk


def plane_rows(tiles):
    return -(-(plane_row(tiles * LANES, tiles) + 1) // SUB) * SUB


def prepare_kernel(
    elev, ocean, outlet, floor, lock, floor_t, lock_t, stats, stats_t, north, south,
    elev_buf, ocean_buf, outlet_buf, paired, turn, sems,
):
    tiles, rows, _ = floor.shape
    planes = floor_t.shape[0]
    margin = interior(tiles)[0]
    blocks = rows // BLK
    lane = lane_iota()
    sub = lax.broadcasted_iota(jnp.int32, (SUB, LANES), 0)
    unused = jnp.zeros((LANES - 3 * blocks, LANES), jnp.float32)

    def copies(j):
        cols = pl.ds(pl.multiple_of(j * LANES, LANES), LANES)
        return [
            pltpu.make_async_copy(src.at[:, cols], dst.at[j], sems.at[n, j])
            for n, (src, dst) in enumerate(
                ((elev, elev_buf), (ocean, ocean_buf), (outlet, outlet_buf))
            )
        ]

    for j in range(tiles):
        for copy in copies(j):
            copy.start()
    turn[...] = jnp.zeros(turn.shape, jnp.float32)
    for band in (north, south):
        band[tiles:, :, :] = jnp.zeros((2, 2 * FINE, LANES), jnp.float32)

    def tile(j, carry):
        for copy in copies(j):
            copy.wait()
        is_ocean = ocean_buf[j] == 1
        g = jnp.where(is_ocean, jnp.float32(0.0), elev_buf[j])
        k = jnp.where(is_ocean | (outlet_buf[j] == 1), g, jnp.float32(huge_level))
        low = jnp.minimum(g, k)
        elev_buf[j] = g
        floor[j] = low
        lock[j] = k
        north[j, 0:FINE, :] = low[0:FINE]
        north[j, FINE:, :] = k[0:FINE]
        south[j, 0:FINE, :] = low[rows - FINE :]
        south[j, FINE:, :] = k[rows - FINE :]
        for b in range(blocks):
            at = slice(b * BLK, b * BLK + SUB)
            also = slice(b * BLK + SUB, (b + 1) * BLK)
            to = slice(b * PITCH, b * PITCH + SUB)
            paired[0, to, :] = jnp.minimum(g[at], g[also])
            paired[1, to, :] = jnp.minimum(k[at], k[also])
            paired[2, to, :] = -jnp.maximum(g[at], g[also])
        for c in range(planes):
            turned = [
                jnp.concatenate(
                    [
                        ref[j, pl.ds(margin + a * SUB * planes + c, SUB, stride=planes), :]
                        for a in range(LANES // SUB)
                    ],
                    axis=0,
                ).T
                for ref in (elev_buf, lock)
            ]
            for v in range(LANES // SUB):
                g, k = (x[v * SUB : (v + 1) * SUB] for x in turned)
                at = plane_row(j * LANES + v * SUB, tiles)
                floor_t[c, pl.ds(at, SUB), :] = jnp.minimum(g, k)
                lock_t[c, pl.ds(at, SUB), :] = k
        found = [[], [], []]
        for q in range(blocks // SUB):
            for which in range(3):
                for r in range(SUB):
                    value = paired[which, pl.ds(q * SUB * PITCH + r, SUB, stride=PITCH), :]
                    low = value if r == 0 else jnp.minimum(low, value)
                found[which].append(low)
        turned = jnp.concatenate(found[0] + found[1] + found[2] + [unused], axis=0).T
        total = None
        for b in range(LANES // BLK):
            value = jnp.minimum(
                turned[b * BLK : b * BLK + SUB], turned[b * BLK + SUB : (b + 1) * BLK]
            )
            for shift in (4, 2, 1):
                value = jnp.minimum(value, roll(value, shift, 0))
            total = value if b == 0 else jnp.where(sub == b, value, total)
        total = jnp.where(lane // blocks == 2, -total, total)
        at = pl.ds(pl.multiple_of(j * SUB, SUB), SUB)
        stats_t[at, :] = total
        turn[at, :] = total
        return carry

    lax.fori_loop(0, tiles, tile, 0)
    stats[...] = turn[...].T[: 3 * blocks]
    for which in range(3):
        slot = tiles + which // 2
        at = (which % 2) * HALO_C
        first = which * blocks
        north[slot, at : at + HALO_C, :] = stats[first : first + HALO_C, :]
        south[slot, at : at + HALO_C, :] = stats[first + blocks - HALO_C : first + blocks, :]


def prepare(elevation, ocean, outlet):
    rows, cols = elevation.shape
    tiles = cols // LANES
    f32 = jnp.float32
    hbm = pl.BlockSpec(memory_space=pltpu.HBM)
    vmem = pl.BlockSpec(memory_space=pltpu.VMEM)
    natural = (tiles, rows, LANES)
    turned = (interior_planes(rows), plane_rows(tiles), LANES)
    band = (tiles + 2, 2 * FINE, LANES)
    shapes = [natural, natural, turned, turned, (3 * rows // BLK, LANES), (cols // BLK, LANES), band, band]
    return pl.pallas_call(
        prepare_kernel,
        in_specs=[hbm] * 3,
        out_specs=[vmem] * len(shapes),
        out_shape=[jax.ShapeDtypeStruct(shape, f32) for shape in shapes],
        scratch_shapes=[
            pltpu.VMEM(natural, f32),
            pltpu.VMEM(natural, jnp.int32),
            pltpu.VMEM(natural, jnp.int32),
            pltpu.VMEM((3, rows // BLK * PITCH, LANES), f32),
            pltpu.VMEM((LANES, LANES), f32),
            pltpu.SemaphoreType.DMA((3, tiles)),
        ],
        compiler_params=pltpu.CompilerParams(vmem_limit_bytes=24 * MIB),
        name="prepare",
    )(*(pltpu.with_memory_space_constraint(x, pltpu.HBM) for x in (elevation, ocean, outlet)))


def sealed(value, is_edge):
    return jnp.where(is_edge, jnp.float32(huge_level), value)


def edges():
    pos = lax.axis_index("row")
    return pos == 0, pos == lax.axis_size("row") - 1


def coarse_fields(stats, from_north, from_south):
    tiles = from_north.shape[0] - 2
    blocks = stats.shape[0] // 3
    at_north, at_south = edges()
    fields = []
    for which in range(3):
        slot = tiles + which // 2
        at = (which % 2) * HALO_C
        top = sealed(from_north[slot, at : at + HALO_C, :], at_north)
        low = sealed(from_south[slot, at : at + HALO_C, :], at_south)
        mid = stats[which * blocks : (which + 1) * blocks, :]
        fields.append(jnp.concatenate([top, mid, low], axis=0))
    return fields


def coarse_sweeps(ground_c, lock_c, value):
    for _ in range(COARSE):
        across = jnp.minimum(value, jnp.minimum(roll(value, 1, 1), roll(value, -1, 1)))
        around = jnp.minimum(across, jnp.minimum(roll(across, 1, 0), roll(across, -1, 0)))
        lowered = jnp.minimum(value, around + coarse_step)
        value = jnp.minimum(jnp.maximum(ground_c, lowered), lock_c)
    return value


def start_value(floor, lock, lifted):
    return jnp.maximum(floor, jnp.minimum(lifted, lock))


def edge_rolls(tiles):
    return roll(tiles[-1], 1, 1), roll(tiles[0], -1, 1)


def plane_min(edges, groups):
    out = []
    for (above, below), tiles in zip(edges, groups):
        line = [above] + tiles + [below]
        mins = []
        for c in range(0, len(tiles), 2):
            pair = jnp.minimum(line[c + 1], line[c + 2])
            mins.append(jnp.minimum(line[c], pair))
            if c + 1 < len(tiles):
                mins.append(jnp.minimum(pair, line[c + 3]))
        out.append(mins)
    return out


def each(function, *args):
    return [[function(*values) for values in zip(*groups)] for groups in zip(*args)]


def least(*args):
    return each(lambda *values: functools.reduce(jnp.minimum, values), *args)


def lowered(floor, value, around):
    return each(
        lambda f, v, m: jnp.maximum(f, jnp.minimum(v, m + fine_step)), floor, value, around
    )


def grouped_sweep(count, load, edges_at, load_floor, store, unroll):
    def finish(t, around, value):
        store(t, lowered(load_floor(t), value, around))

    first, last = load(0), load(count - 1)
    h_first = plane_min(edges_at(0, first), first)
    h_before = each(lambda h: roll(h, 1, 0), plane_min(edges_at(count - 1, last), last))
    h_after = each(lambda h: roll(h, -1, 0), h_first)

    def line_at(t):
        if isinstance(t, int) and t == count:
            return None, h_after
        value = load(t)
        return value, plane_min(edges_at(t, value), value)

    def span(start, size, carry):
        h_west, h_here, here = carry
        u = 0
        while u < size:
            t = start + u
            value, h_east = line_at(t + 1)
            pair = least(h_here, h_east)
            finish(t, least(h_west, pair), here)
            if u + 1 < size:
                far, h_far = line_at(t + 2)
                finish(t + 1, least(pair, h_far), value)
                h_west, h_here, here = h_east, h_far, far
                u += 2
            else:
                h_west, h_here, here = h_here, h_east, value
                u += 1
        return h_west, h_here, here

    loops = (count - 1) // unroll
    carry = (h_before, h_first, first)
    if loops:
        carry = lax.fori_loop(0, loops, lambda q, c: span(q * unroll, unroll, c), carry)
    span(loops * unroll, count - loops * unroll, carry)


def lines_first_sweep(count, load, edges_at, load_floor, store, unroll):
    def finish(t, lines, value):
        store(t, lowered(load_floor(t), value, plane_min(edges_at(t, lines), lines)))

    first = load(0)
    before = each(lambda v: roll(v, 1, 0), load(count - 1))
    after = each(lambda v: roll(v, -1, 0), first)

    def line_at(t):
        return after if isinstance(t, int) and t == count else load(t)

    def span(start, size, carry):
        west, here = carry
        u = 0
        while u < size:
            t = start + u
            east = line_at(t + 1)
            pair = least(here, east)
            finish(t, least(west, pair), here)
            if u + 1 < size:
                far = line_at(t + 2)
                finish(t + 1, least(pair, far), east)
                west, here = east, far
                u += 2
            else:
                west, here = here, east
                u += 1
        return west, here

    loops = (count - 1) // unroll
    carry = (before, first)
    if loops:
        carry = lax.fori_loop(0, loops, lambda q, c: span(q * unroll, unroll, c), carry)
    span(loops * unroll, count - loops * unroll, carry)


def main_kernel(
    floor_t, lock_t, stats_t, natural, va, vb, coarse, spread, turned
):
    tiles, rows, _ = natural.shape
    planes = floor_t.shape[0]
    blocks = rows // BLK
    margin, chunk = interior(tiles)
    first = plane_row(margin, tiles)
    pitch = chunk + 1
    ground_c = stats_t[...]
    lock_c = roll(ground_c, -blocks, 1)
    value = roll(ground_c, -2 * blocks, 1)
    for _ in range(COARSE):
        across = jnp.minimum(value, jnp.minimum(roll(value, 1, 0), roll(value, -1, 0)))
        around = jnp.minimum(across, jnp.minimum(roll(across, 1, 1), roll(across, -1, 1)))
        lowered = jnp.minimum(value, around + coarse_step)
        value = jnp.minimum(jnp.maximum(ground_c, lowered), lock_c)
    coarse[...] = value
    lane = lane_iota()
    for b in range(chunk // BLK):
        part = coarse[pl.ds(margin // BLK + b, SUB, stride=chunk // BLK), :]
        for c in range(planes):
            spread[c, b] = gather_lanes(part, (planes * lane + c + margin) // BLK)

    def strided(ref):
        return lambda t: [[ref[c, pl.ds(first + t, SUB, stride=pitch), :] for c in range(planes)]]

    load_floor, load_lock = strided(floor_t), strided(lock_t)

    def keep(dst):
        def store(t, groups):
            for c, value in enumerate(groups[0]):
                dst[c, t] = value

        return store

    def start(b, carry):
        for u in range(BLK):
            t = b * BLK + u
            both = zip(load_floor(t)[0], load_lock(t)[0])
            tiles = [[start_value(f, k, spread[c, b]) for c, (f, k) in enumerate(both)]]
            keep(va)(t, tiles)
        return carry

    lax.fori_loop(0, chunk // BLK, start, 0, unroll=True)

    def sweep(src, store):
        grouped_sweep(
            chunk,
            lambda t: [[src[c, t] for c in range(planes)]],
            lambda t, groups: [edge_rolls(groups[0])],
            load_floor,
            store,
            UNROLL_T,
        )

    def twice(i, carry):
        sweep(va, keep(vb))
        sweep(vb, keep(va))
        return carry

    lax.fori_loop(0, FINE // 2 - 1, twice, 0)
    sweep(va, keep(vb))

    def store_last(t, groups):
        for c, value in enumerate(groups[0]):
            turned[c, pl.ds(first + t, SUB, stride=pitch), :] = value

    sweep(vb, store_last)
    cols = tiles * LANES
    for c in range(planes):
        for col in list(range(0, margin, SUB)) + list(range(cols - margin, cols, SUB)):
            at = plane_row(col, tiles)
            turned[c, at : at + SUB, :] = jnp.zeros((SUB, LANES), jnp.float32)

    def finish(j, carry):
        for c in range(planes):
            parts = []
            for v in range(LANES // SUB):
                at = plane_row(j * LANES + v * SUB, tiles)
                parts.append(turned[c, pl.ds(at, SUB), :])
            back = jnp.concatenate(parts, axis=0).T
            for a in range(LANES // SUB):
                natural[j, pl.ds(margin + a * SUB * planes + c, SUB, stride=planes), :] = back[
                    a * SUB : (a + 1) * SUB
                ]
        return carry

    lax.fori_loop(0, tiles, finish, 0, unroll=True)


def main_part(floor_t, lock_t, stats_t, rows):
    planes, length, _ = floor_t.shape
    tiles = stats_t.shape[0] * BLK // LANES
    chunk = interior(tiles)[1]
    vmem = pl.BlockSpec(memory_space=pltpu.VMEM)
    tall = (planes, chunk, SUB, LANES)
    f32 = jnp.float32
    return pl.pallas_call(
        main_kernel,
        in_specs=[vmem] * 3,
        out_specs=vmem,
        out_shape=jax.ShapeDtypeStruct((tiles, rows, LANES), f32),
        scratch_shapes=[
            pltpu.VMEM(tall, f32),
            pltpu.VMEM(tall, f32),
            pltpu.VMEM(stats_t.shape, f32),
            pltpu.VMEM((planes, chunk // BLK, SUB, LANES), f32),
            pltpu.VMEM((planes, length, LANES), f32),
        ],
        compiler_params=pltpu.CompilerParams(vmem_limit_bytes=16 * MIB),
        cost_estimate=pl.CostEstimate(flops=100_000_000, bytes_accessed=20_000_000, transcendentals=0),
        name="middle",
    )(floor_t, lock_t, stats_t)


def split_pair(first, second, even_lane):
    even = jnp.where(even_lane, first, roll(second, 1, 1))
    odd = jnp.where(even_lane, roll(first, -1, 1), second)
    return even, odd


def join_pair(even, odd, even_lane):
    first = jnp.where(even_lane, even, roll(odd, 1, 1))
    second = jnp.where(even_lane, roll(even, -1, 1), odd)
    return first, second


def bands_kernel(
    floor_in, lock, stats, from_north, from_south, out, va_n, va_s, vb_n, vb_s, floor_n, floor_s, lifted
):
    tiles, rows, _ = floor_in.shape
    blocks = rows // BLK
    va, vb, floor = (va_n, va_s), (vb_n, vb_s), (floor_n, floor_s)
    height = va_n.shape[1]
    inner = height - FINE
    pairs = tiles // 2
    at_north, at_south = edges()
    lane = lane_iota()
    even_lane = lane % 2 == 0
    coarse = coarse_sweeps(*coarse_fields(stats, from_north, from_south))
    wide = lane_iota(coarse.shape)
    for j in range(tiles):
        lifted[j] = gather_lanes(coarse, wide // BLK + 8 * j)
    for side, (band, is_edge, at_band, at_inner, first) in enumerate(
        ((from_north, at_north, 0, FINE, 0), (from_south, at_south, inner, 0, rows - inner))
    ):

        def put(at, c_row, fields):
            both = []
            for j in range(2):
                low, k, tile = fields[j]
                both.append((start_value(low, k, lifted[tile, c_row : c_row + 1, :]), low))
            q = fields[0][2]
            for dst, pair in zip((va, floor), zip(*both)):
                for n, value in enumerate(split_pair(*pair, even_lane)):
                    dst[side][q + n, at : at + SUB, :] = value

        for q in range(pairs):
            pair = (2 * q, 2 * q + 1)
            put(
                at_band,
                HALO_C - 1 if side == 0 else HALO_C + blocks,
                [
                    (sealed(band[j, 0:FINE, :], is_edge), sealed(band[j, FINE:, :], is_edge), j)
                    for j in pair
                ],
            )
            for i in range(inner // SUB):
                at = slice(first + i * SUB, first + (i + 1) * SUB)
                c_row = HALO_C + (first + i * SUB) // BLK
                put(at_inner + i * SUB, c_row, [(floor_in[j, at, :], lock[j, at, :], j) for j in pair])

    count = height // SUB
    before = jnp.where(lane < 2, LANES - 1 - lane, lane - 2)
    after = jnp.where(lane < LANES - 2, lane + 2, LANES - 1 - lane)

    def strided(ref):
        return lambda t: [
            [ref[2 * q + n, pl.ds(t, SUB, stride=count), :] for n in range(2)]
            for q in range(pairs)
        ]

    def pair_edges(t, groups):
        above = [gather_lanes(odd, before) for _, odd in groups]
        below = [gather_lanes(even, after) for even, _ in groups]
        return [
            (
                jnp.where(lane == 0, above[q - 1], above[q]),
                jnp.where(lane == LANES - 1, below[(q + 1) % pairs], below[q]),
            )
            for q in range(pairs)
        ]

    def keep(dst):
        def store(t, groups):
            for q, pair in enumerate(groups):
                for n, value in enumerate(pair):
                    dst[2 * q + n, pl.ds(t, SUB, stride=count), :] = value

        return store

    def twice(i, carry):
        for src, dst in ((va, vb), (vb, va)):
            for side in range(2):
                lines_first_sweep(
                    count,
                    strided(src[side]),
                    pair_edges,
                    strided(floor[side]),
                    keep(dst[side]),
                    count,
                )
        return carry

    lax.fori_loop(0, FINE // 2, twice, 0, unroll=True)
    for side in range(2):
        for i in range(out.shape[2] // SUB):
            at = slice(FINE + i * SUB, FINE + (i + 1) * SUB)
            for q in range(pairs):
                pair = join_pair(va[side][2 * q, at, :], va[side][2 * q + 1, at, :], even_lane)
                for n, value in enumerate(pair):
                    out[side, 2 * q + n, i * SUB : (i + 1) * SUB, :] = value


def bands(floor, lock, stats, from_north, from_south):
    tiles, rows, _ = floor.shape
    blocks = rows // BLK
    vmem = pl.BlockSpec(memory_space=pltpu.VMEM)
    height = COARSE * BLK + 3 * FINE
    tall = (tiles, height, LANES)
    f32 = jnp.float32
    return pl.pallas_call(
        bands_kernel,
        in_specs=[vmem] * 5,
        out_specs=vmem,
        out_shape=jax.ShapeDtypeStruct((2, tiles, height - 2 * FINE, LANES), f32),
        scratch_shapes=[
            *[pltpu.VMEM(tall, f32)] * 6,
            pltpu.VMEM((tiles, blocks + 2 * HALO_C, LANES), f32),
        ],
        compiler_params=pltpu.CompilerParams(vmem_limit_bytes=16 * MIB),
        cost_estimate=pl.CostEstimate(flops=60_000_000, bytes_accessed=12_000_000, transcendentals=0),
        name="bands",
    )(floor, lock, stats, from_north, from_south)


def strip_planes(rows):
    return -(-(rows + 2 * FINE) // LANES)


def pack_kernel(
    floor, lock, stats, from_north, from_south, west, east, turned, tall
):
    tiles, rows, _ = floor.shape
    blocks = rows // BLK
    planes = turned.shape[2]
    at_north, at_south = edges()
    group = lane_iota() // 8
    fields = coarse_fields(stats, from_north, from_south)
    coarse = fields[0].shape[0] // SUB
    coarse_cols = tiles * LANES // BLK
    rest = tall.shape[2] - rows - 2 * FINE
    for side, (dst, j, col_at, lane_at) in enumerate(
        ((west, 0, 0, 0), (east, tiles - 1, LANES - FINE, coarse_cols - 8))
    ):
        for which, ref in enumerate((floor, lock)):
            at = slice(which * FINE, (which + 1) * FINE)
            tall[side, which, 0:FINE, :] = sealed(from_north[j, at, :], at_north)
            tall[side, which, FINE : FINE + rows, :] = ref[j]
            tall[side, which, FINE + rows : 2 * FINE + rows, :] = sealed(from_south[j, at, :], at_south)
            tall[side, which, 2 * FINE + rows :, :] = jnp.full((rest, LANES), huge_level, jnp.float32)
            for c in range(planes):
                parts = [
                    tall[side, which, pl.ds(a * SUB * planes + c, SUB, stride=planes), :]
                    for a in range(LANES // SUB)
                ]
                value = jnp.concatenate(parts, axis=0).T
                turned[side, which, c] = value
                slot = which * planes + c
                dst[slot * SUB : (slot + 1) * SUB, :] = value[col_at : col_at + FINE]
        sources = [field[i * SUB : (i + 1) * SUB] for field in fields for i in range(coarse)]
        for n in range(0, len(sources), 16):
            packed = jnp.zeros((SUB, LANES), jnp.float32)
            for m, value in enumerate(sources[n : n + 16]):
                packed = jnp.where(group == m, roll(value, 8 * m - lane_at, 1), packed)
            slot = 2 * planes + n // 16
            dst[slot * SUB : (slot + 1) * SUB, :] = packed


def pack_columns(floor, lock, stats, from_north, from_south):
    tiles, rows, _ = floor.shape
    blocks = rows // BLK
    planes = strip_planes(rows)
    slots = 2 * planes + -(-3 * (blocks + 2 * HALO_C) // SUB // 16)
    vmem = pl.BlockSpec(memory_space=pltpu.VMEM)
    f32 = jnp.float32
    out = jax.ShapeDtypeStruct((slots * SUB, LANES), f32)
    turned = jax.ShapeDtypeStruct((2, 2, planes, LANES, LANES), f32)
    return pl.pallas_call(
        pack_kernel,
        in_specs=[vmem] * 5,
        out_specs=[vmem] * 3,
        out_shape=[out, out, turned],
        scratch_shapes=[pltpu.VMEM((2, 2, planes * LANES, LANES), f32)],
        compiler_params=pltpu.CompilerParams(vmem_limit_bytes=12 * MIB),
        name="pack",
    )(floor, lock, stats, from_north, from_south)


def strip_kernel(
    stats, from_north, from_south, turned, from_west, from_east, natural, banded,
    out, va_w, va_e, vb_w, vb_e, floor_w, floor_e, lifted, tall, edge, sems, edge_sems,
):
    tiles, rows, _ = natural.shape
    planes = turned.shape[2]
    coarse_cols = tiles * LANES // BLK
    lane = lane_iota()
    va, vb, floor = (va_w, va_e), (vb_w, vb_e), (floor_w, floor_e)
    width = va_w.shape[1]
    inner = width - FINE
    valid = inner - FINE
    spans = (
        (pl.ds(0, valid), lambda j: banded.at[0, j]),
        (pl.ds(valid, rows - 2 * valid), lambda j: natural.at[j, pl.ds(valid, rows - 2 * valid), :]),
        (pl.ds(rows - valid, valid), lambda j: banded.at[1, j]),
    )
    copies = [
        pltpu.make_async_copy(part(j), out.at[span, pl.ds(j * LANES, LANES)], sems.at[n, j])
        for j in range(1, tiles - 1)
        for n, (span, part) in enumerate(spans)
    ]
    for copy in copies:
        copy.start()

    def piece(ref, n, to):
        slot = 2 * planes + n // 16
        return roll(ref[slot * SUB : (slot + 1) * SUB, :], to - 8 * (n % 16), 1)

    fields = []
    for which, field in enumerate(coarse_fields(stats, from_north, from_south)):
        parts = []
        count = field.shape[0] // SUB
        for i in range(count):
            n = which * count + i
            here = field[i * SUB : (i + 1) * SUB]
            here = jnp.where(lane // 8 == coarse_cols // 8, piece(from_east, n, coarse_cols), here)
            here = jnp.where(lane // 8 == 15, piece(from_west, n, LANES - 8), here)
            parts.append(here)
        fields.append(jnp.concatenate(parts, axis=0))
    value = coarse_sweeps(*fields)
    value = jnp.concatenate([value, jnp.zeros((LANES - value.shape[0], LANES), jnp.float32)], axis=0).T
    for c in range(planes):
        index = (planes * lane + (c + HALO_C * BLK - FINE)) // BLK
        for side, groups in enumerate(((LANES - 8, 0), (coarse_cols - 8, coarse_cols))):
            for n, at in enumerate(groups):
                lifted[side, c, n * SUB : (n + 1) * SUB, :] = gather_lanes(value[at : at + SUB], index)

    for side, ref in enumerate((from_west, from_east)):
        for c in range(planes):
            for i in range(width // SUB):
                if (side, i) in ((0, 0), (1, width // SUB - 1)):
                    low, k = (ref[(w * planes + c) * SUB : (w * planes + c + 1) * SUB, :] for w in range(2))
                else:
                    col = (i - 1) * SUB if side == 0 else LANES - inner + i * SUB
                    low, k = (turned[side, w, c, col : col + SUB, :] for w in range(2))
                c_row = (i + 15) // 2 if side == 0 else 8 - COARSE - 1 + i // 2
                at = slice(i * SUB, (i + 1) * SUB)
                floor[side][c, at, :] = low
                va[side][c, at, :] = start_value(low, k, lifted[side, c, c_row : c_row + 1, :])

    count = width // SUB

    def strided(ref):
        return lambda t: [[ref[c, pl.ds(t, SUB, stride=count), :] for c in range(planes)]]

    def keep(dst):
        def store(t, groups):
            for c, value in enumerate(groups[0]):
                dst[c, pl.ds(t, SUB, stride=count), :] = value

        return store

    def twice(i, carry):
        for src, dst in ((va, vb), (vb, va)):
            for side in range(2):
                grouped_sweep(
                    count,
                    strided(src[side]),
                    lambda t, groups: [edge_rolls(groups[0])],
                    strided(floor[side]),
                    keep(dst[side]),
                    count,
                )
        return carry

    lax.fori_loop(0, FINE // 2, twice, 0)

    stores = []
    for side, j in enumerate((0, tiles - 1)):
        fill = jnp.zeros((LANES - inner, LANES), jnp.float32)
        for c in range(planes):
            parts = [va[side][c, FINE:, :], fill] if side == 0 else [fill, va[side][c, 0:inner, :]]
            back = jnp.concatenate(parts, axis=0).T
            for a in range(LANES // SUB):
                tall[side, pl.ds(a * SUB * planes + c, SUB, stride=planes), :] = back[a * SUB : (a + 1) * SUB]
        mine = (lane < valid) if side == 0 else (lane >= LANES - valid)
        for i in range(rows // SUB):
            at = i * SUB
            if at < valid:
                other = banded[0, j, at : at + SUB, :]
            elif at >= rows - valid:
                at_band = at - (rows - valid)
                other = banded[1, j, at_band : at_band + SUB, :]
            else:
                other = natural[j, at : at + SUB, :]
            edge[side, at : at + SUB, :] = jnp.where(mine, tall[side, FINE + at : FINE + at + SUB, :], other)
        stores.append(
            pltpu.make_async_copy(edge.at[side], out.at[:, pl.ds(j * LANES, LANES)], edge_sems.at[side])
        )
        stores[-1].start()
    for copy in copies + stores:
        copy.wait()


def strips(stats, from_north, from_south, turned, from_west, from_east, natural, banded):
    tiles, rows, _ = natural.shape
    planes = turned.shape[2]
    vmem = pl.BlockSpec(memory_space=pltpu.VMEM)
    wide = (planes, COARSE * BLK + 3 * FINE, LANES)
    f32 = jnp.float32
    return pl.pallas_call(
        strip_kernel,
        in_specs=[vmem] * 8,
        out_specs=pl.BlockSpec(memory_space=pltpu.HBM),
        out_shape=jax.ShapeDtypeStruct((rows, tiles * LANES), f32),
        scratch_shapes=[
            *[pltpu.VMEM(wide, f32)] * 6,
            pltpu.VMEM((2, planes, 2 * SUB, LANES), f32),
            pltpu.VMEM((2, planes * LANES, LANES), f32),
            pltpu.VMEM((2, rows, LANES), f32),
            pltpu.SemaphoreType.DMA((3, tiles)),
            pltpu.SemaphoreType.DMA((2,)),
        ],
        compiler_params=pltpu.CompilerParams(vmem_limit_bytes=12 * MIB),
        name="strips",
    )(stats, from_north, from_south, turned, from_west, from_east, natural, banded)


def ring(value, axis, shift):
    count = lax.axis_size(axis)
    return lax.ppermute(value, axis, [(i, (i + shift) % count) for i in range(count)])


def shards(elevation, ocean, outlet):
    floor, lock, floor_t, lock_t, stats, stats_t, north, south = prepare(elevation, ocean, outlet)
    from_south = ring(north, "row", -1)
    from_north = ring(south, "row", 1)
    natural = main_part(floor_t, lock_t, stats_t, elevation.shape[0])
    from_north, from_south, natural = lax.optimization_barrier((from_north, from_south, natural))
    halo_args = (stats, from_north, from_south)
    west, east, turned = pack_columns(floor, lock, *halo_args)
    from_east = ring(west, "col", -1)
    from_west = ring(east, "col", 1)
    banded = bands(floor, lock, *halo_args)
    return strips(*halo_args, turned, from_west, from_east, natural, banded)


def solution(mesh):
    return jax.shard_map(
        shards,
        mesh=mesh,
        in_specs=(P("row", "col"), P("row", "col"), P("row", "col")),
        out_specs=P("row", "col"),
        check_vma=False,
    )
```

```python
import functools

import jax
import jax.numpy as jnp
from jax import lax
from jax.experimental import pallas as pl
from jax.experimental.pallas import tpu as pltpu
from jax.sharding import PartitionSpec as P

BLK = 16
COARSE = 4
FINE = 8
LANES = 128
SUB = 8
HALO_C = 8
UNROLL_T = 112
PITCH = SUB + 1

huge_level = 1e30
fine_step = 2.0 ** (-10)
coarse_step = 2.0 ** (-6)
MIB = 2**20


def roll(x, shift, axis):
    return pltpu.roll(x, shift % x.shape[axis], axis)


def lane_iota(shape=(SUB, LANES)):
    return lax.broadcasted_iota(jnp.int32, shape, 1)


def gather_lanes(x, index):
    return jnp.take_along_axis(x, index, axis=1, mode="promise_in_bounds")


def interior(tiles):
    margin = COARSE * BLK
    chunk = (tiles * LANES - 2 * margin) // SUB
    return margin, chunk


def interior_planes(rows):
    return (rows - 2 * COARSE * BLK) // LANES


def plane_row(col, tiles):
    margin, chunk = interior(tiles)
    return col + (col + chunk - margin) // chunk


def plane_rows(tiles):
    return -(-(plane_row(tiles * LANES, tiles) + 1) // SUB) * SUB


def prepare_kernel(
    elev, ocean, outlet, floor, lock, floor_t, lock_t, stats, stats_t, north, south,
    elev_buf, ocean_buf, outlet_buf, paired, turn, sems,
):
    tiles, rows, _ = floor.shape
    planes = floor_t.shape[0]
    margin = interior(tiles)[0]
    blocks = rows // BLK
    lane = lane_iota()
    sub = lax.broadcasted_iota(jnp.int32, (SUB, LANES), 0)
    unused = jnp.zeros((LANES - 3 * blocks, LANES), jnp.float32)

    def copies(j):
        cols = pl.ds(pl.multiple_of(j * LANES, LANES), LANES)
        return [
            pltpu.make_async_copy(src.at[:, cols], dst.at[j], sems.at[n, j])
            for n, (src, dst) in enumerate(
                ((elev, elev_buf), (ocean, ocean_buf), (outlet, outlet_buf))
            )
        ]

    for j in range(tiles):
        for copy in copies(j):
            copy.start()
    turn[...] = jnp.zeros(turn.shape, jnp.float32)
    for band in (north, south):
        band[tiles:, :, :] = jnp.zeros((2, 2 * FINE, LANES), jnp.float32)

    def tile(j, carry):
        for copy in copies(j):
            copy.wait()
        is_ocean = ocean_buf[j] == 1
        g = jnp.where(is_ocean, jnp.float32(0.0), elev_buf[j])
        k = jnp.where(is_ocean | (outlet_buf[j] == 1), g, jnp.float32(huge_level))
        low = jnp.minimum(g, k)
        elev_buf[j] = g
        floor[j] = low
        lock[j] = k
        north[j, 0:FINE, :] = low[0:FINE]
        north[j, FINE:, :] = k[0:FINE]
        south[j, 0:FINE, :] = low[rows - FINE :]
        south[j, FINE:, :] = k[rows - FINE :]
        for b in range(blocks):
            at = slice(b * BLK, b * BLK + SUB)
            also = slice(b * BLK + SUB, (b + 1) * BLK)
            to = slice(b * PITCH, b * PITCH + SUB)
            paired[0, to, :] = jnp.minimum(g[at], g[also])
            paired[1, to, :] = jnp.minimum(k[at], k[also])
            paired[2, to, :] = -jnp.maximum(g[at], g[also])
        for c in range(planes):
            turned = [
                jnp.concatenate(
                    [
                        ref[j, pl.ds(margin + a * SUB * planes + c, SUB, stride=planes), :]
                        for a in range(LANES // SUB)
                    ],
                    axis=0,
                ).T
                for ref in (elev_buf, lock)
            ]
            for v in range(LANES // SUB):
                g, k = (x[v * SUB : (v + 1) * SUB] for x in turned)
                at = plane_row(j * LANES + v * SUB, tiles)
                floor_t[c, pl.ds(at, SUB), :] = jnp.minimum(g, k)
                lock_t[c, pl.ds(at, SUB), :] = k
        found = [[], [], []]
        for q in range(blocks // SUB):
            for which in range(3):
                for r in range(SUB):
                    value = paired[which, pl.ds(q * SUB * PITCH + r, SUB, stride=PITCH), :]
                    low = value if r == 0 else jnp.minimum(low, value)
                found[which].append(low)
        turned = jnp.concatenate(found[0] + found[1] + found[2] + [unused], axis=0).T
        total = None
        for b in range(LANES // BLK):
            value = jnp.minimum(
                turned[b * BLK : b * BLK + SUB], turned[b * BLK + SUB : (b + 1) * BLK]
            )
            for shift in (4, 2, 1):
                value = jnp.minimum(value, roll(value, shift, 0))
            total = value if b == 0 else jnp.where(sub == b, value, total)
        total = jnp.where(lane // blocks == 2, -total, total)
        at = pl.ds(pl.multiple_of(j * SUB, SUB), SUB)
        stats_t[at, :] = total
        turn[at, :] = total
        return carry

    lax.fori_loop(0, tiles, tile, 0)
    stats[...] = turn[...].T[: 3 * blocks]
    for which in range(3):
        slot = tiles + which // 2
        at = (which % 2) * HALO_C
        first = which * blocks
        north[slot, at : at + HALO_C, :] = stats[first : first + HALO_C, :]
        south[slot, at : at + HALO_C, :] = stats[first + blocks - HALO_C : first + blocks, :]


def prepare(elevation, ocean, outlet):
    rows, cols = elevation.shape
    tiles = cols // LANES
    f32 = jnp.float32
    hbm = pl.BlockSpec(memory_space=pltpu.HBM)
    vmem = pl.BlockSpec(memory_space=pltpu.VMEM)
    natural = (tiles, rows, LANES)
    turned = (interior_planes(rows), plane_rows(tiles), LANES)
    band = (tiles + 2, 2 * FINE, LANES)
    shapes = [natural, natural, turned, turned, (3 * rows // BLK, LANES), (cols // BLK, LANES), band, band]
    return pl.pallas_call(
        prepare_kernel,
        in_specs=[hbm] * 3,
        out_specs=[vmem] * len(shapes),
        out_shape=[jax.ShapeDtypeStruct(shape, f32) for shape in shapes],
        scratch_shapes=[
            pltpu.VMEM(natural, f32),
            pltpu.VMEM(natural, jnp.int32),
            pltpu.VMEM(natural, jnp.int32),
            pltpu.VMEM((3, rows // BLK * PITCH, LANES), f32),
            pltpu.VMEM((LANES, LANES), f32),
            pltpu.SemaphoreType.DMA((3, tiles)),
        ],
        compiler_params=pltpu.CompilerParams(vmem_limit_bytes=24 * MIB),
        name="prepare",
    )(*(pltpu.with_memory_space_constraint(x, pltpu.HBM) for x in (elevation, ocean, outlet)))


def sealed(value, is_edge):
    return jnp.where(is_edge, jnp.float32(huge_level), value)


def edges():
    pos = lax.axis_index("row")
    return pos == 0, pos == lax.axis_size("row") - 1


def coarse_fields(stats, from_north, from_south):
    tiles = from_north.shape[0] - 2
    blocks = stats.shape[0] // 3
    at_north, at_south = edges()
    fields = []
    for which in range(3):
        slot = tiles + which // 2
        at = (which % 2) * HALO_C
        top = sealed(from_north[slot, at : at + HALO_C, :], at_north)
        low = sealed(from_south[slot, at : at + HALO_C, :], at_south)
        mid = stats[which * blocks : (which + 1) * blocks, :]
        fields.append(jnp.concatenate([top, mid, low], axis=0))
    return fields


def coarse_sweeps(ground_c, lock_c, value):
    for _ in range(COARSE):
        across = jnp.minimum(value, jnp.minimum(roll(value, 1, 1), roll(value, -1, 1)))
        around = jnp.minimum(across, jnp.minimum(roll(across, 1, 0), roll(across, -1, 0)))
        lowered = jnp.minimum(value, around + coarse_step)
        value = jnp.minimum(jnp.maximum(ground_c, lowered), lock_c)
    return value


def start_value(floor, lock, lifted):
    return jnp.maximum(floor, jnp.minimum(lifted, lock))


def edge_rolls(tiles):
    return roll(tiles[-1], 1, 1), roll(tiles[0], -1, 1)


def plane_min(edges, groups):
    out = []
    for (above, below), tiles in zip(edges, groups):
        line = [above] + tiles + [below]
        mins = []
        for c in range(0, len(tiles), 2):
            pair = jnp.minimum(line[c + 1], line[c + 2])
            mins.append(jnp.minimum(line[c], pair))
            if c + 1 < len(tiles):
                mins.append(jnp.minimum(pair, line[c + 3]))
        out.append(mins)
    return out


def each(function, *args):
    return [[function(*values) for values in zip(*groups)] for groups in zip(*args)]


def least(*args):
    return each(lambda *values: functools.reduce(jnp.minimum, values), *args)


def lowered(floor, value, around):
    return each(
        lambda f, v, m: jnp.maximum(f, jnp.minimum(v, m + fine_step)), floor, value, around
    )


def grouped_sweep(count, load, edges_at, load_floor, store, unroll):
    def finish(t, around, value):
        store(t, lowered(load_floor(t), value, around))

    first, last = load(0), load(count - 1)
    h_first = plane_min(edges_at(0, first), first)
    h_before = each(lambda h: roll(h, 1, 0), plane_min(edges_at(count - 1, last), last))
    h_after = each(lambda h: roll(h, -1, 0), h_first)

    def line_at(t):
        if isinstance(t, int) and t == count:
            return None, h_after
        value = load(t)
        return value, plane_min(edges_at(t, value), value)

    def span(start, size, carry):
        h_west, h_here, here = carry
        u = 0
        while u < size:
            t = start + u
            value, h_east = line_at(t + 1)
            pair = least(h_here, h_east)
            finish(t, least(h_west, pair), here)
            if u + 1 < size:
                far, h_far = line_at(t + 2)
                finish(t + 1, least(pair, h_far), value)
                h_west, h_here, here = h_east, h_far, far
                u += 2
            else:
                h_west, h_here, here = h_here, h_east, value
                u += 1
        return h_west, h_here, here

    loops = (count - 1) // unroll
    carry = (h_before, h_first, first)
    if loops:
        carry = lax.fori_loop(0, loops, lambda q, c: span(q * unroll, unroll, c), carry)
    span(loops * unroll, count - loops * unroll, carry)


def lines_first_sweep(count, load, edges_at, load_floor, store, unroll):
    def finish(t, lines, value):
        store(t, lowered(load_floor(t), value, plane_min(edges_at(t, lines), lines)))

    first = load(0)
    before = each(lambda v: roll(v, 1, 0), load(count - 1))
    after = each(lambda v: roll(v, -1, 0), first)

    def line_at(t):
        return after if isinstance(t, int) and t == count else load(t)

    def span(start, size, carry):
        west, here = carry
        u = 0
        while u < size:
            t = start + u
            east = line_at(t + 1)
            pair = least(here, east)
            finish(t, least(west, pair), here)
            if u + 1 < size:
                far = line_at(t + 2)
                finish(t + 1, least(pair, far), east)
                west, here = east, far
                u += 2
            else:
                west, here = here, east
                u += 1
        return west, here

    loops = (count - 1) // unroll
    carry = (before, first)
    if loops:
        carry = lax.fori_loop(0, loops, lambda q, c: span(q * unroll, unroll, c), carry)
    span(loops * unroll, count - loops * unroll, carry)


def main_kernel(
    floor_t, lock_t, stats_t, natural, va, vb, coarse, spread, turned
):
    tiles, rows, _ = natural.shape
    planes = floor_t.shape[0]
    blocks = rows // BLK
    margin, chunk = interior(tiles)
    first = plane_row(margin, tiles)
    pitch = chunk + 1
    ground_c = stats_t[...]
    lock_c = roll(ground_c, -blocks, 1)
    value = roll(ground_c, -2 * blocks, 1)
    for _ in range(COARSE):
        across = jnp.minimum(value, jnp.minimum(roll(value, 1, 0), roll(value, -1, 0)))
        around = jnp.minimum(across, jnp.minimum(roll(across, 1, 1), roll(across, -1, 1)))
        lowered = jnp.minimum(value, around + coarse_step)
        value = jnp.minimum(jnp.maximum(ground_c, lowered), lock_c)
    coarse[...] = value
    lane = lane_iota()
    for b in range(chunk // BLK):
        part = coarse[pl.ds(margin // BLK + b, SUB, stride=chunk // BLK), :]
        for c in range(planes):
            spread[c, b] = gather_lanes(part, (planes * lane + c + margin) // BLK)

    def strided(ref):
        return lambda t: [[ref[c, pl.ds(first + t, SUB, stride=pitch), :] for c in range(planes)]]

    load_floor, load_lock = strided(floor_t), strided(lock_t)

    def keep(dst):
        def store(t, groups):
            for c, value in enumerate(groups[0]):
                dst[c, t] = value

        return store

    def start(b, carry):
        for u in range(BLK):
            t = b * BLK + u
            both = zip(load_floor(t)[0], load_lock(t)[0])
            tiles = [[start_value(f, k, spread[c, b]) for c, (f, k) in enumerate(both)]]
            keep(va)(t, tiles)
        return carry

    lax.fori_loop(0, chunk // BLK, start, 0, unroll=True)

    def sweep(src, store):
        grouped_sweep(
            chunk,
            lambda t: [[src[c, t] for c in range(planes)]],
            lambda t, groups: [edge_rolls(groups[0])],
            load_floor,
            store,
            UNROLL_T,
        )

    def twice(i, carry):
        sweep(va, keep(vb))
        sweep(vb, keep(va))
        return carry

    lax.fori_loop(0, FINE // 2 - 1, twice, 0)
    sweep(va, keep(vb))

    def store_last(t, groups):
        for c, value in enumerate(groups[0]):
            turned[c, pl.ds(first + t, SUB, stride=pitch), :] = value

    sweep(vb, store_last)
    cols = tiles * LANES
    for c in range(planes):
        for col in list(range(0, margin, SUB)) + list(range(cols - margin, cols, SUB)):
            at = plane_row(col, tiles)
            turned[c, at : at + SUB, :] = jnp.zeros((SUB, LANES), jnp.float32)

    def finish(j, carry):
        for c in range(planes):
            parts = []
            for v in range(LANES // SUB):
                at = plane_row(j * LANES + v * SUB, tiles)
                parts.append(turned[c, pl.ds(at, SUB), :])
            back = jnp.concatenate(parts, axis=0).T
            for a in range(LANES // SUB):
                natural[j, pl.ds(margin + a * SUB * planes + c, SUB, stride=planes), :] = back[
                    a * SUB : (a + 1) * SUB
                ]
        return carry

    lax.fori_loop(0, tiles, finish, 0, unroll=True)


def main_part(floor_t, lock_t, stats_t, rows):
    planes, length, _ = floor_t.shape
    tiles = stats_t.shape[0] * BLK // LANES
    chunk = interior(tiles)[1]
    vmem = pl.BlockSpec(memory_space=pltpu.VMEM)
    tall = (planes, chunk, SUB, LANES)
    f32 = jnp.float32
    return pl.pallas_call(
        main_kernel,
        in_specs=[vmem] * 3,
        out_specs=vmem,
        out_shape=jax.ShapeDtypeStruct((tiles, rows, LANES), f32),
        scratch_shapes=[
            pltpu.VMEM(tall, f32),
            pltpu.VMEM(tall, f32),
            pltpu.VMEM(stats_t.shape, f32),
            pltpu.VMEM((planes, chunk // BLK, SUB, LANES), f32),
            pltpu.VMEM((planes, length, LANES), f32),
        ],
        compiler_params=pltpu.CompilerParams(vmem_limit_bytes=16 * MIB),
        cost_estimate=pl.CostEstimate(flops=100_000_000, bytes_accessed=20_000_000, transcendentals=0),
        name="middle",
    )(floor_t, lock_t, stats_t)


def split_pair(first, second, even_lane):
    even = jnp.where(even_lane, first, roll(second, 1, 1))
    odd = jnp.where(even_lane, roll(first, -1, 1), second)
    return even, odd


def join_pair(even, odd, even_lane):
    first = jnp.where(even_lane, even, roll(odd, 1, 1))
    second = jnp.where(even_lane, roll(even, -1, 1), odd)
    return first, second


def bands_kernel(
    floor_in, lock, stats, from_north, from_south, out, va_n, va_s, vb_n, vb_s, floor_n, floor_s, lifted
):
    tiles, rows, _ = floor_in.shape
    blocks = rows // BLK
    va, vb, floor = (va_n, va_s), (vb_n, vb_s), (floor_n, floor_s)
    height = va_n.shape[1]
    inner = height - FINE
    pairs = tiles // 2
    at_north, at_south = edges()
    lane = lane_iota()
    even_lane = lane % 2 == 0
    coarse = coarse_sweeps(*coarse_fields(stats, from_north, from_south))
    wide = lane_iota(coarse.shape)
    for j in range(tiles):
        lifted[j] = gather_lanes(coarse, wide // BLK + 8 * j)
    for side, (band, is_edge, at_band, at_inner, first) in enumerate(
        ((from_north, at_north, 0, FINE, 0), (from_south, at_south, inner, 0, rows - inner))
    ):

        def put(at, c_row, fields):
            both = []
            for j in range(2):
                low, k, tile = fields[j]
                both.append((start_value(low, k, lifted[tile, c_row : c_row + 1, :]), low))
            q = fields[0][2]
            for dst, pair in zip((va, floor), zip(*both)):
                for n, value in enumerate(split_pair(*pair, even_lane)):
                    dst[side][q + n, at : at + SUB, :] = value

        for q in range(pairs):
            pair = (2 * q, 2 * q + 1)
            put(
                at_band,
                HALO_C - 1 if side == 0 else HALO_C + blocks,
                [
                    (sealed(band[j, 0:FINE, :], is_edge), sealed(band[j, FINE:, :], is_edge), j)
                    for j in pair
                ],
            )
            for i in range(inner // SUB):
                at = slice(first + i * SUB, first + (i + 1) * SUB)
                c_row = HALO_C + (first + i * SUB) // BLK
                put(at_inner + i * SUB, c_row, [(floor_in[j, at, :], lock[j, at, :], j) for j in pair])

    count = height // SUB
    before = jnp.where(lane < 2, LANES - 1 - lane, lane - 2)
    after = jnp.where(lane < LANES - 2, lane + 2, LANES - 1 - lane)

    def strided(ref):
        return lambda t: [
            [ref[2 * q + n, pl.ds(t, SUB, stride=count), :] for n in range(2)]
            for q in range(pairs)
        ]

    def pair_edges(t, groups):
        above = [gather_lanes(odd, before) for _, odd in groups]
        below = [gather_lanes(even, after) for even, _ in groups]
        return [
            (
                jnp.where(lane == 0, above[q - 1], above[q]),
                jnp.where(lane == LANES - 1, below[(q + 1) % pairs], below[q]),
            )
            for q in range(pairs)
        ]

    def keep(dst):
        def store(t, groups):
            for q, pair in enumerate(groups):
                for n, value in enumerate(pair):
                    dst[2 * q + n, pl.ds(t, SUB, stride=count), :] = value

        return store

    def twice(i, carry):
        for src, dst in ((va, vb), (vb, va)):
            for side in range(2):
                lines_first_sweep(
                    count,
                    strided(src[side]),
                    pair_edges,
                    strided(floor[side]),
                    keep(dst[side]),
                    count,
                )
        return carry

    lax.fori_loop(0, FINE // 2, twice, 0, unroll=True)
    for side in range(2):
        for i in range(out.shape[2] // SUB):
            at = slice(FINE + i * SUB, FINE + (i + 1) * SUB)
            for q in range(pairs):
                pair = join_pair(va[side][2 * q, at, :], va[side][2 * q + 1, at, :], even_lane)
                for n, value in enumerate(pair):
                    out[side, 2 * q + n, i * SUB : (i + 1) * SUB, :] = value


def bands(floor, lock, stats, from_north, from_south):
    tiles, rows, _ = floor.shape
    blocks = rows // BLK
    vmem = pl.BlockSpec(memory_space=pltpu.VMEM)
    height = COARSE * BLK + 3 * FINE
    tall = (tiles, height, LANES)
    f32 = jnp.float32
    return pl.pallas_call(
        bands_kernel,
        in_specs=[vmem] * 5,
        out_specs=vmem,
        out_shape=jax.ShapeDtypeStruct((2, tiles, height - 2 * FINE, LANES), f32),
        scratch_shapes=[
            *[pltpu.VMEM(tall, f32)] * 6,
            pltpu.VMEM((tiles, blocks + 2 * HALO_C, LANES), f32),
        ],
        compiler_params=pltpu.CompilerParams(vmem_limit_bytes=16 * MIB),
        cost_estimate=pl.CostEstimate(flops=60_000_000, bytes_accessed=12_000_000, transcendentals=0),
        name="bands",
    )(floor, lock, stats, from_north, from_south)


def strip_planes(rows):
    return -(-(rows + 2 * FINE) // LANES)


def pack_kernel(
    floor, lock, stats, from_north, from_south, west, east, turned, tall
):
    tiles, rows, _ = floor.shape
    blocks = rows // BLK
    planes = turned.shape[2]
    at_north, at_south = edges()
    group = lane_iota() // 8
    fields = coarse_fields(stats, from_north, from_south)
    coarse = fields[0].shape[0] // SUB
    coarse_cols = tiles * LANES // BLK
    rest = tall.shape[2] - rows - 2 * FINE
    span = SUB * planes
    inside = [a * span >= FINE and (a + 1) * span - FINE <= rows for a in range(LANES // SUB)]
    head = inside.index(True) * span - FINE
    foot = (LANES // SUB - inside[::-1].index(True)) * span - FINE
    for side, (dst, j, col_at, lane_at) in enumerate(
        ((west, 0, 0, 0), (east, tiles - 1, LANES - FINE, coarse_cols - 8))
    ):
        for which, ref in enumerate((floor, lock)):
            at = slice(which * FINE, (which + 1) * FINE)
            tall[side, which, 0:FINE, :] = sealed(from_north[j, at, :], at_north)
            for at_local in range(0, rows, SUB):
                if at_local < head or at_local + SUB > foot:
                    to = FINE + at_local
                    tall[side, which, to : to + SUB, :] = ref[j, at_local : at_local + SUB, :]
            tall[side, which, FINE + rows : 2 * FINE + rows, :] = sealed(from_south[j, at, :], at_south)
            tall[side, which, 2 * FINE + rows :, :] = jnp.full((rest, LANES), huge_level, jnp.float32)
            for c in range(planes):
                parts = []
                for a in range(LANES // SUB):
                    at = a * span + c
                    if inside[a]:
                        part = ref[j, pl.ds(at - FINE, SUB, stride=planes), :]
                    else:
                        part = tall[side, which, pl.ds(at, SUB, stride=planes), :]
                    parts.append(part)
                value = jnp.concatenate(parts, axis=0).T
                turned[side, which, c] = value
                slot = which * planes + c
                dst[slot * SUB : (slot + 1) * SUB, :] = value[col_at : col_at + FINE]
        sources = [field[i * SUB : (i + 1) * SUB] for field in fields for i in range(coarse)]
        for n in range(0, len(sources), 16):
            packed = jnp.zeros((SUB, LANES), jnp.float32)
            for m, value in enumerate(sources[n : n + 16]):
                packed = jnp.where(group == m, roll(value, 8 * m - lane_at, 1), packed)
            slot = 2 * planes + n // 16
            dst[slot * SUB : (slot + 1) * SUB, :] = packed


def pack_columns(floor, lock, stats, from_north, from_south):
    tiles, rows, _ = floor.shape
    blocks = rows // BLK
    planes = strip_planes(rows)
    slots = 2 * planes + -(-3 * (blocks + 2 * HALO_C) // SUB // 16)
    vmem = pl.BlockSpec(memory_space=pltpu.VMEM)
    f32 = jnp.float32
    out = jax.ShapeDtypeStruct((slots * SUB, LANES), f32)
    turned = jax.ShapeDtypeStruct((2, 2, planes, LANES, LANES), f32)
    return pl.pallas_call(
        pack_kernel,
        in_specs=[vmem] * 5,
        out_specs=[vmem] * 3,
        out_shape=[out, out, turned],
        scratch_shapes=[pltpu.VMEM((2, 2, planes * LANES, LANES), f32)],
        compiler_params=pltpu.CompilerParams(vmem_limit_bytes=12 * MIB),
        name="pack",
    )(floor, lock, stats, from_north, from_south)


def strip_kernel(
    stats, from_north, from_south, turned, from_west, from_east, natural, banded,
    out, va_w, va_e, vb_w, vb_e, floor_w, floor_e, lifted, tall, edge, sems, edge_sems,
):
    tiles, rows, _ = natural.shape
    planes = turned.shape[2]
    coarse_cols = tiles * LANES // BLK
    lane = lane_iota()
    va, vb, floor = (va_w, va_e), (vb_w, vb_e), (floor_w, floor_e)
    width = va_w.shape[1]
    inner = width - FINE
    valid = inner - FINE
    spans = (
        (pl.ds(0, valid), lambda j: banded.at[0, j]),
        (pl.ds(valid, rows - 2 * valid), lambda j: natural.at[j, pl.ds(valid, rows - 2 * valid), :]),
        (pl.ds(rows - valid, valid), lambda j: banded.at[1, j]),
    )
    copies = [
        pltpu.make_async_copy(part(j), out.at[span, pl.ds(j * LANES, LANES)], sems.at[n, j])
        for j in range(1, tiles - 1)
        for n, (span, part) in enumerate(spans)
    ]
    for copy in copies:
        copy.start()

    def piece(ref, n, to):
        slot = 2 * planes + n // 16
        return roll(ref[slot * SUB : (slot + 1) * SUB, :], to - 8 * (n % 16), 1)

    fields = []
    for which, field in enumerate(coarse_fields(stats, from_north, from_south)):
        parts = []
        count = field.shape[0] // SUB
        for i in range(count):
            n = which * count + i
            here = field[i * SUB : (i + 1) * SUB]
            here = jnp.where(lane // 8 == coarse_cols // 8, piece(from_east, n, coarse_cols), here)
            here = jnp.where(lane // 8 == 15, piece(from_west, n, LANES - 8), here)
            parts.append(here)
        fields.append(jnp.concatenate(parts, axis=0))
    value = coarse_sweeps(*fields)
    value = jnp.concatenate([value, jnp.zeros((LANES - value.shape[0], LANES), jnp.float32)], axis=0).T
    for c in range(planes):
        index = (planes * lane + (c + HALO_C * BLK - FINE)) // BLK
        for side, groups in enumerate(((LANES - 8, 0), (coarse_cols - 8, coarse_cols))):
            for n, at in enumerate(groups):
                lifted[side, c, n * SUB : (n + 1) * SUB, :] = gather_lanes(value[at : at + SUB], index)

    for side, ref in enumerate((from_west, from_east)):
        for c in range(planes):
            for i in range(width // SUB):
                if (side, i) in ((0, 0), (1, width // SUB - 1)):
                    low, k = (ref[(w * planes + c) * SUB : (w * planes + c + 1) * SUB, :] for w in range(2))
                else:
                    col = (i - 1) * SUB if side == 0 else LANES - inner + i * SUB
                    low, k = (turned[side, w, c, col : col + SUB, :] for w in range(2))
                c_row = (i + 15) // 2 if side == 0 else 8 - COARSE - 1 + i // 2
                at = slice(i * SUB, (i + 1) * SUB)
                floor[side][c, at, :] = low
                va[side][c, at, :] = start_value(low, k, lifted[side, c, c_row : c_row + 1, :])

    count = width // SUB

    def strided(ref):
        return lambda t: [[ref[c, pl.ds(t, SUB, stride=count), :] for c in range(planes)]]

    def keep(dst):
        def store(t, groups):
            for c, value in enumerate(groups[0]):
                dst[c, pl.ds(t, SUB, stride=count), :] = value

        return store

    def twice(i, carry):
        for src, dst in ((va, vb), (vb, va)):
            for side in range(2):
                grouped_sweep(
                    count,
                    strided(src[side]),
                    lambda t, groups: [edge_rolls(groups[0])],
                    strided(floor[side]),
                    keep(dst[side]),
                    count,
                )
        return carry

    lax.fori_loop(0, FINE // 2, twice, 0)

    stores = []
    for side, j in enumerate((0, tiles - 1)):
        fill = jnp.zeros((LANES - inner, LANES), jnp.float32)
        for c in range(planes):
            parts = [va[side][c, FINE:, :], fill] if side == 0 else [fill, va[side][c, 0:inner, :]]
            back = jnp.concatenate(parts, axis=0).T
            for a in range(LANES // SUB):
                tall[side, pl.ds(a * SUB * planes + c, SUB, stride=planes), :] = back[a * SUB : (a + 1) * SUB]
        mine = (lane < valid) if side == 0 else (lane >= LANES - valid)
        for i in range(rows // SUB):
            at = i * SUB
            if at < valid:
                other = banded[0, j, at : at + SUB, :]
            elif at >= rows - valid:
                at_band = at - (rows - valid)
                other = banded[1, j, at_band : at_band + SUB, :]
            else:
                other = natural[j, at : at + SUB, :]
            edge[side, at : at + SUB, :] = jnp.where(mine, tall[side, FINE + at : FINE + at + SUB, :], other)
        stores.append(
            pltpu.make_async_copy(edge.at[side], out.at[:, pl.ds(j * LANES, LANES)], edge_sems.at[side])
        )
        stores[-1].start()
    for copy in copies + stores:
        copy.wait()


def strips(stats, from_north, from_south, turned, from_west, from_east, natural, banded):
    tiles, rows, _ = natural.shape
    planes = turned.shape[2]
    vmem = pl.BlockSpec(memory_space=pltpu.VMEM)
    wide = (planes, COARSE * BLK + 3 * FINE, LANES)
    f32 = jnp.float32
    return pl.pallas_call(
        strip_kernel,
        in_specs=[vmem] * 8,
        out_specs=pl.BlockSpec(memory_space=pltpu.HBM),
        out_shape=jax.ShapeDtypeStruct((rows, tiles * LANES), f32),
        scratch_shapes=[
            *[pltpu.VMEM(wide, f32)] * 6,
            pltpu.VMEM((2, planes, 2 * SUB, LANES), f32),
            pltpu.VMEM((2, planes * LANES, LANES), f32),
            pltpu.VMEM((2, rows, LANES), f32),
            pltpu.SemaphoreType.DMA((3, tiles)),
            pltpu.SemaphoreType.DMA((2,)),
        ],
        compiler_params=pltpu.CompilerParams(vmem_limit_bytes=12 * MIB),
        name="strips",
    )(stats, from_north, from_south, turned, from_west, from_east, natural, banded)


def ring(value, axis, shift):
    count = lax.axis_size(axis)
    return lax.ppermute(value, axis, [(i, (i + shift) % count) for i in range(count)])


def shards(elevation, ocean, outlet):
    floor, lock, floor_t, lock_t, stats, stats_t, north, south = prepare(elevation, ocean, outlet)
    from_north = ring(south, "row", 1)
    from_south = ring(north, "row", -1)
    natural = main_part(floor_t, lock_t, stats_t, elevation.shape[0])
    from_north, from_south, natural = lax.optimization_barrier((from_north, from_south, natural))
    halo_args = (stats, from_north, from_south)
    west, east, turned = pack_columns(floor, lock, *halo_args)
    from_west = ring(east, "col", 1)
    from_east = ring(west, "col", -1)
    banded = bands(floor, lock, *halo_args)
    return strips(*halo_args, turned, from_west, from_east, natural, banded)


def solution(mesh):
    return jax.shard_map(
        shards,
        mesh=mesh,
        in_specs=(P("row", "col"), P("row", "col"), P("row", "col")),
        out_specs=P("row", "col"),
        check_vma=False,
    )
```

```python
import functools

import jax
import jax.numpy as jnp
from jax import lax
from jax.experimental import pallas as pl
from jax.experimental.pallas import tpu as pltpu
from jax.sharding import PartitionSpec as P

BLK = 16
COARSE = 4
FINE = 8
LANES = 128
SUB = 8
HALO_C = 8
UNROLL_T = 112
PITCH = SUB + 1

huge_level = 1e30
fine_step = 2.0 ** (-10)
coarse_step = 2.0 ** (-6)
MIB = 2**20


def roll(x, shift, axis):
    return pltpu.roll(x, shift % x.shape[axis], axis)


def lane_iota(shape=(SUB, LANES)):
    return lax.broadcasted_iota(jnp.int32, shape, 1)


def gather_lanes(x, index):
    return jnp.take_along_axis(x, index, axis=1, mode="promise_in_bounds")


def interior(tiles):
    margin = COARSE * BLK
    chunk = (tiles * LANES - 2 * margin) // SUB
    return margin, chunk


def interior_planes(rows):
    return (rows - 2 * COARSE * BLK) // LANES


def plane_row(col, tiles):
    margin, chunk = interior(tiles)
    return col + (col + chunk - margin) // chunk


def plane_rows(tiles):
    return -(-(plane_row(tiles * LANES, tiles) + 1) // SUB) * SUB


def prepare_kernel(
    elev, ocean, outlet, floor, lock, floor_t, lock_t, stats, stats_t, north, south,
    elev_buf, ocean_buf, outlet_buf, paired, turn, sems,
):
    tiles, rows, _ = floor.shape
    planes = floor_t.shape[0]
    margin = interior(tiles)[0]
    blocks = rows // BLK
    lane = lane_iota()
    sub = lax.broadcasted_iota(jnp.int32, (SUB, LANES), 0)
    unused = jnp.zeros((LANES - 3 * blocks, LANES), jnp.float32)

    def copies(j):
        cols = pl.ds(pl.multiple_of(j * LANES, LANES), LANES)
        return [
            pltpu.make_async_copy(src.at[:, cols], dst.at[j], sems.at[n, j])
            for n, (src, dst) in enumerate(
                ((elev, elev_buf), (ocean, ocean_buf), (outlet, outlet_buf))
            )
        ]

    for j in range(tiles):
        for copy in copies(j):
            copy.start()
    turn[...] = jnp.zeros(turn.shape, jnp.float32)
    for band in (north, south):
        band[tiles:, :, :] = jnp.zeros((2, 2 * FINE, LANES), jnp.float32)

    def tile(j, carry):
        for copy in copies(j):
            copy.wait()
        is_ocean = ocean_buf[j] == 1
        g = jnp.where(is_ocean, jnp.float32(0.0), elev_buf[j])
        k = jnp.where(is_ocean | (outlet_buf[j] == 1), g, jnp.float32(huge_level))
        low = jnp.minimum(g, k)
        elev_buf[j] = g
        floor[j] = low
        lock[j] = k
        north[j, 0:FINE, :] = low[0:FINE]
        north[j, FINE:, :] = k[0:FINE]
        south[j, 0:FINE, :] = low[rows - FINE :]
        south[j, FINE:, :] = k[rows - FINE :]
        for b in range(blocks):
            at = slice(b * BLK, b * BLK + SUB)
            also = slice(b * BLK + SUB, (b + 1) * BLK)
            to = slice(b * PITCH, b * PITCH + SUB)
            paired[0, to, :] = jnp.minimum(g[at], g[also])
            paired[1, to, :] = jnp.minimum(k[at], k[also])
            paired[2, to, :] = -jnp.maximum(g[at], g[also])
        for c in range(planes):
            turned = [
                jnp.concatenate(
                    [
                        ref[j, pl.ds(margin + a * SUB * planes + c, SUB, stride=planes), :]
                        for a in range(LANES // SUB)
                    ],
                    axis=0,
                ).T
                for ref in (elev_buf, lock)
            ]
            for v in range(LANES // SUB):
                g, k = (x[v * SUB : (v + 1) * SUB] for x in turned)
                at = plane_row(j * LANES + v * SUB, tiles)
                floor_t[c, pl.ds(at, SUB), :] = jnp.minimum(g, k)
                lock_t[c, pl.ds(at, SUB), :] = k
        found = [[], [], []]
        for q in range(blocks // SUB):
            for which in range(3):
                for r in range(SUB):
                    value = paired[which, pl.ds(q * SUB * PITCH + r, SUB, stride=PITCH), :]
                    low = value if r == 0 else jnp.minimum(low, value)
                found[which].append(low)
        turned = jnp.concatenate(found[0] + found[1] + found[2] + [unused], axis=0).T
        total = None
        for b in range(LANES // BLK):
            value = jnp.minimum(
                turned[b * BLK : b * BLK + SUB], turned[b * BLK + SUB : (b + 1) * BLK]
            )
            for shift in (4, 2, 1):
                value = jnp.minimum(value, roll(value, shift, 0))
            total = value if b == 0 else jnp.where(sub == b, value, total)
        total = jnp.where(lane // blocks == 2, -total, total)
        at = pl.ds(pl.multiple_of(j * SUB, SUB), SUB)
        stats_t[at, :] = total
        turn[at, :] = total
        return carry

    lax.fori_loop(0, tiles, tile, 0)
    stats[...] = turn[...].T[: 3 * blocks]
    for which in range(3):
        slot = tiles + which // 2
        at = (which % 2) * HALO_C
        first = which * blocks
        north[slot, at : at + HALO_C, :] = stats[first : first + HALO_C, :]
        south[slot, at : at + HALO_C, :] = stats[first + blocks - HALO_C : first + blocks, :]


def prepare(elevation, ocean, outlet):
    rows, cols = elevation.shape
    tiles = cols // LANES
    f32 = jnp.float32
    hbm = pl.BlockSpec(memory_space=pltpu.HBM)
    vmem = pl.BlockSpec(memory_space=pltpu.VMEM)
    natural = (tiles, rows, LANES)
    turned = (interior_planes(rows), plane_rows(tiles), LANES)
    band = (tiles + 2, 2 * FINE, LANES)
    shapes = [natural, natural, turned, turned, (3 * rows // BLK, LANES), (cols // BLK, LANES), band, band]
    return pl.pallas_call(
        prepare_kernel,
        in_specs=[hbm] * 3,
        out_specs=[vmem] * len(shapes),
        out_shape=[jax.ShapeDtypeStruct(shape, f32) for shape in shapes],
        scratch_shapes=[
            pltpu.VMEM(natural, f32),
            pltpu.VMEM(natural, jnp.int32),
            pltpu.VMEM(natural, jnp.int32),
            pltpu.VMEM((3, rows // BLK * PITCH, LANES), f32),
            pltpu.VMEM((LANES, LANES), f32),
            pltpu.SemaphoreType.DMA((3, tiles)),
        ],
        compiler_params=pltpu.CompilerParams(vmem_limit_bytes=24 * MIB),
        name="prepare",
    )(*(pltpu.with_memory_space_constraint(x, pltpu.HBM) for x in (elevation, ocean, outlet)))


def sealed(value, is_edge):
    return jnp.where(is_edge, jnp.float32(huge_level), value)


def edges():
    pos = lax.axis_index("row")
    return pos == 0, pos == lax.axis_size("row") - 1


def coarse_fields(stats, from_north, from_south):
    tiles = from_north.shape[0] - 2
    blocks = stats.shape[0] // 3
    at_north, at_south = edges()
    fields = []
    for which in range(3):
        slot = tiles + which // 2
        at = (which % 2) * HALO_C
        top = sealed(from_north[slot, at : at + HALO_C, :], at_north)
        low = sealed(from_south[slot, at : at + HALO_C, :], at_south)
        mid = stats[which * blocks : (which + 1) * blocks, :]
        fields.append(jnp.concatenate([top, mid, low], axis=0))
    return fields


def coarse_sweeps(ground_c, lock_c, value):
    for _ in range(COARSE):
        across = jnp.minimum(value, jnp.minimum(roll(value, 1, 1), roll(value, -1, 1)))
        around = jnp.minimum(across, jnp.minimum(roll(across, 1, 0), roll(across, -1, 0)))
        lowered = jnp.minimum(value, around + coarse_step)
        value = jnp.minimum(jnp.maximum(ground_c, lowered), lock_c)
    return value


def start_value(floor, lock, lifted):
    return jnp.maximum(floor, jnp.minimum(lifted, lock))


def edge_rolls(tiles):
    return roll(tiles[-1], 1, 1), roll(tiles[0], -1, 1)


def plane_min(edges, groups):
    out = []
    for (above, below), tiles in zip(edges, groups):
        line = [above] + tiles + [below]
        mins = []
        for c in range(0, len(tiles), 2):
            pair = jnp.minimum(line[c + 1], line[c + 2])
            mins.append(jnp.minimum(line[c], pair))
            if c + 1 < len(tiles):
                mins.append(jnp.minimum(pair, line[c + 3]))
        out.append(mins)
    return out


def each(function, *args):
    return [[function(*values) for values in zip(*groups)] for groups in zip(*args)]


def least(*args):
    return each(lambda *values: functools.reduce(jnp.minimum, values), *args)


def lowered(floor, value, around):
    return each(
        lambda f, v, m: jnp.maximum(f, jnp.minimum(v, m + fine_step)), floor, value, around
    )


def grouped_sweep(count, load, edges_at, load_floor, store, unroll):
    def finish(t, around, value):
        store(t, lowered(load_floor(t), value, around))

    first, last = load(0), load(count - 1)
    h_first = plane_min(edges_at(0, first), first)
    h_before = each(lambda h: roll(h, 1, 0), plane_min(edges_at(count - 1, last), last))
    h_after = each(lambda h: roll(h, -1, 0), h_first)

    def line_at(t):
        if isinstance(t, int) and t == count:
            return None, h_after
        value = load(t)
        return value, plane_min(edges_at(t, value), value)

    def span(start, size, carry):
        h_west, h_here, here = carry
        u = 0
        while u < size:
            t = start + u
            value, h_east = line_at(t + 1)
            pair = least(h_here, h_east)
            finish(t, least(h_west, pair), here)
            if u + 1 < size:
                far, h_far = line_at(t + 2)
                finish(t + 1, least(pair, h_far), value)
                h_west, h_here, here = h_east, h_far, far
                u += 2
            else:
                h_west, h_here, here = h_here, h_east, value
                u += 1
        return h_west, h_here, here

    loops = (count - 1) // unroll
    carry = (h_before, h_first, first)
    if loops:
        carry = lax.fori_loop(0, loops, lambda q, c: span(q * unroll, unroll, c), carry)
    span(loops * unroll, count - loops * unroll, carry)


def lines_first_sweep(count, load, edges_at, load_floor, store, unroll):
    def finish(t, lines, value):
        store(t, lowered(load_floor(t), value, plane_min(edges_at(t, lines), lines)))

    first = load(0)
    before = each(lambda v: roll(v, 1, 0), load(count - 1))
    after = each(lambda v: roll(v, -1, 0), first)

    def line_at(t):
        return after if isinstance(t, int) and t == count else load(t)

    def span(start, size, carry):
        west, here = carry
        u = 0
        while u < size:
            t = start + u
            east = line_at(t + 1)
            pair = least(here, east)
            finish(t, least(west, pair), here)
            if u + 1 < size:
                far = line_at(t + 2)
                finish(t + 1, least(pair, far), east)
                west, here = east, far
                u += 2
            else:
                west, here = here, east
                u += 1
        return west, here

    loops = (count - 1) // unroll
    carry = (before, first)
    if loops:
        carry = lax.fori_loop(0, loops, lambda q, c: span(q * unroll, unroll, c), carry)
    span(loops * unroll, count - loops * unroll, carry)


def main_kernel(
    floor_t, lock_t, stats_t, natural, va, vb, coarse, spread, turned
):
    tiles, rows, _ = natural.shape
    planes = floor_t.shape[0]
    blocks = rows // BLK
    margin, chunk = interior(tiles)
    first = plane_row(margin, tiles)
    pitch = chunk + 1
    ground_c = stats_t[...]
    lock_c = roll(ground_c, -blocks, 1)
    value = roll(ground_c, -2 * blocks, 1)
    for _ in range(COARSE):
        across = jnp.minimum(value, jnp.minimum(roll(value, 1, 0), roll(value, -1, 0)))
        around = jnp.minimum(across, jnp.minimum(roll(across, 1, 1), roll(across, -1, 1)))
        lowered = jnp.minimum(value, around + coarse_step)
        value = jnp.minimum(jnp.maximum(ground_c, lowered), lock_c)
    coarse[...] = value
    lane = lane_iota()
    for b in range(chunk // BLK):
        part = coarse[pl.ds(margin // BLK + b, SUB, stride=chunk // BLK), :]
        for c in range(planes):
            spread[c, b] = gather_lanes(part, (planes * lane + c + margin) // BLK)

    def strided(ref):
        return lambda t: [[ref[c, pl.ds(first + t, SUB, stride=pitch), :] for c in range(planes)]]

    load_floor, load_lock = strided(floor_t), strided(lock_t)

    def keep(dst):
        def store(t, groups):
            for c, value in enumerate(groups[0]):
                dst[c, t] = value

        return store

    def start(b, carry):
        for u in range(BLK):
            t = b * BLK + u
            both = zip(load_floor(t)[0], load_lock(t)[0])
            tiles = [[start_value(f, k, spread[c, b]) for c, (f, k) in enumerate(both)]]
            keep(va)(t, tiles)
        return carry

    lax.fori_loop(0, chunk // BLK, start, 0, unroll=True)

    def sweep(src, store):
        grouped_sweep(
            chunk,
            lambda t: [[src[c, t] for c in range(planes)]],
            lambda t, groups: [edge_rolls(groups[0])],
            load_floor,
            store,
            UNROLL_T,
        )

    def twice(i, carry):
        sweep(va, keep(vb))
        sweep(vb, keep(va))
        return carry

    lax.fori_loop(0, FINE // 2 - 1, twice, 0)
    sweep(va, keep(vb))

    def store_last(t, groups):
        for c, value in enumerate(groups[0]):
            turned[c, pl.ds(first + t, SUB, stride=pitch), :] = value

    sweep(vb, store_last)
    cols = tiles * LANES
    for c in range(planes):
        for col in list(range(0, margin, SUB)) + list(range(cols - margin, cols, SUB)):
            at = plane_row(col, tiles)
            turned[c, at : at + SUB, :] = jnp.zeros((SUB, LANES), jnp.float32)

    def finish(j, carry):
        for c in range(planes):
            parts = []
            for v in range(LANES // SUB):
                at = plane_row(j * LANES + v * SUB, tiles)
                parts.append(turned[c, pl.ds(at, SUB), :])
            back = jnp.concatenate(parts, axis=0).T
            for a in range(LANES // SUB):
                natural[j, pl.ds(margin + a * SUB * planes + c, SUB, stride=planes), :] = back[
                    a * SUB : (a + 1) * SUB
                ]
        return carry

    lax.fori_loop(0, tiles, finish, 0, unroll=True)


def main_part(floor_t, lock_t, stats_t, rows):
    planes, length, _ = floor_t.shape
    tiles = stats_t.shape[0] * BLK // LANES
    chunk = interior(tiles)[1]
    vmem = pl.BlockSpec(memory_space=pltpu.VMEM)
    tall = (planes, chunk, SUB, LANES)
    f32 = jnp.float32
    return pl.pallas_call(
        main_kernel,
        in_specs=[vmem] * 3,
        out_specs=vmem,
        out_shape=jax.ShapeDtypeStruct((tiles, rows, LANES), f32),
        scratch_shapes=[
            pltpu.VMEM(tall, f32),
            pltpu.VMEM(tall, f32),
            pltpu.VMEM(stats_t.shape, f32),
            pltpu.VMEM((planes, chunk // BLK, SUB, LANES), f32),
            pltpu.VMEM((planes, length, LANES), f32),
        ],
        compiler_params=pltpu.CompilerParams(vmem_limit_bytes=16 * MIB),
        cost_estimate=pl.CostEstimate(flops=100_000_000, bytes_accessed=20_000_000, transcendentals=0),
        name="middle",
    )(floor_t, lock_t, stats_t)


def split_pair(first, second, even_lane):
    even = jnp.where(even_lane, first, roll(second, 1, 1))
    odd = jnp.where(even_lane, roll(first, -1, 1), second)
    return even, odd


def join_pair(even, odd, even_lane):
    first = jnp.where(even_lane, even, roll(odd, 1, 1))
    second = jnp.where(even_lane, roll(even, -1, 1), odd)
    return first, second


def bands_kernel(
    floor_in, lock, stats, from_north, from_south, out, va_n, va_s, vb_n, vb_s, floor_n, floor_s, lifted
):
    tiles, rows, _ = floor_in.shape
    blocks = rows // BLK
    va, vb, floor = (va_n, va_s), (vb_n, vb_s), (floor_n, floor_s)
    height = va_n.shape[1]
    inner = height - FINE
    pairs = tiles // 2
    at_north, at_south = edges()
    lane = lane_iota()
    even_lane = lane % 2 == 0
    coarse = coarse_sweeps(*coarse_fields(stats, from_north, from_south))
    wide = lane_iota(coarse.shape)
    for j in range(tiles):
        for part in (slice(0, 2 * SUB), slice(coarse.shape[0] - 2 * SUB, coarse.shape[0])):
            lifted[j, part, :] = gather_lanes(coarse[part], wide[part] // BLK + 8 * j)
    for side, (band, is_edge, at_band, at_inner, first) in enumerate(
        ((from_north, at_north, 0, FINE, 0), (from_south, at_south, inner, 0, rows - inner))
    ):

        def put(at, c_row, fields):
            both = []
            for j in range(2):
                low, k, tile = fields[j]
                both.append((start_value(low, k, lifted[tile, c_row : c_row + 1, :]), low))
            q = fields[0][2]
            for dst, pair in zip((va, floor), zip(*both)):
                for n, value in enumerate(split_pair(*pair, even_lane)):
                    dst[side][q + n, at : at + SUB, :] = value

        for q in range(pairs):
            pair = (2 * q, 2 * q + 1)
            put(
                at_band,
                HALO_C - 1 if side == 0 else HALO_C + blocks,
                [
                    (sealed(band[j, 0:FINE, :], is_edge), sealed(band[j, FINE:, :], is_edge), j)
                    for j in pair
                ],
            )
            for i in range(inner // SUB):
                at = slice(first + i * SUB, first + (i + 1) * SUB)
                c_row = HALO_C + (first + i * SUB) // BLK
                put(at_inner + i * SUB, c_row, [(floor_in[j, at, :], lock[j, at, :], j) for j in pair])

    count = height // SUB
    before = jnp.where(lane < 2, LANES - 1 - lane, lane - 2)
    after = jnp.where(lane < LANES - 2, lane + 2, LANES - 1 - lane)

    def strided(ref):
        return lambda t: [
            [ref[2 * q + n, pl.ds(t, SUB, stride=count), :] for n in range(2)]
            for q in range(pairs)
        ]

    def pair_edges(t, groups):
        above = [gather_lanes(odd, before) for _, odd in groups]
        below = [gather_lanes(even, after) for even, _ in groups]
        return [
            (
                jnp.where(lane == 0, above[q - 1], above[q]),
                jnp.where(lane == LANES - 1, below[(q + 1) % pairs], below[q]),
            )
            for q in range(pairs)
        ]

    def keep(dst):
        def store(t, groups):
            for q, pair in enumerate(groups):
                for n, value in enumerate(pair):
                    dst[2 * q + n, pl.ds(t, SUB, stride=count), :] = value

        return store

    def twice(i, carry):
        for src, dst in ((va, vb), (vb, va)):
            for side in range(2):
                lines_first_sweep(
                    count,
                    strided(src[side]),
                    pair_edges,
                    strided(floor[side]),
                    keep(dst[side]),
                    count,
                )
        return carry

    lax.fori_loop(0, FINE // 2, twice, 0, unroll=True)
    for side in range(2):
        for i in range(out.shape[2] // SUB):
            at = slice(FINE + i * SUB, FINE + (i + 1) * SUB)
            for q in range(pairs):
                pair = join_pair(va[side][2 * q, at, :], va[side][2 * q + 1, at, :], even_lane)
                for n, value in enumerate(pair):
                    out[side, 2 * q + n, i * SUB : (i + 1) * SUB, :] = value


def bands(floor, lock, stats, from_north, from_south):
    tiles, rows, _ = floor.shape
    blocks = rows // BLK
    vmem = pl.BlockSpec(memory_space=pltpu.VMEM)
    height = COARSE * BLK + 3 * FINE
    tall = (tiles, height, LANES)
    f32 = jnp.float32
    return pl.pallas_call(
        bands_kernel,
        in_specs=[vmem] * 5,
        out_specs=vmem,
        out_shape=jax.ShapeDtypeStruct((2, tiles, height - 2 * FINE, LANES), f32),
        scratch_shapes=[
            *[pltpu.VMEM(tall, f32)] * 6,
            pltpu.VMEM((tiles, blocks + 2 * HALO_C, LANES), f32),
        ],
        compiler_params=pltpu.CompilerParams(vmem_limit_bytes=16 * MIB),
        cost_estimate=pl.CostEstimate(flops=60_000_000, bytes_accessed=12_000_000, transcendentals=0),
        name="bands",
    )(floor, lock, stats, from_north, from_south)


def strip_planes(rows):
    return -(-(rows + 2 * FINE) // LANES)


def pack_kernel(
    floor, lock, stats, from_north, from_south, west, east, turned, tall
):
    tiles, rows, _ = floor.shape
    blocks = rows // BLK
    planes = turned.shape[2]
    at_north, at_south = edges()
    group = lane_iota() // 8
    fields = coarse_fields(stats, from_north, from_south)
    coarse = fields[0].shape[0] // SUB
    coarse_cols = tiles * LANES // BLK
    rest = tall.shape[2] - rows - 2 * FINE
    span = SUB * planes
    inside = [a * span >= FINE and (a + 1) * span - FINE <= rows for a in range(LANES // SUB)]
    head = inside.index(True) * span - FINE
    foot = (LANES // SUB - inside[::-1].index(True)) * span - FINE
    for side, (dst, j, col_at, lane_at) in enumerate(
        ((west, 0, 0, 0), (east, tiles - 1, LANES - FINE, coarse_cols - 8))
    ):
        for which, ref in enumerate((floor, lock)):
            at = slice(which * FINE, (which + 1) * FINE)
            tall[side, which, 0:FINE, :] = sealed(from_north[j, at, :], at_north)
            for at_local in range(0, rows, SUB):
                if at_local < head or at_local + SUB > foot:
                    to = FINE + at_local
                    tall[side, which, to : to + SUB, :] = ref[j, at_local : at_local + SUB, :]
            tall[side, which, FINE + rows : 2 * FINE + rows, :] = sealed(from_south[j, at, :], at_south)
            tall[side, which, 2 * FINE + rows :, :] = jnp.full((rest, LANES), huge_level, jnp.float32)
            for c in range(planes):
                parts = []
                for a in range(LANES // SUB):
                    at = a * span + c
                    if inside[a]:
                        part = ref[j, pl.ds(at - FINE, SUB, stride=planes), :]
                    else:
                        part = tall[side, which, pl.ds(at, SUB, stride=planes), :]
                    parts.append(part)
                value = jnp.concatenate(parts, axis=0).T
                used = slice(0, COARSE * BLK + 2 * FINE) if side == 0 else slice(LANES - COARSE * BLK - 2 * FINE, LANES)
                turned[side, which, c, used, :] = value[used]
                slot = which * planes + c
                dst[slot * SUB : (slot + 1) * SUB, :] = value[col_at : col_at + FINE]
        sources = [field[i * SUB : (i + 1) * SUB] for field in fields for i in range(coarse)]
        for n in range(0, len(sources), 16):
            packed = jnp.zeros((SUB, LANES), jnp.float32)
            for m, value in enumerate(sources[n : n + 16]):
                packed = jnp.where(group == m, roll(value, 8 * m - lane_at, 1), packed)
            slot = 2 * planes + n // 16
            dst[slot * SUB : (slot + 1) * SUB, :] = packed


def pack_columns(floor, lock, stats, from_north, from_south):
    tiles, rows, _ = floor.shape
    blocks = rows // BLK
    planes = strip_planes(rows)
    slots = 2 * planes + -(-3 * (blocks + 2 * HALO_C) // SUB // 16)
    vmem = pl.BlockSpec(memory_space=pltpu.VMEM)
    f32 = jnp.float32
    out = jax.ShapeDtypeStruct((slots * SUB, LANES), f32)
    turned = jax.ShapeDtypeStruct((2, 2, planes, LANES, LANES), f32)
    return pl.pallas_call(
        pack_kernel,
        in_specs=[vmem] * 5,
        out_specs=[vmem] * 3,
        out_shape=[out, out, turned],
        scratch_shapes=[pltpu.VMEM((2, 2, planes * LANES, LANES), f32)],
        compiler_params=pltpu.CompilerParams(vmem_limit_bytes=12 * MIB),
        name="pack",
    )(floor, lock, stats, from_north, from_south)


def strip_kernel(
    stats, from_north, from_south, turned, from_west, from_east, natural, banded,
    out, va_w, va_e, vb_w, vb_e, floor_w, floor_e, lifted, tall, edge, sems, edge_sems,
):
    tiles, rows, _ = natural.shape
    planes = turned.shape[2]
    coarse_cols = tiles * LANES // BLK
    lane = lane_iota()
    va, vb, floor = (va_w, va_e), (vb_w, vb_e), (floor_w, floor_e)
    width = va_w.shape[1]
    inner = width - FINE
    valid = inner - FINE
    spans = (
        (pl.ds(0, valid), lambda j: banded.at[0, j]),
        (pl.ds(valid, rows - 2 * valid), lambda j: natural.at[j, pl.ds(valid, rows - 2 * valid), :]),
        (pl.ds(rows - valid, valid), lambda j: banded.at[1, j]),
    )
    copies = [
        pltpu.make_async_copy(part(j), out.at[span, pl.ds(j * LANES, LANES)], sems.at[n, j])
        for j in range(1, tiles - 1)
        for n, (span, part) in enumerate(spans)
    ]
    for copy in copies:
        copy.start()

    def piece(ref, n, to):
        slot = 2 * planes + n // 16
        return roll(ref[slot * SUB : (slot + 1) * SUB, :], to - 8 * (n % 16), 1)

    fields = []
    for which, field in enumerate(coarse_fields(stats, from_north, from_south)):
        parts = []
        count = field.shape[0] // SUB
        for i in range(count):
            n = which * count + i
            here = field[i * SUB : (i + 1) * SUB]
            here = jnp.where(lane // 8 == coarse_cols // 8, piece(from_east, n, coarse_cols), here)
            here = jnp.where(lane // 8 == 15, piece(from_west, n, LANES - 8), here)
            parts.append(here)
        fields.append(jnp.concatenate(parts, axis=0))
    value = coarse_sweeps(*fields)
    value = jnp.concatenate([value, jnp.zeros((LANES - value.shape[0], LANES), jnp.float32)], axis=0).T
    for c in range(planes):
        index = (planes * lane + (c + HALO_C * BLK - FINE)) // BLK
        for side, groups in enumerate(((LANES - 8, 0), (coarse_cols - 8, coarse_cols))):
            for n, at in enumerate(groups):
                lifted[side, c, n * SUB : (n + 1) * SUB, :] = gather_lanes(value[at : at + SUB], index)

    for side, ref in enumerate((from_west, from_east)):
        for c in range(planes):
            for i in range(width // SUB):
                if (side, i) in ((0, 0), (1, width // SUB - 1)):
                    low, k = (ref[(w * planes + c) * SUB : (w * planes + c + 1) * SUB, :] for w in range(2))
                else:
                    col = (i - 1) * SUB if side == 0 else LANES - inner + i * SUB
                    low, k = (turned[side, w, c, col : col + SUB, :] for w in range(2))
                c_row = (i + 15) // 2 if side == 0 else 8 - COARSE - 1 + i // 2
                at = slice(i * SUB, (i + 1) * SUB)
                floor[side][c, at, :] = low
                va[side][c, at, :] = start_value(low, k, lifted[side, c, c_row : c_row + 1, :])

    count = width // SUB

    def strided(ref):
        return lambda t: [[ref[c, pl.ds(t, SUB, stride=count), :] for c in range(planes)]]

    def keep(dst):
        def store(t, groups):
            for c, value in enumerate(groups[0]):
                dst[c, pl.ds(t, SUB, stride=count), :] = value

        return store

    def twice(i, carry):
        for src, dst in ((va, vb), (vb, va)):
            for side in range(2):
                grouped_sweep(
                    count,
                    strided(src[side]),
                    lambda t, groups: [edge_rolls(groups[0])],
                    strided(floor[side]),
                    keep(dst[side]),
                    count,
                )
        return carry

    lax.fori_loop(0, FINE // 2, twice, 0)

    stores = []
    for side, j in enumerate((0, tiles - 1)):
        fill = jnp.zeros((LANES - inner, LANES), jnp.float32)
        for c in range(planes):
            parts = [va[side][c, FINE:, :], fill] if side == 0 else [fill, va[side][c, 0:inner, :]]
            back = jnp.concatenate(parts, axis=0).T
            for a in range(LANES // SUB):
                tall[side, pl.ds(a * SUB * planes + c, SUB, stride=planes), :] = back[a * SUB : (a + 1) * SUB]
        mine = (lane < valid) if side == 0 else (lane >= LANES - valid)
        for i in range(rows // SUB):
            at = i * SUB
            if at < valid:
                other = banded[0, j, at : at + SUB, :]
            elif at >= rows - valid:
                at_band = at - (rows - valid)
                other = banded[1, j, at_band : at_band + SUB, :]
            else:
                other = natural[j, at : at + SUB, :]
            edge[side, at : at + SUB, :] = jnp.where(mine, tall[side, FINE + at : FINE + at + SUB, :], other)
        stores.append(
            pltpu.make_async_copy(edge.at[side], out.at[:, pl.ds(j * LANES, LANES)], edge_sems.at[side])
        )
        stores[-1].start()
    for copy in copies + stores:
        copy.wait()


def strips(stats, from_north, from_south, turned, from_west, from_east, natural, banded):
    tiles, rows, _ = natural.shape
    planes = turned.shape[2]
    vmem = pl.BlockSpec(memory_space=pltpu.VMEM)
    wide = (planes, COARSE * BLK + 3 * FINE, LANES)
    f32 = jnp.float32
    return pl.pallas_call(
        strip_kernel,
        in_specs=[vmem] * 8,
        out_specs=pl.BlockSpec(memory_space=pltpu.HBM),
        out_shape=jax.ShapeDtypeStruct((rows, tiles * LANES), f32),
        scratch_shapes=[
            *[pltpu.VMEM(wide, f32)] * 6,
            pltpu.VMEM((2, planes, 2 * SUB, LANES), f32),
            pltpu.VMEM((2, planes * LANES, LANES), f32),
            pltpu.VMEM((2, rows, LANES), f32),
            pltpu.SemaphoreType.DMA((3, tiles)),
            pltpu.SemaphoreType.DMA((2,)),
        ],
        compiler_params=pltpu.CompilerParams(vmem_limit_bytes=12 * MIB),
        name="strips",
    )(stats, from_north, from_south, turned, from_west, from_east, natural, banded)


def ring(value, axis, shift):
    count = lax.axis_size(axis)
    return lax.ppermute(value, axis, [(i, (i + shift) % count) for i in range(count)])


def shards(elevation, ocean, outlet):
    floor, lock, floor_t, lock_t, stats, stats_t, north, south = prepare(elevation, ocean, outlet)
    from_north = ring(south, "row", 1)
    from_south = ring(north, "row", -1)
    natural = main_part(floor_t, lock_t, stats_t, elevation.shape[0])
    from_north, from_south, natural = lax.optimization_barrier((from_north, from_south, natural))
    halo_args = (stats, from_north, from_south)
    west, east, turned = pack_columns(floor, lock, *halo_args)
    from_west = ring(east, "col", 1)
    from_east = ring(west, "col", -1)
    banded = bands(floor, lock, *halo_args)
    return strips(*halo_args, turned, from_west, from_east, natural, banded)


def solution(mesh):
    return jax.shard_map(
        shards,
        mesh=mesh,
        in_specs=(P("row", "col"), P("row", "col"), P("row", "col")),
        out_specs=P("row", "col"),
        check_vma=False,
    )
```
